32 devices in a mesh: section: 4 (over y, core), tp: 8 (over z, x).
Axes of the slice: x: 2, y: 2, z: 4, core: 2. Of those that a mesh axis runs over, the one named last changes fastest.
Arguments:
- inputs: bfloat16 [4, 32, 8192], P(None, None, 'tp'), may hold values from -6 to 6
- cotangent: bfloat16 [4, 32, 8192], P(None, None, 'tp'), may hold values from -6 to 6
- weights: bfloat16 [4, 8192, 8192], P('section', 'tp'), may hold values from -0.0625 to 0.0625
- gains: float32 [4, 8192], P('section', 'tp'), may hold values from 0.1 to 1.9
Outputs:
- activations: bfloat16 [4, 4, 32, 8192], P('section', None, None, 'tp')
- gradients: bfloat16 [4, 4, 32, 8192], P('section', None, None, 'tp')
The draws below stay inside these ranges and needn't reach their ends.
All inputs are finite; a program needn't handle non-finite values.
Results may differ from the reference program's by a relative error of at most 0.019.
Values may be sent and summed in bfloat16 or wider, within the bound.
No kernel may reach another device: no remote copies, remote signals or barrier semaphores. Data moves between devices by JAX's collectives and lax.ppermute only.
A program may use at most 64 MiB of HBM per device.

```python
import jax
import jax.numpy as jnp
from jax import lax

D = 8192
MICRO = 4
ROWS = 32
SECTIONS = 4
N_TP = 8


def block_scale(rng, extent, cuts, smallest, high):
    loudness, own = 1.0, jax.random.fold_in(rng, 6)
    for position, parts in cuts:
        steps = jnp.exp(jax.random.uniform(jax.random.fold_in(own, position), (parts,), jnp.float32, smallest / len(cuts), high / len(cuts)))
        loudness = loudness * jnp.repeat(steps, extent[position] // parts).reshape([-1 if axis == position else 1 for axis in range(len(extent))])
    return loudness


def normal_values(own_key, shape, deviation, limit, pieces=(), held_as=jnp.bfloat16):
    result = jax.random.normal(own_key, shape, jnp.float32) * deviation
    if len(pieces) > 0:
        result = block_scale(own_key, shape, pieces, -0.22, 0.18) * result
    return jnp.clip(result, min=-limit, max=limit).astype(held_as)


def setup_inputs(seed: int = 0) -> dict:
    key_list = jax.random.split(jax.random.key(seed), 5)
    inputs = normal_values(key_list[0], (MICRO, ROWS, D), 1.0, 6.0, ((2, 8),))
    cotangent = normal_values(key_list[1], (MICRO, ROWS, D), 1.0, 6.0, ((2, 8),))
    weights = normal_values(key_list[2], (SECTIONS, D, D), D ** -0.5, 0.0625, ((0, 4), (1, 8)))
    gains = jnp.clip(1.0 + 0.18 * jax.random.normal(key_list[3], (SECTIONS, D), jnp.float32), 0.1, 1.9)
    return {"inputs": inputs, "cotangent": cotangent, "weights": weights, "gains": gains}


EPSILON = 1e-05

def rounded(value):
    return lax.optimization_barrier(value.astype(jnp.bfloat16)).astype(jnp.float32)

def reference(inputs, cotangent, weights, gains):
    local_width = D // N_TP
    row_total = MICRO * ROWS
    section_in = inputs.reshape(row_total, D)
    saved_in = []
    saved_branch = []
    saved_rms = []
    outputs = []
    for level in range(SECTIONS):
        wide_in = section_in.astype(jnp.float32)
        scaled = (wide_in * gains[level]).astype(jnp.bfloat16)
        squares = jnp.zeros((row_total,), jnp.float32)
        for block_no in range(N_TP):
            lower = block_no * local_width
            piece = wide_in[:, lower:lower + local_width]
            squares = squares + rounded(lax.optimization_barrier(jnp.sum(piece * piece, axis=1)))
        branch = jnp.dot(scaled, weights[level], preferred_element_type=jnp.float32)
        inv_rms = lax.rsqrt(squares / D + EPSILON)
        output = (wide_in + inv_rms[:, None] * branch).astype(jnp.bfloat16)
        saved_in.append(section_in)
        saved_branch.append(branch)
        saved_rms.append(inv_rms)
        outputs.append(output.reshape(MICRO, ROWS, D))
        section_in = output
    upstream = cotangent.reshape(row_total, D)
    grads = [None] * SECTIONS
    for level in range(SECTIONS - 1, -1, -1):
        wide_up = upstream.astype(jnp.float32)
        back_rows = jnp.dot(upstream, weights[level].T, preferred_element_type=jnp.float32)
        product = wide_up * saved_branch[level]
        row_dot = jnp.zeros((row_total,), jnp.float32)
        for block_no in range(N_TP):
            lower = block_no * local_width
            row_dot = row_dot + rounded(lax.optimization_barrier(jnp.sum(product[:, lower:lower + local_width], axis=1)))
        inv_rms = saved_rms[level]
        grad_in = (wide_up + inv_rms[:, None] * gains[level] * back_rows - (inv_rms ** 3 / D * row_dot)[:, None] * saved_in[level].astype(jnp.float32)).astype(jnp.bfloat16)
        grads[level] = grad_in.reshape(MICRO, ROWS, D)
        upstream = grad_in
    return (jnp.stack(outputs), jnp.stack(grads))
```

```python
import jax
import jax.numpy as jnp
from jax import lax
from jax.experimental import pallas as pl
from jax.experimental.pallas import tpu as pltpu
from jax.sharding import PartitionSpec as P

EPSILON = 1e-05
MIB = 1 << 20


def forward_kernel(block_count, place_ref, a_ref, gain_ref, w_ref, *rest):
    out_refs, scaled_ref = rest[:-1], rest[-1]
    step = pl.program_id(0)

    @pl.when(step == 0)
    def _():
        wide = a_ref[...].astype(jnp.float32)
        scaled_ref[...] = (wide * gain_ref[...]).astype(jnp.bfloat16)

    partial = jnp.dot(scaled_ref[...], w_ref[...], preferred_element_type=jnp.float32)
    for block in range(block_count):

        @pl.when(step == block)
        def _(block=block):
            out_refs[block][...] = partial.astype(jnp.bfloat16)


def forward_blocks(a, gain_row, w_rows, blocks):
    rows, width = a.shape
    count = len(blocks)
    whole = pl.BlockSpec((rows, width), lambda k, place_ref: (0, 0))
    return pl.pallas_call(
        lambda *refs: forward_kernel(count, *refs),
        out_shape=[jax.ShapeDtypeStruct((rows, width), jnp.bfloat16)] * count,
        grid_spec=pltpu.PrefetchScalarGridSpec(
            num_scalar_prefetch=1,
            grid=(count,),
            in_specs=[
                whole,
                pl.BlockSpec((1, width), lambda k, place_ref: (0, 0)),
                pl.BlockSpec((width, width), lambda k, place_ref: (0, place_ref[k])),
            ],
            out_specs=[whole] * count,
            scratch_shapes=[pltpu.VMEM((rows, width), jnp.bfloat16)],
        ),
        compiler_params=pltpu.CompilerParams(vmem_limit_bytes=24 * MIB),
        cost_estimate=pl.CostEstimate(
            flops=2 * rows * width * width * count,
            bytes_accessed=2 * width * width * count,
            transcendentals=0,
        ),
    )(jnp.stack(blocks), a, gain_row, w_rows)


def backward_kernel(block_count, place_ref, w_ref, *rest):
    g_refs, out_ref, held_ref = rest[:block_count], rest[block_count], rest[block_count + 1]
    step = pl.program_id(0)
    for block in range(block_count):

        @pl.when(step == block)
        def _(block=block):
            held_ref[...] = g_refs[block][...]

    product = lax.dot_general(
        held_ref[...], w_ref[...], (((1,), (1,)), ((), ())), preferred_element_type=jnp.float32
    )

    @pl.when(step == 0)
    def _():
        out_ref[...] = product

    @pl.when(step > 0)
    def _():
        out_ref[...] += product


def backward_blocks(shards, w_rows, blocks):
    rows, width = shards[0].shape
    count = len(blocks)
    whole = pl.BlockSpec((rows, width), lambda k, place_ref: (0, 0))
    return pl.pallas_call(
        lambda *refs: backward_kernel(count, *refs),
        out_shape=jax.ShapeDtypeStruct((rows, width), jnp.float32),
        grid_spec=pltpu.PrefetchScalarGridSpec(
            num_scalar_prefetch=1,
            grid=(count,),
            in_specs=[pl.BlockSpec((width, width), lambda k, place_ref: (0, place_ref[k]))]
            + [whole] * count,
            out_specs=whole,
            scratch_shapes=[pltpu.VMEM((rows, width), jnp.bfloat16)],
        ),
        compiler_params=pltpu.CompilerParams(vmem_limit_bytes=24 * MIB),
        cost_estimate=pl.CostEstimate(
            flops=2 * rows * width * width * count,
            bytes_accessed=2 * width * width * count,
            transcendentals=0,
        ),
    )(jnp.stack(blocks), w_rows, *shards)


def on_device(inputs, cotangent, weights, gains):
    section_no = lax.axis_index("section")
    section_count = lax.axis_size("section")
    tp_no = lax.axis_index("tp")
    tp_count = lax.axis_size("tp")
    inner = tp_count // 4 if tp_count % 4 == 0 else tp_count
    outer = tp_count // inner
    micro_count, row_count, width = inputs.shape
    rows = micro_count * row_count
    full_width = weights.shape[2]
    w_rows = weights[0]
    gain_row = gains
    last = section_count - 1

    def send(value, sections, step=0, hop=0):
        pairs = [
            (s * tp_count + t, (s + hop) * tp_count + (t ^ step))
            for s in sections
            for t in range(tp_count)
        ]
        return lax.ppermute(value, ("section", "tp"), pairs)

    def chosen(section, new, old):
        return jnp.where(section_no == section, new, old)

    def row_totals(partial, sections):
        total = partial
        step = 1
        while step < tp_count:
            total = total + send(total, sections, step)
            step *= 2
        return total

    def row_sum(value):
        return jnp.sum(value, axis=1).astype(jnp.bfloat16).astype(jnp.float32)

    def place(dz, dx):
        return tp_no ^ (dz * inner + dx)

    def gathered(shard, sections):
        found = []
        for dz in [0] + list(range(1, outer)):
            column = shard if dz == 0 else send(shard, sections, dz * inner)
            found.append((column, place(dz, 0)))
            for dx in range(1, inner):
                found.append((send(column, sections, dx), place(dz, dx)))
        return found

    def scattered_sum(a, sections):
        order = list(range(outer - 1, -1, -1))
        mine = {}
        theirs = {}
        for dx in range(inner - 1, -1, -1):
            parts = forward_blocks(a, gain_row, w_rows, [place(dz, dx) for dz in order])
            for dz, part in zip(order, parts):
                if dx == 0:
                    mine[dz] = part
                else:
                    theirs[dz, dx] = send(part, sections, dx)
        total = None
        for dz in order:
            column = mine[dz].astype(jnp.float32)
            for dx in range(1, inner):
                column = column + theirs[dz, dx].astype(jnp.float32)
            if dz:
                column = send(column.astype(jnp.bfloat16), sections, dz * inner).astype(jnp.float32)
            total = column if total is None else total + column
        return total

    def forward(a, sections):
        wide = a.astype(jnp.float32)
        squares = row_totals(row_sum(wide * wide), sections)
        inv_rms = lax.rsqrt(squares / full_width + EPSILON)
        branch = scattered_sum(a, sections)
        return branch, inv_rms, (wide + inv_rms[:, None] * branch).astype(jnp.bfloat16)

    def back_rows(g, sections):
        found = gathered(g, sections)
        return backward_blocks([f[0] for f in found], w_rows, [f[1] for f in found])

    cot = cotangent.reshape(rows, width)
    last_back = gain_row * back_rows(cot, [last])

    block_in = inputs.reshape(rows, width)
    outputs = jnp.zeros_like(block_in)
    inv_rms = jnp.zeros((rows,), jnp.float32)
    branch = jnp.zeros((rows, width), jnp.float32)
    for section in range(last):
        new_branch, new_rms, output = forward(block_in, [section])
        incoming = send(output, [section], hop=1)
        outputs = chosen(section, output, outputs)
        inv_rms = chosen(section, new_rms, inv_rms)
        branch = chosen(section, new_branch, branch)
        block_in = chosen(section + 1, incoming, block_in)

    wide = block_in.astype(jnp.float32)
    sums = row_totals(jnp.stack([row_sum(wide * wide), row_sum(wide * last_back)]), [last])
    last_rms = lax.rsqrt(sums[0] / full_width + EPSILON)
    grad = (
        cot.astype(jnp.float32)
        + last_rms[:, None] * last_back
        - (last_rms**3 / full_width * sums[1])[:, None] * wide
    ).astype(jnp.bfloat16)
    grads = grad
    last_branch = scattered_sum(block_in, [last])
    outputs = chosen(
        last, (wide + last_rms[:, None] * last_branch).astype(jnp.bfloat16), outputs
    )
    for section in range(last - 1, -1, -1):
        upstream = send(grad, [section + 1], hop=-1)
        wide_up = upstream.astype(jnp.float32)
        row_dot = row_totals(row_sum(wide_up * branch), [section])
        back = back_rows(upstream, [section])
        grad = (
            wide_up
            + inv_rms[:, None] * gain_row * back
            - (inv_rms**3 / full_width * row_dot)[:, None] * wide
        ).astype(jnp.bfloat16)
        grads = chosen(section, grad, grads)
    shape = (1, micro_count, row_count, width)
    return outputs.reshape(shape), grads.reshape(shape)


def solution(mesh):
    placed = (
        P(None, None, "tp"),
        P(None, None, "tp"),
        P("section", "tp", None),
        P("section", "tp"),
    )
    return jax.shard_map(
        on_device,
        mesh=mesh,
        in_specs=placed,
        out_specs=(P("section", None, None, "tp"), P("section", None, None, "tp")),
        check_vma=False,
    )
```

```python
import jax
import jax.numpy as jnp
from jax import lax
from jax.experimental import pallas as pl
from jax.experimental.pallas import tpu as pltpu
from jax.sharding import PartitionSpec as P

EPSILON = 1e-05
MIB = 1 << 20
TAIL = 16
LANES = 128
VMEM_LIMIT = 20 * MIB
SMEM_SPEC = pl.BlockSpec(memory_space=pltpu.SMEM)
VMEM_SPEC = pl.BlockSpec(memory_space=pltpu.VMEM)


def as_line(column):
    return jnp.broadcast_to(column, (column.shape[0], LANES)).T[:1]


def as_column(line):
    return jnp.broadcast_to(line, (LANES, line.shape[1])).T[:, :1]


def store_tail(out_ref, rows, line, row_no):
    row_ids = lax.broadcasted_iota(jnp.int32, (TAIL, rows), 0)
    tile = jnp.where(row_ids == row_no, jnp.broadcast_to(line, (TAIL, rows)), 0.0)
    out_ref[rows:, :] = jnp.zeros((TAIL, out_ref.shape[1]), out_ref.dtype)
    out_ref[rows:, :rows] = tile.astype(out_ref.dtype)


def tail_sum(chunk_refs, rows):
    total = chunk_refs[0][rows:, :rows].astype(jnp.float32)
    for chunk in chunk_refs[1:]:
        total = total + chunk[rows:, :rows].astype(jnp.float32)
    return jnp.sum(total, axis=0, keepdims=True)


def matmul_cost(rows, width, count):
    return pl.CostEstimate(
        flops=2 * rows * width * width * count,
        bytes_accessed=2 * width * width * count,
        transcendentals=0,
    )


def forward_blocks(a, gain_row, w_rows, blocks, tail_row, other=None, use_other=None):
    rows, width = a.shape
    count = len(blocks)
    with_other = other is not None
    meta = jnp.stack(blocks + [tail_row] + ([use_other] if with_other else []))

    def kernel(meta_ref, *refs):
        a_ref, gain_ref, w_ref = refs[:3]
        other_ref = refs[3] if with_other else None
        out_refs = refs[4 if with_other else 3 : -1]
        scaled_ref = refs[-1]
        step = pl.program_id(0)

        @pl.when(step == 0)
        def _():
            wide = a_ref[...].astype(jnp.float32)
            scaled_ref[...] = (wide * gain_ref[...]).astype(jnp.bfloat16)
            line = as_line(jnp.sum(wide * wide, axis=1, keepdims=True))
            for out_ref in out_refs:
                store_tail(out_ref, rows, line, meta_ref[count])

        partial = jnp.dot(scaled_ref[...], w_ref[...], preferred_element_type=jnp.float32)
        for block in range(count):

            @pl.when(step == block)
            def _(block=block):
                out_refs[block][:rows, :] = partial.astype(jnp.bfloat16)

        if with_other:

            @pl.when((step == count - 1) & (meta_ref[count + 1] == 1))
            def _():
                for out_ref in out_refs:
                    out_ref[...] = other_ref[...]

    def whole(shape):
        return pl.BlockSpec(shape, lambda k, meta_ref: (0, 0))

    chunk = (rows + TAIL, width)
    return pl.pallas_call(
        kernel,
        out_shape=[jax.ShapeDtypeStruct(chunk, jnp.bfloat16)] * count,
        grid_spec=pltpu.PrefetchScalarGridSpec(
            num_scalar_prefetch=1,
            grid=(count,),
            in_specs=[
                whole((rows, width)),
                whole((1, width)),
                pl.BlockSpec((width, width), lambda k, meta_ref: (0, meta_ref[k])),
            ]
            + [whole(chunk)] * with_other,
            out_specs=[whole(chunk)] * count,
            scratch_shapes=[pltpu.VMEM((rows, width), jnp.bfloat16)],
        ),
        compiler_params=pltpu.CompilerParams(vmem_limit_bytes=VMEM_LIMIT),
        cost_estimate=matmul_cost(rows, width, count),
    )(meta, a, gain_row, w_rows, *([other] if with_other else []))


def add_chunks(chunks, other=None, use_other=None):
    def kernel(meta_ref, *refs):
        total = refs[0][...].astype(jnp.float32)
        for chunk in refs[1 : len(chunks)]:
            total = total + chunk[...].astype(jnp.float32)
        refs[-1][...] = total.astype(jnp.bfloat16)
        if other is not None:

            @pl.when(meta_ref[0] == 1)
            def _():
                refs[-1][...] = refs[len(chunks)][...]

    operands = chunks + ([other] if other is not None else [])
    meta = jnp.stack([use_other if other is not None else jnp.int32(0)])
    return pl.pallas_call(
        kernel,
        out_shape=jax.ShapeDtypeStruct(chunks[0].shape, jnp.bfloat16),
        in_specs=[SMEM_SPEC] + [VMEM_SPEC] * len(operands),
        out_specs=VMEM_SPEC,
        compiler_params=pltpu.CompilerParams(vmem_limit_bytes=VMEM_LIMIT),
    )(meta, *operands)


def finish_forward(chunks, a, full_width, kept, keep):
    rows, width = a.shape

    def kernel(meta_ref, a_ref, *refs):
        chunk_refs, rest = refs[: len(chunks)], refs[len(chunks) :]
        old_refs, (out_ref, *new_refs) = rest[:3], rest[3:]
        branch = chunk_refs[0][:rows, :].astype(jnp.float32)
        for chunk in chunk_refs[1:]:
            branch = branch + chunk[:rows, :].astype(jnp.float32)
        squares = as_column(tail_sum(chunk_refs, rows))
        inv_rms = lax.rsqrt(squares / full_width + EPSILON)
        out_ref[...] = (a_ref[...].astype(jnp.float32) + inv_rms * branch).astype(jnp.bfloat16)
        held = meta_ref[0] == 1

        @pl.when(held)
        def _():
            new_refs[0][...] = out_ref[...]
            new_refs[1][...] = branch
            new_refs[2][...] = jnp.broadcast_to(inv_rms, (rows, LANES))

        @pl.when(jnp.logical_not(held))
        def _():
            for new, old in zip(new_refs, old_refs):
                new[...] = old[...]

    out = jax.ShapeDtypeStruct((rows, width), jnp.bfloat16)
    return pl.pallas_call(
        kernel,
        out_shape=[out, out, jax.ShapeDtypeStruct((rows, width), jnp.float32), jax.ShapeDtypeStruct((rows, LANES), jnp.float32)],
        in_specs=[SMEM_SPEC] + [VMEM_SPEC] * (1 + len(chunks) + 3),
        out_specs=[VMEM_SPEC] * 4,
        compiler_params=pltpu.CompilerParams(vmem_limit_bytes=VMEM_LIMIT),
    )(jnp.stack([keep]), a, *chunks, *kept)


def gradient_chunks(upstream, branch, tail_row, others, use_other):
    rows, width = upstream.shape
    replaced = [other for other in others if other is not None]

    def kernel(meta_ref, up_ref, branch_ref, *refs):
        other_refs, out_refs = list(refs[: len(replaced)]), refs[len(replaced) :]
        up = up_ref[...]
        line = as_line(
            jnp.sum(up.astype(jnp.float32) * branch_ref[...], axis=1, keepdims=True)
        )
        for out_ref in out_refs:
            out_ref[:rows, :] = up
            store_tail(out_ref, rows, line, meta_ref[0])

        @pl.when(meta_ref[1] == 1)
        def _():
            for other, out_ref in zip(others, out_refs):
                if other is not None:
                    out_ref[...] = other_refs.pop(0)[...]

    return pl.pallas_call(
        kernel,
        out_shape=[jax.ShapeDtypeStruct((rows + TAIL, width), jnp.bfloat16)] * len(others),
        in_specs=[SMEM_SPEC] + [VMEM_SPEC] * (2 + len(replaced)),
        out_specs=[VMEM_SPEC] * len(others),
        compiler_params=pltpu.CompilerParams(vmem_limit_bytes=VMEM_LIMIT),
    )(jnp.stack([tail_row, use_other]), upstream, branch, *replaced)


def backward_blocks(chunks, w_rows, blocks):
    rows = chunks[0].shape[0] - TAIL
    width = w_rows.shape[0]
    count = len(blocks)

    def kernel(meta_ref, w_ref, *refs):
        chunk_refs, (out_ref, sum_ref, held_ref) = refs[:count], refs[count:]
        step = pl.program_id(0)
        for block in range(count):

            @pl.when(step == block)
            def _(block=block):
                held_ref[...] = chunk_refs[block][:rows, :]

        product = lax.dot_general(
            w_ref[...], held_ref[...], (((1,), (1,)), ((), ())), preferred_element_type=jnp.float32
        )

        @pl.when(step == 0)
        def _():
            out_ref[...] = product
            sum_ref[...] = jnp.broadcast_to(tail_sum(chunk_refs, rows), (8, rows))

        @pl.when(step > 0)
        def _():
            out_ref[...] += product

    def whole(shape):
        return pl.BlockSpec(shape, lambda k, meta_ref: (0, 0))

    return pl.pallas_call(
        kernel,
        out_shape=[jax.ShapeDtypeStruct((width, rows), jnp.float32), jax.ShapeDtypeStruct((8, rows), jnp.float32)],
        grid_spec=pltpu.PrefetchScalarGridSpec(
            num_scalar_prefetch=1,
            grid=(count,),
            in_specs=[pl.BlockSpec((width, width), lambda k, meta_ref: (0, meta_ref[k]))]
            + [whole((rows + TAIL, width))] * count,
            out_specs=[whole((width, rows)), whole((8, rows))],
            scratch_shapes=[pltpu.VMEM((rows, width), jnp.bfloat16)],
        ),
        compiler_params=pltpu.CompilerParams(vmem_limit_bytes=VMEM_LIMIT),
        cost_estimate=matmul_cost(rows, width, count),
    )(jnp.stack(blocks), w_rows, *chunks)


def finish_backward(halves, upstream, inv_rms, gain_row, a, full_width, grads, keep):
    rows, width = a.shape

    def kernel(meta_ref, b0_ref, s0_ref, b1_ref, s1_ref, up_ref, rms_ref, gain_ref, a_ref, old_ref, out_ref, new_ref):
        back = (b0_ref[...] + b1_ref[...]).T
        row_dot = as_column((s0_ref[...] + s1_ref[...])[:1])
        rms = rms_ref[:, :1]
        grad = (
            up_ref[...].astype(jnp.float32)
            + rms * gain_ref[...] * back
            - (rms * rms * rms / full_width * row_dot) * a_ref[...].astype(jnp.float32)
        ).astype(jnp.bfloat16)
        out_ref[...] = grad
        held = meta_ref[0] == 1

        @pl.when(held)
        def _():
            new_ref[...] = grad

        @pl.when(jnp.logical_not(held))
        def _():
            new_ref[...] = old_ref[...]

    out = jax.ShapeDtypeStruct((rows, width), jnp.bfloat16)
    return pl.pallas_call(
        kernel,
        out_shape=[out, out],
        in_specs=[SMEM_SPEC] + [VMEM_SPEC] * 9,
        out_specs=[VMEM_SPEC] * 2,
        compiler_params=pltpu.CompilerParams(vmem_limit_bytes=VMEM_LIMIT),
    )(jnp.stack([keep]), *halves[0], *halves[1], upstream, inv_rms, gain_row, a, grads)


def on_device(inputs, cotangent, weights, gains):
    section_no = lax.axis_index("section")
    section_count = lax.axis_size("section")
    tp_no = lax.axis_index("tp")
    tp_count = lax.axis_size("tp")
    micro_count, row_count, width = inputs.shape
    rows = micro_count * row_count
    full_width = weights.shape[2]
    w_rows = weights[0]
    last = section_count - 1
    across = tp_count // 2
    near = list(range(1, across))
    tail_row = tp_no % TAIL

    def send(value, sections, step=0, hop=0):
        pairs = [
            (s * tp_count + t, (s + hop) * tp_count + (t ^ step))
            for s in sections
            for t in range(tp_count)
        ]
        return lax.ppermute(value, ("section", "tp"), pairs)

    def is_section(section):
        return (section_no == section).astype(jnp.int32)

    def row_totals(partial, sections):
        total = partial
        step = 1
        while step < tp_count:
            total = total + send(total, sections, step)
            step *= 2
        return total

    def row_sum(value):
        return jnp.sum(value, axis=1).astype(jnp.bfloat16).astype(jnp.float32)

    cot = cotangent.reshape(rows, width)
    block_in = inputs.reshape(rows, width)
    kept = (
        jnp.zeros_like(block_in),
        jnp.zeros((rows, width), jnp.float32),
        jnp.zeros((rows, LANES), jnp.float32),
    )
    far_blocks = [tp_no ^ across ^ e for e in [0] + near]
    near_blocks = [tp_no ^ e for e in [0] + near]

    cot_chunk = jnp.pad(cot, ((0, TAIL), (0, 0)))
    other = cot_chunk
    cot_found = {0: cot_chunk}
    last_back = None
    for section in range(last):
        shared = section < 2
        sections = [section] + ([last] if shared else [])
        use_other = is_section(last) if shared else None
        far = forward_blocks(
            block_in, gains, w_rows, far_blocks, tail_row, other if shared else None, use_other
        )
        arrived = [send(chunk, sections, e) for e, chunk in zip(near, far[1:])]
        own = forward_blocks(block_in, gains, w_rows, near_blocks, tail_row)
        if shared:
            for e, chunk in zip(near, arrived):
                cot_found[e if section == 0 else across ^ e] = chunk
        first_pass = section == 0
        combined = add_chunks(
            [far[0]] + arrived, other if first_pass else None, use_other if first_pass else None
        )
        crossed = send(combined, [section] + ([last] if first_pass else []), across)
        if first_pass:
            cot_found[across] = other = crossed
        direct = [send(chunk, [section], e) for e, chunk in zip(near, own[1:])]
        output, *kept = finish_forward(
            [own[0]] + direct + [crossed], block_in, full_width, kept, is_section(section)
        )
        incoming = send(output, [section], hop=1)
        block_in = jnp.where(section_no == section + 1, incoming, block_in)
        if section == 1:
            order = sorted(cot_found)

            def cotangent_rows():
                chunks = [cot_found[e] for e in order]
                back, _ = backward_blocks(chunks, w_rows, [tp_no ^ e for e in order])
                return gains * back.T

            last_back = lax.cond(
                section_no == last, cotangent_rows, lambda: jnp.zeros((rows, width), jnp.float32)
            )

    outputs, branch, inv_rms = kept
    wide = block_in.astype(jnp.float32)
    sums = row_totals(jnp.stack([row_sum(wide * wide), row_sum(wide * last_back)]), [last])
    last_rms = lax.rsqrt(sums[0] / full_width + EPSILON)[:, None]
    grad = (
        cot.astype(jnp.float32)
        + last_rms * last_back
        - (last_rms**3 / full_width * sums[1][:, None]) * wide
    ).astype(jnp.bfloat16)
    grads = grad

    chunk_zero = jnp.zeros((rows + TAIL, width), jnp.bfloat16)
    upstream = send(grad, [last], hop=-1)
    last_in, upstream = lax.optimization_barrier((block_in, upstream))
    parts = lax.cond(
        section_no == last,
        lambda: tuple(forward_blocks(last_in, gains, w_rows, far_blocks, tail_row))
        + tuple(forward_blocks(last_in, gains, w_rows, near_blocks, tail_row)),
        lambda: (chunk_zero,) * tp_count,
    )
    far, own = parts[:across], parts[across:]
    for section in range(last - 1, -1, -1):
        turn = last - 1 - section
        if turn == 0:
            others = [None] + list(far[1:])
            cross_sections, near_sections = [section], [section, last]
        elif turn == 1:
            others = [combined] + list(own[1:])
            cross_sections, near_sections = [section, last], [section, last]
        else:
            others = [None] * across
            cross_sections, near_sections = [section], [section]
        chunks = gradient_chunks(upstream, branch, tail_row, others, is_section(last))
        crossed = send(chunks[0], cross_sections, across)
        direct = [send(chunk, near_sections, e) for e, chunk in zip(near, chunks[1:])]
        half = backward_blocks([chunks[0]] + direct, w_rows, near_blocks)
        forwarded = [send(crossed, [section], e) for e in near]
        if turn == 0:
            combined = add_chunks([far[0]] + direct)
        if turn == 1:
            _, outputs, _, _ = finish_forward(
                [own[0]] + direct + [crossed], block_in, full_width, (outputs, branch, inv_rms), is_section(last)
            )
        other_half = backward_blocks([crossed] + forwarded, w_rows, far_blocks)
        grad, grads = finish_backward(
            (half, other_half), upstream, inv_rms, gains, block_in, full_width, grads, is_section(section)
        )
        if section:
            upstream = send(grad, [section], hop=-1)
    shape = (1, micro_count, row_count, width)
    return outputs.reshape(shape), grads.reshape(shape)


def solution(mesh):
    placed = (
        P(None, None, "tp"),
        P(None, None, "tp"),
        P("section", "tp", None),
        P("section", "tp"),
    )
    return jax.shard_map(
        on_device,
        mesh=mesh,
        in_specs=placed,
        out_specs=(P("section", None, None, "tp"), P("section", None, None, "tp")),
        check_vma=False,
    )
```

```python
import jax
import jax.numpy as jnp
from jax import lax
from jax.experimental import pallas as pl
from jax.experimental.pallas import tpu as pltpu
from jax.sharding import PartitionSpec as P

EPSILON = 1e-05
MIB = 1 << 20
TAIL = 16
LANES = 128
VMEM_LIMIT = 20 * MIB
SMEM_SPEC = pl.BlockSpec(memory_space=pltpu.SMEM)
VMEM_SPEC = pl.BlockSpec(memory_space=pltpu.VMEM)


def as_line(column):
    return jnp.broadcast_to(column, (column.shape[0], LANES)).T[:1]


def as_column(line):
    return jnp.broadcast_to(line, (LANES, line.shape[1])).T[:, :1]


def store_tail(out_ref, rows, line, row_no):
    row_ids = lax.broadcasted_iota(jnp.int32, (TAIL, rows), 0)
    tile = jnp.where(row_ids == row_no, jnp.broadcast_to(line, (TAIL, rows)), 0.0)
    out_ref[rows:, :] = jnp.zeros((TAIL, out_ref.shape[1]), out_ref.dtype)
    out_ref[rows:, :rows] = tile.astype(out_ref.dtype)


def tail_sum(chunk_refs, rows):
    total = chunk_refs[0][rows:, :rows].astype(jnp.float32)
    for chunk in chunk_refs[1:]:
        total = total + chunk[rows:, :rows].astype(jnp.float32)
    return jnp.sum(total, axis=0, keepdims=True)


def matmul_cost(rows, width, count):
    return pl.CostEstimate(
        flops=2 * rows * width * width * count,
        bytes_accessed=2 * width * width * count,
        transcendentals=0,
    )


def forward_blocks(a, gain_row, w_rows, blocks, tail_row, other=None, use_other=None):
    rows, width = a.shape
    count = len(blocks)
    tile = min(width, 512)
    with_other = other is not None
    meta = jnp.stack(blocks + [tail_row] + ([use_other] if with_other else []))

    def kernel(meta_ref, a_ref, gain_ref, w_ref, *refs):
        other_ref = refs[0] if with_other else None
        out_refs = refs[with_other:]
        wide = a_ref[...].astype(jnp.float32)
        scaled = (wide * gain_ref[...]).astype(jnp.bfloat16)
        for block, out_ref in enumerate(out_refs):
            for start in range(0, width, tile):
                columns = pl.ds(pl.multiple_of(meta_ref[block] * width + start, tile), tile)
                partial = jnp.dot(scaled, w_ref[:, columns], preferred_element_type=jnp.float32)
                out_ref[:rows, start : start + tile] = partial.astype(jnp.bfloat16)
        line = as_line(jnp.sum(wide * wide, axis=1, keepdims=True))
        for out_ref in out_refs:
            store_tail(out_ref, rows, line, meta_ref[count])
        if with_other:

            @pl.when(meta_ref[count + 1] == 1)
            def _():
                for out_ref in out_refs:
                    out_ref[...] = other_ref[...]

    return pl.pallas_call(
        kernel,
        out_shape=[jax.ShapeDtypeStruct((rows + TAIL, width), jnp.bfloat16)] * count,
        in_specs=[SMEM_SPEC] + [VMEM_SPEC] * (3 + with_other),
        out_specs=[VMEM_SPEC] * count,
        compiler_params=pltpu.CompilerParams(vmem_limit_bytes=VMEM_LIMIT),
        cost_estimate=matmul_cost(rows, width, count),
    )(meta, a, gain_row, w_rows, *([other] if with_other else []))


def add_chunks(chunks, other=None, use_other=None):
    def kernel(meta_ref, *refs):
        total = refs[0][...].astype(jnp.float32)
        for chunk in refs[1 : len(chunks)]:
            total = total + chunk[...].astype(jnp.float32)
        refs[-1][...] = total.astype(jnp.bfloat16)
        if other is not None:

            @pl.when(meta_ref[0] == 1)
            def _():
                refs[-1][...] = refs[len(chunks)][...]

    operands = chunks + ([other] if other is not None else [])
    meta = jnp.stack([use_other if other is not None else jnp.int32(0)])
    return pl.pallas_call(
        kernel,
        out_shape=jax.ShapeDtypeStruct(chunks[0].shape, jnp.bfloat16),
        in_specs=[SMEM_SPEC] + [VMEM_SPEC] * len(operands),
        out_specs=VMEM_SPEC,
        compiler_params=pltpu.CompilerParams(vmem_limit_bytes=VMEM_LIMIT),
    )(meta, *operands)


def finish_forward(chunks, a, full_width, kept, keep):
    rows, width = a.shape

    def kernel(meta_ref, a_ref, *refs):
        chunk_refs, rest = refs[: len(chunks)], refs[len(chunks) :]
        old_refs, (out_ref, *new_refs) = rest[:3], rest[3:]
        branch = chunk_refs[0][:rows, :].astype(jnp.float32)
        for chunk in chunk_refs[1:]:
            branch = branch + chunk[:rows, :].astype(jnp.float32)
        squares = as_column(tail_sum(chunk_refs, rows))
        inv_rms = lax.rsqrt(squares / full_width + EPSILON)
        out_ref[...] = (a_ref[...].astype(jnp.float32) + inv_rms * branch).astype(jnp.bfloat16)
        held = meta_ref[0] == 1

        @pl.when(held)
        def _():
            new_refs[0][...] = out_ref[...]
            new_refs[1][...] = branch
            new_refs[2][...] = jnp.broadcast_to(inv_rms, (rows, LANES))

        @pl.when(jnp.logical_not(held))
        def _():
            for new, old in zip(new_refs, old_refs):
                new[...] = old[...]

    out = jax.ShapeDtypeStruct((rows, width), jnp.bfloat16)
    return pl.pallas_call(
        kernel,
        out_shape=[out, out, jax.ShapeDtypeStruct((rows, width), jnp.float32), jax.ShapeDtypeStruct((rows, LANES), jnp.float32)],
        in_specs=[SMEM_SPEC] + [VMEM_SPEC] * (1 + len(chunks) + 3),
        out_specs=[VMEM_SPEC] * 4,
        compiler_params=pltpu.CompilerParams(vmem_limit_bytes=VMEM_LIMIT),
    )(jnp.stack([keep]), a, *chunks, *kept)


def gradient_chunks(upstream, branch, tail_row, others, use_other):
    rows, width = upstream.shape
    replaced = [other for other in others if other is not None]

    def kernel(meta_ref, up_ref, branch_ref, *refs):
        other_refs, out_refs = list(refs[: len(replaced)]), refs[len(replaced) :]
        up = up_ref[...]
        line = as_line(
            jnp.sum(up.astype(jnp.float32) * branch_ref[...], axis=1, keepdims=True)
        )
        for out_ref in out_refs:
            out_ref[:rows, :] = up
            store_tail(out_ref, rows, line, meta_ref[0])

        @pl.when(meta_ref[1] == 1)
        def _():
            for other, out_ref in zip(others, out_refs):
                if other is not None:
                    out_ref[...] = other_refs.pop(0)[...]

    return pl.pallas_call(
        kernel,
        out_shape=[jax.ShapeDtypeStruct((rows + TAIL, width), jnp.bfloat16)] * len(others),
        in_specs=[SMEM_SPEC] + [VMEM_SPEC] * (2 + len(replaced)),
        out_specs=[VMEM_SPEC] * len(others),
        compiler_params=pltpu.CompilerParams(vmem_limit_bytes=VMEM_LIMIT),
    )(jnp.stack([tail_row, use_other]), upstream, branch, *replaced)


def backward_blocks(chunks, w_rows, blocks):
    rows = chunks[0].shape[0] - TAIL
    width = w_rows.shape[0]
    count = len(blocks)
    tile = min(width, 256)

    def kernel(meta_ref, w_ref, *refs):
        chunk_refs, (out_ref, sum_ref) = refs[:count], refs[count:]
        for start in range(0, width, tile):
            total = None
            for block, chunk in enumerate(chunk_refs):
                columns = pl.ds(pl.multiple_of(meta_ref[block] * width, width), width)
                product = lax.dot_general(
                    w_ref[start : start + tile, columns],
                    chunk[:rows, :],
                    (((1,), (1,)), ((), ())),
                    preferred_element_type=jnp.float32,
                )
                total = product if total is None else total + product
            out_ref[start : start + tile, :] = total
        sum_ref[...] = jnp.broadcast_to(tail_sum(chunk_refs, rows), (8, rows))

    return pl.pallas_call(
        kernel,
        out_shape=[
            jax.ShapeDtypeStruct((width, rows), jnp.float32),
            jax.ShapeDtypeStruct((8, rows), jnp.float32),
        ],
        in_specs=[SMEM_SPEC] + [VMEM_SPEC] * (1 + count),
        out_specs=[VMEM_SPEC] * 2,
        compiler_params=pltpu.CompilerParams(vmem_limit_bytes=VMEM_LIMIT),
        cost_estimate=matmul_cost(rows, width, count),
    )(jnp.stack(blocks), w_rows, *chunks)


def finish_backward(halves, upstream, inv_rms, gain_row, a, full_width, grads, keep):
    rows, width = a.shape

    def kernel(meta_ref, b0_ref, s0_ref, b1_ref, s1_ref, up_ref, rms_ref, gain_ref, a_ref, old_ref, out_ref, new_ref):
        back = (b0_ref[...] + b1_ref[...]).T
        row_dot = as_column((s0_ref[...] + s1_ref[...])[:1])
        rms = rms_ref[:, :1]
        grad = (
            up_ref[...].astype(jnp.float32)
            + rms * gain_ref[...] * back
            - (rms * rms * rms / full_width * row_dot) * a_ref[...].astype(jnp.float32)
        ).astype(jnp.bfloat16)
        out_ref[...] = grad
        held = meta_ref[0] == 1

        @pl.when(held)
        def _():
            new_ref[...] = grad

        @pl.when(jnp.logical_not(held))
        def _():
            new_ref[...] = old_ref[...]

    out = jax.ShapeDtypeStruct((rows, width), jnp.bfloat16)
    return pl.pallas_call(
        kernel,
        out_shape=[out, out],
        in_specs=[SMEM_SPEC] + [VMEM_SPEC] * 9,
        out_specs=[VMEM_SPEC] * 2,
        compiler_params=pltpu.CompilerParams(vmem_limit_bytes=VMEM_LIMIT),
    )(jnp.stack([keep]), *halves[0], *halves[1], upstream, inv_rms, gain_row, a, grads)


def on_device(inputs, cotangent, weights, gains):
    section_no = lax.axis_index("section")
    section_count = lax.axis_size("section")
    tp_no = lax.axis_index("tp")
    tp_count = lax.axis_size("tp")
    micro_count, row_count, width = inputs.shape
    rows = micro_count * row_count
    full_width = weights.shape[2]
    w_rows = weights[0]
    last = section_count - 1
    across = tp_count // 2
    near = list(range(1, across))
    tail_row = tp_no % TAIL

    def send(value, sections, step=0, hop=0):
        pairs = [
            (s * tp_count + t, (s + hop) * tp_count + (t ^ step))
            for s in sections
            for t in range(tp_count)
        ]
        return lax.ppermute(value, ("section", "tp"), pairs)

    def is_section(section):
        return (section_no == section).astype(jnp.int32)

    def row_totals(partial, sections):
        total = partial
        step = 1
        while step < tp_count:
            total = total + send(total, sections, step)
            step *= 2
        return total

    def row_sum(value):
        return jnp.sum(value, axis=1).astype(jnp.bfloat16).astype(jnp.float32)

    cot = cotangent.reshape(rows, width)
    block_in = inputs.reshape(rows, width)
    kept = (
        jnp.zeros_like(block_in),
        jnp.zeros((rows, width), jnp.float32),
        jnp.zeros((rows, LANES), jnp.float32),
    )
    far_blocks = [tp_no ^ across ^ e for e in [0] + near]
    near_blocks = [tp_no ^ e for e in [0] + near]

    cot_chunk = jnp.pad(cot, ((0, TAIL), (0, 0)))
    other = cot_chunk
    cot_found = {0: cot_chunk}
    last_back = None
    for section in range(last):
        shared = section < 2
        sections = [section] + ([last] if shared else [])
        use_other = is_section(last) if shared else None
        far = forward_blocks(
            block_in, gains, w_rows, far_blocks, tail_row, other if shared else None, use_other
        )
        arrived = [send(chunk, sections, e) for e, chunk in zip(near, far[1:])]
        own = forward_blocks(block_in, gains, w_rows, near_blocks, tail_row)
        if shared:
            for e, chunk in zip(near, arrived):
                cot_found[e if section == 0 else across ^ e] = chunk
        first_pass = section == 0
        combined = add_chunks(
            [far[0]] + arrived, other if first_pass else None, use_other if first_pass else None
        )
        crossed = send(combined, [section] + ([last] if first_pass else []), across)
        if first_pass:
            cot_found[across] = other = crossed
        direct = [send(chunk, [section], e) for e, chunk in zip(near, own[1:])]
        output, *kept = finish_forward(
            [own[0]] + direct + [crossed], block_in, full_width, kept, is_section(section)
        )
        incoming = send(output, [section], hop=1)
        block_in = jnp.where(section_no == section + 1, incoming, block_in)
        if section == 1:
            order = sorted(cot_found)

            def cotangent_rows():
                chunks = [cot_found[e] for e in order]
                back, _ = backward_blocks(chunks, w_rows, [tp_no ^ e for e in order])
                return gains * back.T

            last_back = lax.cond(
                section_no == last, cotangent_rows, lambda: jnp.zeros((rows, width), jnp.float32)
            )

    outputs, branch, inv_rms = kept
    wide = block_in.astype(jnp.float32)
    sums = row_totals(jnp.stack([row_sum(wide * wide), row_sum(wide * last_back)]), [last])
    last_rms = lax.rsqrt(sums[0] / full_width + EPSILON)[:, None]
    grad = (
        cot.astype(jnp.float32)
        + last_rms * last_back
        - (last_rms**3 / full_width * sums[1][:, None]) * wide
    ).astype(jnp.bfloat16)
    grads = grad

    chunk_zero = jnp.zeros((rows + TAIL, width), jnp.bfloat16)
    upstream = send(grad, [last], hop=-1)
    last_in, upstream = lax.optimization_barrier((block_in, upstream))
    parts = lax.cond(
        section_no == last,
        lambda: tuple(forward_blocks(last_in, gains, w_rows, far_blocks, tail_row))
        + tuple(forward_blocks(last_in, gains, w_rows, near_blocks, tail_row)),
        lambda: (chunk_zero,) * tp_count,
    )
    far, own = parts[:across], parts[across:]
    for section in range(last - 1, -1, -1):
        turn = last - 1 - section
        if turn == 0:
            others = [None] + list(far[1:])
            cross_sections, near_sections = [section], [section, last]
        elif turn == 1:
            others = [combined] + list(own[1:])
            cross_sections, near_sections = [section, last], [section, last]
        else:
            others = [None] * across
            cross_sections, near_sections = [section], [section]
        chunks = gradient_chunks(upstream, branch, tail_row, others, is_section(last))
        crossed = send(chunks[0], cross_sections, across)
        direct = [send(chunk, near_sections, e) for e, chunk in zip(near, chunks[1:])]
        half = backward_blocks([chunks[0]] + direct, w_rows, near_blocks)
        forwarded = [send(crossed, [section], e) for e in near]
        if turn == 0:
            combined = add_chunks([far[0]] + direct)
        if turn == 1:
            _, outputs, _, _ = finish_forward(
                [own[0]] + direct + [crossed], block_in, full_width, (outputs, branch, inv_rms), is_section(last)
            )
        other_half = backward_blocks([crossed] + forwarded, w_rows, far_blocks)
        grad, grads = finish_backward(
            (half, other_half), upstream, inv_rms, gains, block_in, full_width, grads, is_section(section)
        )
        if section:
            upstream = send(grad, [section], hop=-1)
    shape = (1, micro_count, row_count, width)
    return outputs.reshape(shape), grads.reshape(shape)


def solution(mesh):
    placed = (
        P(None, None, "tp"),
        P(None, None, "tp"),
        P("section", "tp", None),
        P("section", "tp"),
    )
    return jax.shard_map(
        on_device,
        mesh=mesh,
        in_specs=placed,
        out_specs=(P("section", None, None, "tp"), P("section", None, None, "tp")),
        check_vma=False,
    )
```

```python
import jax
import jax.numpy as jnp
from jax import lax
from jax.experimental import pallas as pl
from jax.experimental.pallas import tpu as pltpu
from jax.sharding import PartitionSpec as P

EPSILON = 1e-05
MIB = 1 << 20
TAIL = 16
LANES = 128
VMEM_LIMIT = 20 * MIB
SMEM_SPEC = pl.BlockSpec(memory_space=pltpu.SMEM)
VMEM_SPEC = pl.BlockSpec(memory_space=pltpu.VMEM)


def as_line(column):
    return jnp.broadcast_to(column, (column.shape[0], LANES)).T[:1]


def as_column(line):
    return jnp.broadcast_to(line, (LANES, line.shape[1])).T[:, :1]


def store_tail(out_ref, rows, line, row_no):
    row_ids = lax.broadcasted_iota(jnp.int32, (TAIL, rows), 0)
    tile = jnp.where(row_ids == row_no, jnp.broadcast_to(line, (TAIL, rows)), 0.0)
    out_ref[rows : rows + TAIL, :] = jnp.zeros((TAIL, out_ref.shape[1]), out_ref.dtype)
    out_ref[rows : rows + TAIL, :rows] = tile.astype(out_ref.dtype)


def tail_sum(chunk_refs, rows):
    total = chunk_refs[0][rows : rows + TAIL, :rows].astype(jnp.float32)
    for chunk in chunk_refs[1:]:
        total = total + chunk[rows : rows + TAIL, :rows].astype(jnp.float32)
    return jnp.sum(total, axis=0, keepdims=True)


def matmul_cost(rows, width, count):
    return pl.CostEstimate(
        flops=2 * rows * width * width * count,
        bytes_accessed=2 * width * width * count,
        transcendentals=0,
    )


def forward_blocks(a, gain_row, w_rows, blocks, tail_row, other=None, use_other=None, pack=None):
    rows, width = a.shape
    chunk_rows = rows + TAIL
    count = len(blocks)
    tile = min(width, 512)
    extras = [x for x in (other, pack) if x is not None]
    meta = jnp.stack(blocks + [tail_row] + ([use_other] if other is not None else []))

    def kernel(meta_ref, a_ref, gain_ref, w_ref, *refs):
        out_refs = refs[len(extras) :]
        wide = a_ref[...].astype(jnp.float32)
        scaled = (wide * gain_ref[...]).astype(jnp.bfloat16)
        for block, out_ref in enumerate(out_refs):
            for start in range(0, width, tile):
                columns = pl.ds(pl.multiple_of(meta_ref[block] * width + start, tile), tile)
                partial = jnp.dot(scaled, w_ref[:, columns], preferred_element_type=jnp.float32)
                out_ref[:rows, start : start + tile] = partial.astype(jnp.bfloat16)
        line = as_line(jnp.sum(wide * wide, axis=1, keepdims=True))
        for out_ref in out_refs:
            store_tail(out_ref, rows, line, meta_ref[count])
        if pack is not None:
            out_refs[0][chunk_rows : chunk_rows + rows, :] = a_ref[...]
            out_refs[0][chunk_rows + rows :, :] = refs[len(extras) - 1][...]
        if other is not None:

            @pl.when(meta_ref[count + 1] == 1)
            def _():
                for out_ref in out_refs:
                    out_ref[...] = refs[0][...]

    shapes = [(chunk_rows, width)] * count
    if pack is not None:
        shapes[0] = (2 * chunk_rows + rows, width)
    return pl.pallas_call(
        kernel,
        out_shape=[jax.ShapeDtypeStruct(shape, jnp.bfloat16) for shape in shapes],
        in_specs=[SMEM_SPEC] + [VMEM_SPEC] * (3 + len(extras)),
        out_specs=[VMEM_SPEC] * count,
        compiler_params=pltpu.CompilerParams(vmem_limit_bytes=VMEM_LIMIT),
        cost_estimate=matmul_cost(rows, width, count),
    )(meta, a, gain_row, w_rows, *extras)


def add_chunks(first, first_row, chunks, other=None, use_other=None):
    shape = chunks[0].shape

    def kernel(meta_ref, first_ref, *refs):
        total = first_ref[first_row : first_row + shape[0], :].astype(jnp.float32)
        for chunk in refs[: len(chunks)]:
            total = total + chunk[...].astype(jnp.float32)
        refs[-1][...] = total.astype(jnp.bfloat16)
        if other is not None:

            @pl.when(meta_ref[0] == 1)
            def _():
                refs[-1][...] = refs[len(chunks)][...]

    operands = [first] + chunks + ([other] if other is not None else [])
    meta = jnp.stack([use_other if other is not None else jnp.int32(0)])
    return pl.pallas_call(
        kernel,
        out_shape=jax.ShapeDtypeStruct(shape, jnp.bfloat16),
        in_specs=[SMEM_SPEC] + [VMEM_SPEC] * len(operands),
        out_specs=VMEM_SPEC,
        compiler_params=pltpu.CompilerParams(vmem_limit_bytes=VMEM_LIMIT),
    )(meta, *operands)


def finish_forward(first, chunks, a, full_width, kept, keep):
    chunk_rows, width = chunks[0].shape
    rows = chunk_rows - TAIL
    given = [] if a is None else [a]

    def kernel(meta_ref, first_ref, *refs):
        chunk_refs, rest = refs[: len(chunks)], refs[len(chunks) + len(given) :]
        old_refs, (out_ref, *new_refs) = rest[:3], rest[3:]
        source = first_ref[chunk_rows : chunk_rows + rows, :] if a is None else refs[len(chunks)][...]
        branch = first_ref[:rows, :].astype(jnp.float32)
        for chunk in chunk_refs:
            branch = branch + chunk[:rows, :].astype(jnp.float32)
        squares = as_column(tail_sum((first_ref,) + chunk_refs, rows))
        inv_rms = lax.rsqrt(squares / full_width + EPSILON)
        out_ref[...] = (source.astype(jnp.float32) + inv_rms * branch).astype(jnp.bfloat16)
        held = meta_ref[0] == 1

        @pl.when(held)
        def _():
            new_refs[0][...] = out_ref[...]
            new_refs[1][...] = branch
            new_refs[2][...] = jnp.broadcast_to(inv_rms, (rows, LANES))

        @pl.when(jnp.logical_not(held))
        def _():
            for new, old in zip(new_refs, old_refs):
                new[...] = old[...]

    out = jax.ShapeDtypeStruct((rows, width), jnp.bfloat16)
    return pl.pallas_call(
        kernel,
        out_shape=[
            out,
            out,
            jax.ShapeDtypeStruct((rows, width), jnp.float32),
            jax.ShapeDtypeStruct((rows, LANES), jnp.float32),
        ],
        in_specs=[SMEM_SPEC] + [VMEM_SPEC] * (1 + len(chunks) + len(given) + 3),
        out_specs=[VMEM_SPEC] * 4,
        compiler_params=pltpu.CompilerParams(vmem_limit_bytes=VMEM_LIMIT),
    )(jnp.stack([keep]), first, *chunks, *given, *kept)


def gradient_chunks(upstream, kept, others, use_other):
    rows, width = upstream.shape
    chunk_rows = rows + TAIL
    replaced = [other for other in others if other is not None]

    def kernel(meta_ref, up_ref, act_ref, branch_ref, rms_ref, *refs):
        other_refs, out_refs = list(refs[: len(replaced)]), refs[len(replaced) :]
        up = up_ref[...]
        dots = jnp.sum(up.astype(jnp.float32) * branch_ref[...], axis=1, keepdims=True)
        rms_line = rms_ref[...].T[:1]
        rms_high = rms_line.astype(jnp.bfloat16).astype(jnp.float32)
        row_ids = lax.broadcasted_iota(jnp.int32, (TAIL, rows), 0)
        tile = jnp.where(row_ids == 0, as_line(dots), 0.0)
        tile = jnp.where(row_ids == 1, rms_high, tile)
        tile = jnp.where(row_ids == 2, rms_line - rms_high, tile).astype(jnp.bfloat16)
        for out_ref in out_refs:
            out_ref[:rows, :] = up
            out_ref[rows:chunk_rows, :] = jnp.zeros((TAIL, width), jnp.bfloat16)
            out_ref[rows:chunk_rows, :rows] = tile
        out_refs[-1][chunk_rows:, :] = act_ref[...]

        @pl.when(meta_ref[0] == 1)
        def _():
            for other, out_ref in zip(others, out_refs):
                if other is not None:
                    out_ref[...] = other_refs.pop(0)[...]

    chunk = jax.ShapeDtypeStruct((chunk_rows, width), jnp.bfloat16)
    return pl.pallas_call(
        kernel,
        out_shape=[chunk] * len(others)
        + [jax.ShapeDtypeStruct((chunk_rows + rows, width), jnp.bfloat16)],
        in_specs=[SMEM_SPEC] + [VMEM_SPEC] * (4 + len(replaced)),
        out_specs=[VMEM_SPEC] * (len(others) + 1),
        compiler_params=pltpu.CompilerParams(vmem_limit_bytes=VMEM_LIMIT),
    )(jnp.stack([use_other]), upstream, *kept, *replaced)


def block_products(meta_ref, w_ref, chunk_refs, rows, start, tile):
    width = w_ref.shape[0]
    total = None
    for block, chunk in enumerate(chunk_refs):
        columns = pl.ds(pl.multiple_of(meta_ref[block] * width, width), width)
        product = lax.dot_general(
            w_ref[start : start + tile, columns],
            chunk[:rows, :],
            (((1,), (1,)), ((), ())),
            preferred_element_type=jnp.float32,
        )
        total = product if total is None else total + product
    return total


def backward_blocks(chunks, w_rows, blocks, rows):
    width = w_rows.shape[0]
    count = len(blocks)
    tile = min(width, 256)

    def kernel(meta_ref, w_ref, *refs):
        chunk_refs, (out_ref, sum_ref) = refs[:count], refs[count:]
        for start in range(0, width, tile):
            out_ref[start : start + tile, :] = block_products(
                meta_ref, w_ref, chunk_refs, rows, start, tile
            )
        sum_ref[...] = jnp.broadcast_to(first_sum(chunk_refs, rows), (8, rows))

    return pl.pallas_call(
        kernel,
        out_shape=[
            jax.ShapeDtypeStruct((width, rows), jnp.float32),
            jax.ShapeDtypeStruct((8, rows), jnp.float32),
        ],
        in_specs=[SMEM_SPEC] + [VMEM_SPEC] * (1 + count),
        out_specs=[VMEM_SPEC] * 2,
        compiler_params=pltpu.CompilerParams(vmem_limit_bytes=VMEM_LIMIT),
        cost_estimate=matmul_cost(rows, width, count),
    )(jnp.stack(blocks), w_rows, *chunks)


def first_sum(chunk_refs, rows):
    total = chunk_refs[0][rows : rows + TAIL, :rows].astype(jnp.float32)
    for chunk in chunk_refs[1:]:
        total = total + chunk[rows : rows + TAIL, :rows].astype(jnp.float32)
    return total[:1]


def finish_backward(chunks, w_rows, blocks, half, pack, gain_row, a, full_width, kept, keep):
    rows, width = a.shape
    chunk_rows = rows + TAIL
    count = len(blocks)
    tile = min(width, 256)

    def kernel(meta_ref, w_ref, *refs):
        chunk_refs = refs[:count]
        half_ref, sum_ref, pack_ref, gain_ref, a_ref = refs[count : count + 5]
        old_refs, (out_ref, *new_refs) = refs[count + 5 : count + 7], refs[count + 7 :]
        row_dot = as_column(sum_ref[:1] + first_sum(chunk_refs, rows))
        tail = pack_ref[rows:chunk_rows, :rows].astype(jnp.float32)
        rms = as_column(tail[1:2] + tail[2:3])
        scale = rms * rms * rms / full_width * row_dot
        for start in range(0, width, tile):
            products = block_products(meta_ref, w_ref, chunk_refs, rows, start, tile)
            back = (products + half_ref[start : start + tile, :]).T
            columns = slice(start, start + tile)
            out_ref[:, columns] = (
                pack_ref[:rows, columns].astype(jnp.float32)
                + rms * gain_ref[:, columns] * back
                - scale * a_ref[:, columns].astype(jnp.float32)
            ).astype(jnp.bfloat16)
        held = meta_ref[count] == 1

        @pl.when(held)
        def _():
            new_refs[0][...] = out_ref[...]
            new_refs[1][...] = pack_ref[chunk_rows:, :]

        @pl.when(jnp.logical_not(held))
        def _():
            for new, old in zip(new_refs, old_refs):
                new[...] = old[...]

    out = jax.ShapeDtypeStruct((rows, width), jnp.bfloat16)
    return pl.pallas_call(
        kernel,
        out_shape=[out] * 3,
        in_specs=[SMEM_SPEC] + [VMEM_SPEC] * (1 + count + 7),
        out_specs=[VMEM_SPEC] * 3,
        compiler_params=pltpu.CompilerParams(vmem_limit_bytes=VMEM_LIMIT),
        cost_estimate=matmul_cost(rows, width, count),
    )(jnp.stack(blocks + [keep]), w_rows, *chunks, *half, pack, gain_row, a, *kept)


def on_device(inputs, cotangent, weights, gains):
    section_no = lax.axis_index("section")
    section_count = lax.axis_size("section")
    tp_no = lax.axis_index("tp")
    tp_count = lax.axis_size("tp")
    micro_count, row_count, width = inputs.shape
    rows = micro_count * row_count
    chunk_rows = rows + TAIL
    full_width = weights.shape[2]
    w_rows = pltpu.with_memory_space_constraint(weights[0], pltpu.VMEM)
    last = section_count - 1
    across = tp_count // 2
    near = list(range(1, across))
    tail_row = tp_no % TAIL

    def send(value, routes, step=0):
        pairs = [
            (source * tp_count + t, target * tp_count + (t ^ step))
            for source, target in routes
            for t in range(tp_count)
        ]
        return lax.ppermute(value, ("section", "tp"), pairs)

    def is_section(section):
        return (section_no == section).astype(jnp.int32)

    def row_sum(value):
        return jnp.sum(value, axis=1).astype(jnp.bfloat16).astype(jnp.float32)

    cot = cotangent.reshape(rows, width)
    block_in = inputs.reshape(rows, width)
    kept = (
        jnp.zeros_like(block_in),
        jnp.zeros((rows, width), jnp.float32),
        jnp.zeros((rows, LANES), jnp.float32),
    )
    far_blocks = [tp_no ^ across ^ e for e in [0] + near]
    near_blocks = [tp_no ^ e for e in [0] + near]
    at_last = is_section(last)
    inside = [(last, last)]

    cot_chunk = jnp.pad(cot, ((0, TAIL), (0, 0)))
    other = cot_chunk
    cot_found = {0: cot_chunk}
    for section in range(last):
        beside = section ^ 1
        route = [(section, beside)]
        shared = section < 2
        far = forward_blocks(
            block_in, gains, w_rows, far_blocks, tail_row, other if shared else None, at_last
        )
        far_route = route + inside if shared else route
        arrived = [send(chunk, far_route, e) for e, chunk in zip(near, far[1:])]
        own = forward_blocks(block_in, gains, w_rows, near_blocks, tail_row, pack=far[0])
        pack = send(own[0], route)
        if shared:
            for e, chunk in zip(near, arrived):
                cot_found[e if section == 0 else across ^ e] = chunk
        first_pass = section == 0
        combined = add_chunks(
            pack, chunk_rows + rows, arrived, other if first_pass else None, at_last
        )
        crossed = send(combined, [(beside, beside)] + (inside if first_pass else []), across)
        if first_pass:
            cot_found[across] = other = crossed
        parts = own[1:]
        if not shared:
            parts, combined = lax.optimization_barrier((parts, combined))
        direct = [send(chunk, route, e) for e, chunk in zip(near, parts)]
        output, *kept = finish_forward(
            pack, direct + [crossed], None, full_width, kept, is_section(beside)
        )
        if section % 2:
            output = send(output, [(beside, section + 1)])
        block_in = jnp.where(section_no == section + 1, output, block_in)
        if section == 1:
            order = sorted(cot_found)

            def cotangent_rows():
                chunks = [cot_found[e] for e in order]
                back, _ = backward_blocks(chunks, w_rows, [tp_no ^ e for e in order], rows)
                return gains * back.T

            last_back = lax.cond(
                section_no == last, cotangent_rows, lambda: jnp.zeros((rows, width), jnp.float32)
            )

    wide = block_in.astype(jnp.float32)
    sums = jnp.stack([row_sum(wide * wide), row_sum(wide * last_back)])
    step = 1
    while step < tp_count:
        sums = sums + send(sums, ([(0, 1)] if step < across else [(1, 1)]) + inside, step)
        step *= 2
    last_rms = lax.rsqrt(sums[0] / full_width + EPSILON)[:, None]
    grad = (
        cot.astype(jnp.float32)
        + last_rms * last_back
        - (last_rms**3 / full_width * sums[1][:, None]) * wide
    ).astype(jnp.bfloat16)
    results = (grad, jnp.zeros_like(grad))

    chunk_zero = jnp.zeros((chunk_rows, width), jnp.bfloat16)
    last_in, grad = lax.optimization_barrier((block_in, grad))
    parts = lax.cond(
        section_no == last,
        lambda: tuple(forward_blocks(last_in, gains, w_rows, far_blocks, tail_row))
        + tuple(forward_blocks(last_in, gains, w_rows, near_blocks, tail_row)),
        lambda: (chunk_zero,) * tp_count,
    )
    last_far, last_own = list(parts[:across]), list(parts[across:])
    for section in range(last - 1, -1, -1):
        turn = last - 1 - section
        beside = section ^ 1
        route = [(beside, section)]
        upstream = send(grad, [(section + 1, beside)]) if section % 2 else grad
        if turn == 1:
            others = [None] + last_far[1:]
        elif turn == 2:
            others = [last_combined] + last_own[1:]
        else:
            others = [None]
        riding = inside if turn in (1, 2) else []
        *chunks, pack = gradient_chunks(upstream, kept, others, at_last)
        crossed = send(chunks[0], [(beside, beside)] + (inside if turn == 2 else []), across)
        near_chunks = chunks[1:] if riding else chunks * len(near)
        pack = send(pack, route)
        direct = [send(chunk, route + riding, e) for e, chunk in zip(near, near_chunks)]
        far_chunk, pack, direct = lax.optimization_barrier((crossed, pack, direct))
        forwarded = [send(far_chunk, route)]
        forwarded += [send(far_chunk, route + riding, e) for e in near]
        half = backward_blocks([pack] + direct, w_rows, near_blocks, rows)
        if turn == 1:
            last_combined = add_chunks(last_far[0], 0, direct)
        if turn == 2:
            last_output, *_ = finish_forward(
                last_own[0], direct + [crossed], block_in, full_width, kept, at_last
            )
        grad, *results = finish_backward(
            forwarded, w_rows, far_blocks, half, pack, gains, block_in, full_width, results, is_section(section)
        )
    grads, outputs = results
    outputs = jnp.where(section_no == last, last_output, outputs)
    shape = (1, micro_count, row_count, width)
    return outputs.reshape(shape), grads.reshape(shape)


def solution(mesh):
    placed = (
        P(None, None, "tp"),
        P(None, None, "tp"),
        P("section", "tp", None),
        P("section", "tp"),
    )
    return jax.shard_map(
        on_device,
        mesh=mesh,
        in_specs=placed,
        out_specs=(P("section", None, None, "tp"), P("section", None, None, "tp")),
        check_vma=False,
    )
```

```python
import jax
import jax.numpy as jnp
from jax import lax
from jax.experimental import pallas as pl
from jax.experimental.pallas import tpu as pltpu
from jax.sharding import PartitionSpec as P

EPSILON = 1e-05
MIB = 1 << 20
TAIL = 16
LANES = 128
VMEM_LIMIT = 12 * MIB
SMEM_SPEC = pl.BlockSpec(memory_space=pltpu.SMEM)
VMEM_SPEC = pl.BlockSpec(memory_space=pltpu.VMEM)


def as_line(column):
    return jnp.broadcast_to(column, (column.shape[0], LANES)).T[:1]


def as_column(line):
    return jnp.broadcast_to(line, (LANES, line.shape[1])).T[:, :1]


def store_tail(out_ref, rows, line, row_no):
    row_ids = lax.broadcasted_iota(jnp.int32, (TAIL, rows), 0)
    tile = jnp.where(row_ids == row_no, jnp.broadcast_to(line, (TAIL, rows)), 0.0)
    out_ref[rows : rows + TAIL, :] = jnp.zeros((TAIL, out_ref.shape[1]), out_ref.dtype)
    out_ref[rows : rows + TAIL, :rows] = tile.astype(out_ref.dtype)


def tail_sum(chunk_refs, rows):
    total = chunk_refs[0][rows : rows + TAIL, :rows].astype(jnp.float32)
    for chunk in chunk_refs[1:]:
        total = total + chunk[rows : rows + TAIL, :rows].astype(jnp.float32)
    return jnp.sum(total, axis=0, keepdims=True)


def matmul_cost(rows, width, count):
    return pl.CostEstimate(
        flops=2 * rows * width * width * count,
        bytes_accessed=2 * width * width * count,
        transcendentals=0,
    )


def load_weights(w_rows):
    def kernel(source_ref, out_ref, done):
        copy = pltpu.make_async_copy(source_ref, out_ref, done)
        copy.start()
        copy.wait()

    return pl.pallas_call(
        kernel,
        out_shape=pltpu.VMEM(w_rows.shape, w_rows.dtype),
        in_specs=[pl.BlockSpec(memory_space=pl.ANY)],
        out_specs=VMEM_SPEC,
        scratch_shapes=[pltpu.SemaphoreType.DMA],
        compiler_params=pltpu.CompilerParams(vmem_limit_bytes=MIB),
        cost_estimate=pl.CostEstimate(flops=0, bytes_accessed=2 * w_rows.size, transcendentals=0),
    )(w_rows)


def forward_blocks(a, gain_row, w_rows, blocks, tail_row, other=None, use_other=None, pack=False):
    rows, width = a.shape
    chunk_rows = rows + TAIL
    count = len(blocks)
    tile = min(width, 512)
    extras = [x for x in (other,) if x is not None]
    meta = jnp.stack(blocks + [tail_row] + ([use_other] if other is not None else []))

    def kernel(meta_ref, a_ref, gain_ref, w_ref, *refs):
        out_refs = refs[len(extras) :]
        wide = a_ref[...].astype(jnp.float32)
        scaled = (wide * gain_ref[...]).astype(jnp.bfloat16)
        for block, out_ref in enumerate(out_refs):
            for start in range(0, width, tile):
                columns = pl.ds(pl.multiple_of(meta_ref[block] * width + start, tile), tile)
                partial = jnp.dot(scaled, w_ref[:, columns], preferred_element_type=jnp.float32)
                out_ref[:rows, start : start + tile] = partial.astype(jnp.bfloat16)
        line = as_line(jnp.sum(wide * wide, axis=1, keepdims=True))
        for out_ref in out_refs:
            store_tail(out_ref, rows, line, meta_ref[count])
        if pack:
            out_refs[0][chunk_rows:, :] = a_ref[...]
        if other is not None:

            @pl.when(meta_ref[count + 1] == 1)
            def _():
                for out_ref in out_refs:
                    out_ref[...] = refs[0][...]

    shapes = [(chunk_rows, width)] * count
    if pack:
        shapes[0] = (chunk_rows + rows, width)
    return pl.pallas_call(
        kernel,
        out_shape=[jax.ShapeDtypeStruct(shape, jnp.bfloat16) for shape in shapes],
        in_specs=[SMEM_SPEC] + [VMEM_SPEC] * (3 + len(extras)),
        out_specs=[VMEM_SPEC] * count,
        compiler_params=pltpu.CompilerParams(vmem_limit_bytes=VMEM_LIMIT),
        cost_estimate=matmul_cost(rows, width, count),
    )(meta, a, gain_row, w_rows, *extras)


def add_chunks(chunks, other=None, use_other=None):
    def kernel(meta_ref, *refs):
        total = refs[0][...].astype(jnp.float32)
        for chunk in refs[1 : len(chunks)]:
            total = total + chunk[...].astype(jnp.float32)
        refs[-1][...] = total.astype(jnp.bfloat16)
        if other is not None:

            @pl.when(meta_ref[0] == 1)
            def _():
                refs[-1][...] = refs[len(chunks)][...]

    operands = chunks + ([other] if other is not None else [])
    meta = jnp.stack([use_other if other is not None else jnp.int32(0)])
    return pl.pallas_call(
        kernel,
        out_shape=jax.ShapeDtypeStruct(chunks[0].shape, jnp.bfloat16),
        in_specs=[SMEM_SPEC] + [VMEM_SPEC] * len(operands),
        out_specs=VMEM_SPEC,
        compiler_params=pltpu.CompilerParams(vmem_limit_bytes=VMEM_LIMIT),
    )(meta, *operands)


def finish_forward(first, chunks, a, full_width):
    chunk_rows, width = chunks[0].shape
    rows = chunk_rows - TAIL
    given = [] if a is None else [a]

    def kernel(first_ref, *refs):
        chunk_refs, (out_ref, branch_ref, rms_ref) = refs[: len(chunks)], refs[-3:]
        source = first_ref[chunk_rows:, :] if a is None else refs[len(chunks)][...]
        branch = first_ref[:rows, :].astype(jnp.float32)
        for chunk in chunk_refs:
            branch = branch + chunk[:rows, :].astype(jnp.float32)
        squares = as_column(tail_sum((first_ref,) + chunk_refs, rows))
        inv_rms = lax.rsqrt(squares / full_width + EPSILON)
        out_ref[...] = (source.astype(jnp.float32) + inv_rms * branch).astype(jnp.bfloat16)
        branch_ref[...] = branch
        rms_ref[...] = jnp.broadcast_to(inv_rms, (rows, LANES))

    return pl.pallas_call(
        kernel,
        out_shape=[
            jax.ShapeDtypeStruct((rows, width), jnp.bfloat16),
            jax.ShapeDtypeStruct((rows, width), jnp.float32),
            jax.ShapeDtypeStruct((rows, LANES), jnp.float32),
        ],
        in_specs=[VMEM_SPEC] * (1 + len(chunks) + len(given)),
        out_specs=[VMEM_SPEC] * 3,
        compiler_params=pltpu.CompilerParams(vmem_limit_bytes=VMEM_LIMIT),
    )(first, *chunks, *given)


def gradient_chunks(upstream, passed, others, use_other):
    rows, width = upstream.shape
    chunk_rows = rows + TAIL
    replaced = [other for other in others if other is not None]

    def kernel(meta_ref, up_ref, act_ref, branch_ref, rms_ref, *refs):
        other_refs, out_refs = list(refs[: len(replaced)]), refs[len(replaced) :]
        up = up_ref[...]
        dots = jnp.sum(up.astype(jnp.float32) * branch_ref[...], axis=1, keepdims=True)
        rms_line = rms_ref[...].T[:1]
        rms_high = rms_line.astype(jnp.bfloat16).astype(jnp.float32)
        row_ids = lax.broadcasted_iota(jnp.int32, (TAIL, rows), 0)
        tile = jnp.where(row_ids == 0, as_line(dots), 0.0)
        tile = jnp.where(row_ids == 1, rms_high, tile)
        tile = jnp.where(row_ids == 2, rms_line - rms_high, tile).astype(jnp.bfloat16)
        for out_ref in out_refs:
            out_ref[:rows, :] = up
            out_ref[rows:chunk_rows, :] = jnp.zeros((TAIL, width), jnp.bfloat16)
            out_ref[rows:chunk_rows, :rows] = tile
        out_refs[-1][chunk_rows:, :] = act_ref[...]

        @pl.when(meta_ref[0] == 1)
        def _():
            for other, out_ref in zip(others, out_refs):
                if other is not None:
                    out_ref[...] = other_refs.pop(0)[...]

    chunk = jax.ShapeDtypeStruct((chunk_rows, width), jnp.bfloat16)
    return pl.pallas_call(
        kernel,
        out_shape=[chunk] * len(others)
        + [jax.ShapeDtypeStruct((chunk_rows + rows, width), jnp.bfloat16)],
        in_specs=[SMEM_SPEC] + [VMEM_SPEC] * (4 + len(replaced)),
        out_specs=[VMEM_SPEC] * (len(others) + 1),
        compiler_params=pltpu.CompilerParams(vmem_limit_bytes=VMEM_LIMIT),
    )(jnp.stack([use_other]), upstream, *passed, *replaced)


def block_products(meta_ref, w_ref, chunk_refs, rows, start, tile):
    width = w_ref.shape[0]
    total = None
    for block, chunk in enumerate(chunk_refs):
        columns = pl.ds(pl.multiple_of(meta_ref[block] * width, width), width)
        product = lax.dot_general(
            w_ref[start : start + tile, columns],
            chunk[:rows, :],
            (((1,), (1,)), ((), ())),
            preferred_element_type=jnp.float32,
        )
        total = product if total is None else total + product
    return total


def backward_blocks(chunks, w_rows, blocks, rows):
    width = w_rows.shape[0]
    count = len(blocks)
    tile = min(width, 256)

    def kernel(meta_ref, w_ref, *refs):
        chunk_refs, (out_ref, sum_ref) = refs[:count], refs[count:]
        for start in range(0, width, tile):
            out_ref[start : start + tile, :] = block_products(
                meta_ref, w_ref, chunk_refs, rows, start, tile
            )
        sum_ref[...] = jnp.broadcast_to(first_sum(chunk_refs, rows), (8, rows))

    return pl.pallas_call(
        kernel,
        out_shape=[
            jax.ShapeDtypeStruct((width, rows), jnp.float32),
            jax.ShapeDtypeStruct((8, rows), jnp.float32),
        ],
        in_specs=[SMEM_SPEC] + [VMEM_SPEC] * (1 + count),
        out_specs=[VMEM_SPEC] * 2,
        compiler_params=pltpu.CompilerParams(vmem_limit_bytes=VMEM_LIMIT),
        cost_estimate=matmul_cost(rows, width, count),
    )(jnp.stack(blocks), w_rows, *chunks)


def first_sum(chunk_refs, rows):
    total = chunk_refs[0][rows : rows + TAIL, :rows].astype(jnp.float32)
    for chunk in chunk_refs[1:]:
        total = total + chunk[rows : rows + TAIL, :rows].astype(jnp.float32)
    return total[:1]


def finish_backward(chunks, w_rows, blocks, half, pack, gain_row, a, full_width, kept, keep):
    rows, width = a.shape
    chunk_rows = rows + TAIL
    count = len(blocks)
    tile = min(width, 256)

    def kernel(meta_ref, w_ref, *refs):
        chunk_refs = refs[:count]
        half_ref, sum_ref, pack_ref, gain_ref, a_ref = refs[count : count + 5]
        old_refs, (out_ref, *new_refs) = refs[count + 5 : count + 7], refs[count + 7 :]
        row_dot = as_column(sum_ref[:1] + first_sum(chunk_refs, rows))
        tail = pack_ref[rows:chunk_rows, :rows].astype(jnp.float32)
        rms = as_column(tail[1:2] + tail[2:3])
        scale = rms * rms * rms / full_width * row_dot
        for start in range(0, width, tile):
            products = block_products(meta_ref, w_ref, chunk_refs, rows, start, tile)
            back = (products + half_ref[start : start + tile, :]).T
            columns = slice(start, start + tile)
            out_ref[:, columns] = (
                pack_ref[:rows, columns].astype(jnp.float32)
                + rms * gain_ref[:, columns] * back
                - scale * a_ref[:, columns].astype(jnp.float32)
            ).astype(jnp.bfloat16)
        held = meta_ref[count] == 1

        @pl.when(held)
        def _():
            new_refs[0][...] = out_ref[...]
            new_refs[1][...] = pack_ref[chunk_rows:, :]

        @pl.when(jnp.logical_not(held))
        def _():
            for new, old in zip(new_refs, old_refs):
                new[...] = old[...]

    out = jax.ShapeDtypeStruct((rows, width), jnp.bfloat16)
    return pl.pallas_call(
        kernel,
        out_shape=[out] * 3,
        in_specs=[SMEM_SPEC] + [VMEM_SPEC] * (1 + count + 7),
        out_specs=[VMEM_SPEC] * 3,
        compiler_params=pltpu.CompilerParams(vmem_limit_bytes=VMEM_LIMIT),
        cost_estimate=matmul_cost(rows, width, count),
    )(jnp.stack(blocks + [keep]), w_rows, *chunks, *half, pack, gain_row, a, *kept)


def on_device(inputs, cotangent, weights, gains):
    section_no = lax.axis_index("section")
    section_count = lax.axis_size("section")
    tp_no = lax.axis_index("tp")
    tp_count = lax.axis_size("tp")
    micro_count, row_count, width = inputs.shape
    rows = micro_count * row_count
    chunk_rows = rows + TAIL
    full_width = weights.shape[2]
    w_rows = pltpu.with_memory_space_constraint(load_weights(weights[0]), pltpu.VMEM)
    last = section_count - 1
    across = tp_count // 2
    near = list(range(across - 1, 0, -1))
    tail_row = tp_no % TAIL

    def send(value, routes, step=0):
        pairs = [
            (source * tp_count + t, target * tp_count + (t ^ step))
            for source, target in routes
            for t in range(tp_count)
        ]
        return lax.ppermute(value, ("section", "tp"), pairs)

    def is_section(section):
        return (section_no == section).astype(jnp.int32)

    def row_sum(value):
        return jnp.sum(value, axis=1).astype(jnp.bfloat16).astype(jnp.float32)

    cot = cotangent.reshape(rows, width)
    block_in = inputs.reshape(rows, width)
    block_ins = []
    passed = []
    far_blocks = [tp_no ^ across ^ e for e in [0] + near]
    near_blocks = [tp_no ^ e for e in [0] + near]
    at_last = is_section(last)
    inside = [(last, last)]

    cot_chunk = jnp.pad(cot, ((0, TAIL), (0, 0)))
    other = cot_chunk
    cot_found = {0: cot_chunk}
    for section in range(last):
        beside = section ^ 1
        route = [(section, beside)]
        shared = section < 2
        far = forward_blocks(
            block_in, gains, w_rows, far_blocks, tail_row, other if shared else None, at_last
        )
        far_route = route + inside if shared else route
        arrived = [send(chunk, far_route, e) for e, chunk in zip(near, far[1:])]
        own = forward_blocks(block_in, gains, w_rows, near_blocks, tail_row, pack=True)
        if shared:
            for e, chunk in zip(near, arrived):
                cot_found[e if section == 0 else across ^ e] = chunk
        first_pass = section == 0
        combined = add_chunks(
            [send(far[0], route)] + arrived, other if first_pass else None, at_last
        )
        crossed = send(combined, [(beside, beside)] + (inside if first_pass else []), across)
        if first_pass:
            cot_found[across] = other = crossed
        direct = [send(chunk, route, e) for e, chunk in zip(near, own[1:])]
        output, branch, inv_rms = finish_forward(
            send(own[0], route), direct + [crossed], None, full_width
        )
        block_ins.append(block_in)
        passed.append((output, branch, inv_rms))
        block_in = send(output, [(beside, section + 1)]) if section % 2 else output
        if section == 1:
            order = sorted(cot_found)

            def cotangent_rows():
                chunks = [cot_found[e] for e in order]
                back, _ = backward_blocks(chunks, w_rows, [tp_no ^ e for e in order], rows)
                return gains * back.T

            last_back = lax.cond(
                section_no == last, cotangent_rows, lambda: jnp.zeros((rows, width), jnp.float32)
            )

    wide = block_in.astype(jnp.float32)
    sums = jnp.stack([row_sum(wide * wide), row_sum(wide * last_back)])
    step = 1
    while step < tp_count:
        sums = sums + send(sums, ([(0, 1)] if step < across else [(1, 1)]) + inside, step)
        step *= 2
    last_rms = lax.rsqrt(sums[0] / full_width + EPSILON)[:, None]
    grad = (
        cot.astype(jnp.float32)
        + last_rms * last_back
        - (last_rms**3 / full_width * sums[1][:, None]) * wide
    ).astype(jnp.bfloat16)
    results = (grad, jnp.zeros_like(grad))

    chunk_zero = jnp.zeros((chunk_rows, width), jnp.bfloat16)
    last_in, grad = lax.optimization_barrier((block_in, grad))
    parts = lax.cond(
        section_no == last,
        lambda: tuple(forward_blocks(last_in, gains, w_rows, far_blocks, tail_row))
        + tuple(forward_blocks(last_in, gains, w_rows, near_blocks, tail_row)),
        lambda: (chunk_zero,) * tp_count,
    )
    last_far, last_own = list(parts[:across]), list(parts[across:])
    for section in range(last - 1, -1, -1):
        turn = last - 1 - section
        beside = section ^ 1
        route = [(beside, section)]
        upstream = send(grad, [(section + 1, beside)]) if section % 2 else grad
        if turn == 1:
            others = [None] + last_far[1:]
        elif turn == 2:
            others = [last_combined] + last_own[1:]
        else:
            others = [None]
        riding = inside if turn in (1, 2) else []
        *chunks, pack = gradient_chunks(upstream, passed[section], others, at_last)
        crossed = send(chunks[0], [(beside, beside)] + (inside if turn == 2 else []), across)
        near_chunks = chunks[1:] if riding else chunks * len(near)
        pack = send(pack, route)
        direct = [send(chunk, route + riding, e) for e, chunk in zip(near, near_chunks)]
        forwarded = [send(crossed, route)] + [send(crossed, route, e) for e in near]
        half = backward_blocks([pack] + direct, w_rows, near_blocks, rows)
        if turn == 1:
            last_combined = add_chunks([last_far[0]] + direct)
        if turn == 2:
            last_output, _, _ = finish_forward(
                last_own[0], direct + [crossed], last_in, full_width
            )
        grad, *results = finish_backward(
            forwarded,
            w_rows,
            far_blocks,
            half,
            pack,
            gains,
            block_ins[section],
            full_width,
            results,
            is_section(section),
        )
    grads, outputs = results
    outputs = jnp.where(section_no == last, last_output, outputs)
    shape = (1, micro_count, row_count, width)
    return outputs.reshape(shape), grads.reshape(shape)


def solution(mesh):
    placed = (
        P(None, None, "tp"),
        P(None, None, "tp"),
        P("section", "tp", None),
        P("section", "tp"),
    )
    return jax.shard_map(
        on_device,
        mesh=mesh,
        in_specs=placed,
        out_specs=(P("section", None, None, "tp"), P("section", None, None, "tp")),
        check_vma=False,
    )
```

```python
import jax
import jax.numpy as jnp
from jax import lax
from jax.experimental import pallas as pl
from jax.experimental.pallas import tpu as pltpu
from jax.sharding import PartitionSpec as P

EPSILON = 1e-05
MIB = 1 << 20
TAIL = 16
LANES = 128
SMEM_SPEC = pl.BlockSpec(memory_space=pltpu.SMEM)
VMEM_SPEC = pl.BlockSpec(memory_space=pltpu.VMEM)


def local_kernel(kernel, place, operands, out_shapes, limit=12 * MIB, cost=None, **options):
    def body(place_ref, *refs):
        kernel(place_ref[0], place_ref[1], *refs)

    options.setdefault("in_specs", [SMEM_SPEC] + [VMEM_SPEC] * len(operands))
    call = pl.pallas_call(
        body,
        out_shape=out_shapes,
        out_specs=[VMEM_SPEC] * len(out_shapes),
        compiler_params=pltpu.CompilerParams(vmem_limit_bytes=limit),
        cost_estimate=cost,
        **options,
    )
    return list(call(place, *operands))


def bf16(*shape):
    return jax.ShapeDtypeStruct(shape, jnp.bfloat16)


def f32(*shape):
    return jax.ShapeDtypeStruct(shape, jnp.float32)


def as_line(column):
    return jnp.broadcast_to(column, (column.shape[0], LANES)).T[:1]


def as_column(line):
    return jnp.broadcast_to(line, (LANES, line.shape[1])).T[:, :1]


def row_sum(value):
    return jnp.sum(value, axis=1, keepdims=True).astype(jnp.bfloat16).astype(jnp.float32)


def tail_sum(chunk_refs, rows):
    total = chunk_refs[0][rows : rows + TAIL, :rows].astype(jnp.float32)
    for chunk in chunk_refs[1:]:
        total = total + chunk[rows : rows + TAIL, :rows].astype(jnp.float32)
    return total


def matmul_cost(rows, width, count):
    return pl.CostEstimate(
        flops=2 * rows * width * width * count,
        bytes_accessed=2 * width * width * count,
        transcendentals=0,
    )


def block_columns(tp, code, width, start=0, size=None):
    size = size or width
    return pl.ds(pl.multiple_of((tp ^ code) * width + start, size), size)


def load(place, weights, cot):
    rows, width = cot.shape

    def kernel(tp, section, w_ref, cot_ref, out_ref, chunk_ref, done):
        copy = pltpu.make_async_copy(w_ref, out_ref, done)
        copy.start()
        chunk_ref[:rows, :] = cot_ref[...]
        chunk_ref[rows:, :] = jnp.zeros((TAIL, width), jnp.bfloat16)
        copy.wait()

    return local_kernel(
        kernel,
        place,
        [pltpu.with_memory_space_constraint(weights, pltpu.HBM), cot],
        [pltpu.VMEM(weights.shape, weights.dtype), bf16(rows + TAIL, width)],
        limit=2 * MIB,
        in_specs=[SMEM_SPEC, pl.BlockSpec(memory_space=pltpu.HBM), VMEM_SPEC],
        scratch_shapes=[pltpu.SemaphoreType.DMA],
        cost=pl.CostEstimate(flops=0, bytes_accessed=2 * weights.size, transcendentals=0),
    )


def forward_blocks(place, a, gain_row, w_rows, codes, pack=False, only=None, other=None, other_at=None):
    rows, width = a.shape
    chunk_rows = rows + TAIL
    tile = min(width, 512)
    others = [] if other is None else [other]

    def kernel(tp, section, a_ref, gain_ref, w_ref, *refs):
        out_refs = refs[len(others) :]

        def work():
            wide = a_ref[...].astype(jnp.float32)
            scaled = (wide * gain_ref[...]).astype(jnp.bfloat16)
            for code, out_ref in zip(codes, out_refs):
                for start in range(0, width, tile):
                    partial = jnp.dot(
                        scaled,
                        w_ref[:, block_columns(tp, code, width, start, tile)],
                        preferred_element_type=jnp.float32,
                    )
                    out_ref[:rows, start : start + tile] = partial.astype(jnp.bfloat16)
            line = as_line(jnp.sum(wide * wide, axis=1, keepdims=True))
            row_ids = lax.broadcasted_iota(jnp.int32, (TAIL, rows), 0)
            own_row = jnp.where(row_ids == tp % TAIL, jnp.broadcast_to(line, (TAIL, rows)), 0.0)
            for out_ref in out_refs:
                out_ref[rows:chunk_rows, :] = jnp.zeros((TAIL, width), jnp.bfloat16)
                out_ref[rows:chunk_rows, :rows] = own_row.astype(jnp.bfloat16)
            if pack:
                out_refs[0][chunk_rows:, :] = a_ref[...]

        if only is not None:
            pl.when(section == only)(work)
        else:
            work()
        if others:

            @pl.when(section == other_at)
            def _():
                for out_ref in out_refs:
                    out_ref[...] = refs[0][...]

    shapes = [bf16(chunk_rows, width)] * len(codes)
    if pack:
        shapes[0] = bf16(chunk_rows + rows, width)
    return local_kernel(
        kernel,
        place,
        [a, gain_row, w_rows] + others,
        shapes,
        cost=matmul_cost(rows, width, len(codes)),
    )


def add_chunks(place, chunks, other=None, other_at=None):
    def kernel(tp, section, *refs):
        total = refs[0][...].astype(jnp.float32)
        for chunk in refs[1 : len(chunks)]:
            total = total + chunk[...].astype(jnp.float32)
        refs[-1][...] = total.astype(refs[-1].dtype)
        if other is not None:

            @pl.when(section == other_at)
            def _():
                refs[-1][...] = refs[len(chunks)][...]

    operands = chunks + ([] if other is None else [other])
    shape = jax.ShapeDtypeStruct(chunks[0].shape, chunks[0].dtype)
    return local_kernel(kernel, place, operands, [shape])[0]


def finish_forward(place, first, chunks, a, full_width):
    chunk_rows, width = chunks[0].shape
    rows = chunk_rows - TAIL
    given = [] if a is None else [a]

    def kernel(tp, section, first_ref, *refs):
        chunk_refs, (out_ref, branch_ref, rms_ref) = refs[: len(chunks)], refs[-3:]
        source = first_ref[chunk_rows:, :] if a is None else refs[len(chunks)][...]
        branch = first_ref[:rows, :].astype(jnp.float32)
        for chunk in chunk_refs:
            branch = branch + chunk[:rows, :].astype(jnp.float32)
        squares = jnp.sum(tail_sum((first_ref,) + chunk_refs, rows), axis=0, keepdims=True)
        inv_rms = lax.rsqrt(as_column(squares) / full_width + EPSILON)
        out_ref[...] = (source.astype(jnp.float32) + inv_rms * branch).astype(jnp.bfloat16)
        branch_ref[...] = branch
        rms_ref[...] = jnp.broadcast_to(inv_rms, (rows, LANES))

    return local_kernel(
        kernel,
        place,
        [first] + chunks + given,
        [bf16(rows, width), f32(rows, width), f32(rows, LANES)],
    )


def store_gradient_chunks(out_refs, grad, act_ref, branch_ref, rms_ref):
    rows, width = grad.shape
    chunk_rows = rows + TAIL
    dots = jnp.sum(grad.astype(jnp.float32) * branch_ref[...], axis=1, keepdims=True)
    rms_line = rms_ref[...].T[:1]
    rms_high = rms_line.astype(jnp.bfloat16).astype(jnp.float32)
    row_ids = lax.broadcasted_iota(jnp.int32, (TAIL, rows), 0)
    tile = jnp.where(row_ids == 0, as_line(dots), 0.0)
    tile = jnp.where(row_ids == 1, rms_high, tile)
    tile = jnp.where(row_ids == 2, rms_line - rms_high, tile).astype(jnp.bfloat16)
    for out_ref in out_refs:
        out_ref[:rows, :] = grad
        out_ref[rows:chunk_rows, :] = jnp.zeros((TAIL, width), jnp.bfloat16)
        out_ref[rows:chunk_rows, :rows] = tile
    out_refs[-1][chunk_rows:, :] = act_ref[...]


def gradient_chunks(place, upstream, passed, others, other_at):
    rows, width = upstream.shape
    replaced = [other for other in others if other is not None]

    def kernel(tp, section, up_ref, act_ref, branch_ref, rms_ref, *refs):
        other_refs, out_refs = list(refs[: len(replaced)]), refs[len(replaced) :]
        store_gradient_chunks(out_refs, up_ref[...], act_ref, branch_ref, rms_ref)
        if replaced:

            @pl.when(section == other_at)
            def _():
                for other, out_ref in zip(others, out_refs):
                    if other is not None:
                        out_ref[...] = other_refs.pop(0)[...]

    shapes = [bf16(rows + TAIL, width)] * len(others) + [bf16(2 * rows + TAIL, width)]
    return local_kernel(kernel, place, [upstream, *passed, *replaced], shapes)


def row_statistics(place, a, back):
    rows, _ = a.shape

    def kernel(tp, section, a_ref, back_ref, out_ref):
        wide = a_ref[...].astype(jnp.float32)
        row_ids = lax.broadcasted_iota(jnp.int32, (8, rows), 0)
        lines = jnp.where(row_ids == 0, as_line(row_sum(wide * wide)), 0.0)
        out_ref[...] = jnp.where(row_ids == 1, as_line(row_sum(wide * back_ref[...])), lines)

    return local_kernel(kernel, place, [a, back], [f32(8, rows)])[0]


def last_gradient(place, cot, back, a, sums, passed, full_width):
    rows, width = a.shape

    def kernel(tp, section, cot_ref, back_ref, a_ref, sums_ref, act_ref, branch_ref, rms_ref, grad_ref, *out_refs):
        squares = as_column(sums_ref[0:1, :])
        row_dot = as_column(sums_ref[1:2, :])
        rms = lax.rsqrt(squares / full_width + EPSILON)
        grad = (
            cot_ref[...].astype(jnp.float32)
            + rms * back_ref[...]
            - (rms * rms * rms / full_width * row_dot) * a_ref[...].astype(jnp.float32)
        ).astype(jnp.bfloat16)
        grad_ref[...] = grad
        store_gradient_chunks(out_refs, grad, act_ref, branch_ref, rms_ref)

    return local_kernel(
        kernel,
        place,
        [cot, back, a, sums, *passed],
        [bf16(rows, width), bf16(rows + TAIL, width), bf16(2 * rows + TAIL, width)],
    )


def block_products(tp, w_ref, codes, chunk_refs, rows, start, tile):
    width = w_ref.shape[0]
    total = None
    for code, chunk in zip(codes, chunk_refs):
        product = lax.dot_general(
            w_ref[start : start + tile, block_columns(tp, code, width)],
            chunk[:rows, :],
            (((1,), (1,)), ((), ())),
            preferred_element_type=jnp.float32,
        )
        total = product if total is None else total + product
    return total


def scaled_back(place, chunks, w_rows, codes, gain_row, only):
    width = w_rows.shape[0]
    rows = chunks[0].shape[0] - TAIL
    tile = min(width, 256)

    def kernel(tp, section, w_ref, gain_ref, *refs):
        @pl.when(section == only)
        def _():
            for start in range(0, width, tile):
                products = block_products(tp, w_ref, codes, refs[:-1], rows, start, tile)
                columns = slice(start, start + tile)
                refs[-1][:, columns] = gain_ref[:, columns] * products.T

    return local_kernel(
        kernel,
        place,
        [w_rows, gain_row] + chunks,
        [f32(rows, width)],
        cost=matmul_cost(rows, width, len(codes)),
    )[0]


def backward_half(place, chunks, w_rows, codes, rows):
    width = w_rows.shape[0]
    tile = min(width, 256)

    def kernel(tp, section, w_ref, *refs):
        chunk_refs, (out_ref, sum_ref) = refs[:-2], refs[-2:]
        for start in range(0, width, tile):
            out_ref[start : start + tile, :] = block_products(
                tp, w_ref, codes, chunk_refs, rows, start, tile
            )
        sum_ref[...] = tail_sum(chunk_refs, rows)

    return local_kernel(
        kernel,
        place,
        [w_rows] + chunks,
        [f32(width, rows), f32(TAIL, rows)],
        cost=matmul_cost(rows, width, len(codes)),
    )


def finish_backward(place, chunks, w_rows, codes, half, pack, gain_row, a, full_width, results, at, last_output=None, last=None):
    rows, width = a.shape
    chunk_rows = rows + TAIL
    count = len(codes)
    tile = min(width, 256)
    given = [] if last_output is None else [last_output]

    def kernel(tp, section, w_ref, *refs):
        chunk_refs = refs[:count]
        half_ref, sum_ref, pack_ref, gain_ref, a_ref, *old_refs = refs[count : count + 7]
        out_ref, *new_refs = refs[-3:]
        row_dot = as_column((sum_ref[...] + tail_sum(chunk_refs, rows))[:1])
        tail = pack_ref[rows:chunk_rows, :rows].astype(jnp.float32)
        rms = as_column(tail[1:2] + tail[2:3])
        scale = rms * rms * rms / full_width * row_dot
        for start in range(0, width, tile):
            products = block_products(tp, w_ref, codes, chunk_refs, rows, start, tile)
            back = (products + half_ref[start : start + tile, :]).T
            columns = slice(start, start + tile)
            out_ref[:, columns] = (
                pack_ref[:rows, columns].astype(jnp.float32)
                + rms * gain_ref[:, columns] * back
                - scale * a_ref[:, columns].astype(jnp.float32)
            ).astype(jnp.bfloat16)

        @pl.when(section == at)
        def _():
            new_refs[0][...] = out_ref[...]
            new_refs[1][...] = pack_ref[chunk_rows:, :]

        @pl.when(section != at)
        def _():
            for new, old in zip(new_refs, old_refs):
                new[...] = old[...]

        if given:

            @pl.when(section == last)
            def _():
                new_refs[1][...] = refs[count + 7][...]

    return local_kernel(
        kernel,
        place,
        [w_rows, *chunks, *half, pack, gain_row, a, *results] + given,
        [bf16(rows, width)] * 3,
        cost=matmul_cost(rows, width, count),
    )


def on_device(inputs, cotangent, weights, gains):
    section_count = lax.axis_size("section")
    tp_count = lax.axis_size("tp")
    micro_count, row_count, width = inputs.shape
    rows = micro_count * row_count
    full_width = weights.shape[2]
    last = section_count - 1
    place = jnp.stack([lax.axis_index("tp"), lax.axis_index("section")])
    across = tp_count // 2
    near = list(range(across - 1, 0, -1))
    near_codes = [0] + near
    far_codes = [across ^ e for e in near_codes]
    inside = [(last, last)]

    def across_route(beside, riding):
        if beside == last:
            return [(1, 1)] + inside
        return [(beside, beside)] + (inside if riding else [])

    def send(value, routes, step=0):
        pairs = [
            (source * tp_count + t, target * tp_count + (t ^ step))
            for source, target in routes
            for t in range(tp_count)
        ]
        return lax.ppermute(value, ("section", "tp"), pairs)

    cot = cotangent.reshape(rows, width)
    w_rows, cot_chunk = load(place, weights[0], cot)
    w_rows = pltpu.with_memory_space_constraint(w_rows, pltpu.VMEM)

    block_in = inputs.reshape(rows, width)
    block_ins = []
    passed = []
    other = cot_chunk
    cot_found = {0: cot_chunk}
    for section in range(last):
        beside = section ^ 1
        route = [(section, beside)]
        shared = section < 2
        first_pass = section == 0
        far = forward_blocks(
            place, block_in, gains, w_rows, far_codes, other=other if shared else None, other_at=last
        )
        far_route = route + inside if shared else route
        arrived = [send(chunk, far_route, e) for e, chunk in zip(near, far[1:])]
        own = forward_blocks(place, block_in, gains, w_rows, near_codes, pack=True)
        if shared:
            for e, chunk in zip(near, arrived):
                cot_found[e if first_pass else across ^ e] = chunk
        combined = add_chunks(
            place, [send(far[0], route)] + arrived, other if first_pass else None, last
        )
        crossed = send(combined, across_route(beside, first_pass), across)
        if first_pass:
            cot_found[across] = other = crossed
        direct = [send(chunk, route, e) for e, chunk in zip(near, own[1:])]
        passed.append(
            finish_forward(place, send(own[0], route), direct + [crossed], None, full_width)
        )
        block_ins.append(block_in)
        output = passed[-1][0]
        block_in = send(output, [(beside, section + 1)]) if section % 2 else output
        if section == 1:
            codes = sorted(cot_found)
            last_back = scaled_back(
                place, [cot_found[e] for e in codes], w_rows, codes, gains, last
            )

    sums = row_statistics(place, block_in, last_back)
    step = 1
    while step < tp_count:
        arriving = send(sums, ([(0, 1)] if step < across else [(1, 1)]) + inside, step)
        sums = add_chunks(place, [sums, arriving])
        step *= 2
    last_in = block_in
    grad, *first_chunks = last_gradient(
        place, cot, last_back, block_in, sums, passed[-1], full_width
    )
    results = (grad, grad)

    last_in, first_chunks = lax.optimization_barrier((last_in, first_chunks))
    last_far = forward_blocks(place, last_in, gains, w_rows, far_codes, only=last)
    last_own = forward_blocks(place, last_in, gains, w_rows, near_codes, only=last)
    last_output = None
    for section in range(last - 1, -1, -1):
        turn = last - 1 - section
        beside = section ^ 1
        route = [(beside, section)]
        if turn == 0:
            chunk, pack = first_chunks
        else:
            upstream = send(grad, [(section + 1, beside)]) if section % 2 else grad
            others = [None]
            if turn == 1:
                others = [None] + last_far[1:]
            if turn == 2:
                others = [last_combined] + last_own[1:]
            chunk, *near_chunks, pack = gradient_chunks(
                place, upstream, passed[section], others, last
            )
        riding = inside if turn in (1, 2) else []
        if not riding:
            near_chunks = [chunk] * len(near)
        crossed = send(chunk, across_route(beside, turn == 2), across)
        pack = send(pack, route)
        direct = [send(chunk, route + riding, e) for e, chunk in zip(near, near_chunks)]
        forwarded = [send(crossed, route)] + [send(crossed, route, e) for e in near]
        half = backward_half(place, [pack] + direct, w_rows, near_codes, rows)
        if turn == 1:
            last_combined = add_chunks(place, [last_far[0]] + direct)
        if turn == 2:
            last_output, _, _ = finish_forward(
                place, last_own[0], direct + [crossed], last_in, full_width
            )
        grad, *results = finish_backward(
            place,
            forwarded,
            w_rows,
            far_codes,
            half,
            pack,
            gains,
            block_ins[section],
            full_width,
            results,
            section,
            last_output if section == 0 else None,
            last,
        )
    grads, outputs = results
    shape = (1, micro_count, row_count, width)
    return outputs.reshape(shape), grads.reshape(shape)


def solution(mesh):
    placed = (
        P(None, None, "tp"),
        P(None, None, "tp"),
        P("section", "tp", None),
        P("section", "tp"),
    )
    return jax.shard_map(
        on_device,
        mesh=mesh,
        in_specs=placed,
        out_specs=(P("section", None, None, "tp"), P("section", None, None, "tp")),
        check_vma=False,
    )
```

```python
import jax
import jax.numpy as jnp
from jax import lax
from jax.experimental import pallas as pl
from jax.experimental.pallas import tpu as pltpu
from jax.sharding import PartitionSpec as P

EPSILON = 1e-05
MIB = 1 << 20
TAIL = 16
LANES = 128
SMEM_SPEC = pl.BlockSpec(memory_space=pltpu.SMEM)
VMEM_SPEC = pl.BlockSpec(memory_space=pltpu.VMEM)


def local_kernel(kernel, place, operands, out_shapes, limit=12 * MIB, cost=None, **options):
    def body(place_ref, *refs):
        kernel(place_ref[0], place_ref[1], *refs)

    options.setdefault("in_specs", [SMEM_SPEC] + [VMEM_SPEC] * len(operands))
    call = pl.pallas_call(
        body,
        out_shape=out_shapes,
        out_specs=[VMEM_SPEC] * len(out_shapes),
        compiler_params=pltpu.CompilerParams(vmem_limit_bytes=limit),
        cost_estimate=cost,
        **options,
    )
    return list(call(place, *operands))


def bf16(*shape):
    return jax.ShapeDtypeStruct(shape, jnp.bfloat16)


def f32(*shape):
    return jax.ShapeDtypeStruct(shape, jnp.float32)


def as_line(column):
    return jnp.broadcast_to(column, (column.shape[0], LANES)).T[:1]


def as_column(line):
    return jnp.broadcast_to(line, (LANES, line.shape[1])).T[:, :1]


def row_sum(value):
    return jnp.sum(value, axis=1, keepdims=True).astype(jnp.bfloat16).astype(jnp.float32)


def tail_sum(chunk_refs, rows):
    total = chunk_refs[0][rows : rows + TAIL, :rows].astype(jnp.float32)
    for chunk in chunk_refs[1:]:
        total = total + chunk[rows : rows + TAIL, :rows].astype(jnp.float32)
    return total


def matmul_cost(rows, width, count):
    return pl.CostEstimate(
        flops=2 * rows * width * width * count,
        bytes_accessed=2 * width * width * count,
        transcendentals=0,
    )


def in_hbm(array):
    return pltpu.with_memory_space_constraint(array, pltpu.HBM)


def in_vmem(array):
    return pltpu.with_memory_space_constraint(array, pltpu.VMEM)


def partial_chunks(tp, wide, gain_ref, take_block, out_refs):
    rows, width = wide.shape
    tile = min(width, 512)
    scaled = (wide * gain_ref[...]).astype(jnp.bfloat16)
    for number, out_ref in enumerate(out_refs):
        w_ref = take_block(number)
        for start in range(0, width, tile):
            partial = jnp.dot(
                scaled, w_ref[:, start : start + tile], preferred_element_type=jnp.float32
            )
            out_ref[:rows, start : start + tile] = partial.astype(jnp.bfloat16)
    line = as_line(jnp.sum(wide * wide, axis=1, keepdims=True))
    row_ids = lax.broadcasted_iota(jnp.int32, (TAIL, rows), 0)
    own_row = jnp.where(row_ids == tp % TAIL, jnp.broadcast_to(line, (TAIL, rows)), 0.0)
    for out_ref in out_refs:
        out_ref[rows : rows + TAIL, :] = jnp.zeros((TAIL, width), jnp.bfloat16)
        out_ref[rows : rows + TAIL, :rows] = own_row.astype(jnp.bfloat16)


def chunk_shapes(rows, width, count, pack):
    shapes = [bf16(rows + TAIL, width)] * count
    if pack:
        shapes[0] = bf16(2 * rows + TAIL, width)
    return shapes


def first_forward_blocks(place, a, gain_row, weights, codes, pack=False, other=None, other_at=None):
    rows, width = a.shape
    count = len(codes)
    others = [] if other is None else [other]

    def kernel(tp, section, a_hbm, gain_ref, w_hbm, *refs):
        w_ref, out_refs = refs[len(others)], refs[len(others) + 1 : len(others) + 1 + count]
        a_ref, a_done, w_done = refs[-3:]
        a_copy = pltpu.make_async_copy(a_hbm, a_ref, a_done)
        a_copy.start()
        copies = []
        for number, code in enumerate(codes):
            columns = pl.ds(pl.multiple_of((tp ^ code) * width, width), width)
            copies.append(
                pltpu.make_async_copy(w_hbm.at[:, columns], w_ref.at[number], w_done.at[number])
            )
            copies[-1].start()
        if others:
            chunk_ref = refs[len(others) + 1 + count]
            chunk_ref[:rows, :] = refs[0][...]
            chunk_ref[rows:, :] = jnp.zeros((TAIL, width), jnp.bfloat16)
        a_copy.wait()

        def take_block(number):
            copies[number].wait()
            return w_ref.at[number]

        partial_chunks(tp, a_ref[...].astype(jnp.float32), gain_ref, take_block, out_refs)
        if pack:
            out_refs[0][rows + TAIL :, :] = a_ref[...]
        if others:

            @pl.when(section == other_at)
            def _():
                for out_ref in out_refs:
                    out_ref[...] = chunk_ref[...]

    return local_kernel(
        kernel,
        place,
        [in_hbm(a), gain_row, in_hbm(weights)] + others,
        [pltpu.VMEM((count, width, width), jnp.bfloat16)]
        + chunk_shapes(rows, width, count, pack)
        + [bf16(rows + TAIL, width)] * len(others),
        in_specs=[SMEM_SPEC, pl.BlockSpec(memory_space=pltpu.HBM), VMEM_SPEC]
        + [pl.BlockSpec(memory_space=pltpu.HBM)]
        + [VMEM_SPEC] * len(others),
        scratch_shapes=[
            pltpu.VMEM((rows, width), jnp.bfloat16),
            pltpu.SemaphoreType.DMA,
            pltpu.SemaphoreType.DMA((count,)),
        ],
        cost=matmul_cost(rows, width, count),
    )


def forward_blocks(place, a, gain_row, w_half, pack=False, only=None, other=None, other_at=None):
    rows, width = a.shape
    count = w_half.shape[0]
    others = [] if other is None else [other]

    def kernel(tp, section, a_ref, gain_ref, w_ref, *refs):
        out_refs = refs[len(others) :]

        def work():
            wide = a_ref[...].astype(jnp.float32)
            partial_chunks(tp, wide, gain_ref, lambda number: w_ref.at[number], out_refs)
            if pack:
                out_refs[0][rows + TAIL :, :] = a_ref[...]

        if only is not None:
            pl.when(section == only)(work)
        else:
            work()
        if others:

            @pl.when(section == other_at)
            def _():
                for out_ref in out_refs:
                    out_ref[...] = refs[0][...]

    return local_kernel(
        kernel,
        place,
        [a, gain_row, w_half] + others,
        chunk_shapes(rows, width, count, pack),
        cost=matmul_cost(rows, width, count),
    )


def add_chunks(place, chunks, other=None, other_at=None):
    def kernel(tp, section, *refs):
        total = refs[0][...].astype(jnp.float32)
        for chunk in refs[1 : len(chunks)]:
            total = total + chunk[...].astype(jnp.float32)
        refs[-1][...] = total.astype(refs[-1].dtype)
        if other is not None:

            @pl.when(section == other_at)
            def _():
                refs[-1][...] = refs[len(chunks)][...]

    operands = chunks + ([] if other is None else [other])
    shape = jax.ShapeDtypeStruct(chunks[0].shape, chunks[0].dtype)
    return local_kernel(kernel, place, operands, [shape])[0]


def finish_forward(place, first, chunks, a, full_width):
    chunk_rows, width = chunks[0].shape
    rows = chunk_rows - TAIL
    given = [] if a is None else [a]

    def kernel(tp, section, first_ref, *refs):
        chunk_refs, (out_ref, branch_ref, rms_ref) = refs[: len(chunks)], refs[-3:]
        source = first_ref[chunk_rows:, :] if a is None else refs[len(chunks)][...]
        branch = first_ref[:rows, :].astype(jnp.float32)
        for chunk in chunk_refs:
            branch = branch + chunk[:rows, :].astype(jnp.float32)
        squares = jnp.sum(tail_sum((first_ref,) + chunk_refs, rows), axis=0, keepdims=True)
        inv_rms = lax.rsqrt(as_column(squares) / full_width + EPSILON)
        out_ref[...] = (source.astype(jnp.float32) + inv_rms * branch).astype(jnp.bfloat16)
        branch_ref[...] = branch
        rms_ref[...] = jnp.broadcast_to(inv_rms, (rows, LANES))

    return local_kernel(
        kernel,
        place,
        [first] + chunks + given,
        [bf16(rows, width), f32(rows, width), f32(rows, LANES)],
    )


def store_gradient_chunks(out_refs, grad, act_ref, branch_ref, rms_ref):
    rows, width = grad.shape
    chunk_rows = rows + TAIL
    dots = jnp.sum(grad.astype(jnp.float32) * branch_ref[...], axis=1, keepdims=True)
    rms_line = rms_ref[...].T[:1]
    rms_high = rms_line.astype(jnp.bfloat16).astype(jnp.float32)
    row_ids = lax.broadcasted_iota(jnp.int32, (TAIL, rows), 0)
    tile = jnp.where(row_ids == 0, as_line(dots), 0.0)
    tile = jnp.where(row_ids == 1, rms_high, tile)
    tile = jnp.where(row_ids == 2, rms_line - rms_high, tile).astype(jnp.bfloat16)
    for out_ref in out_refs:
        out_ref[:rows, :] = grad
        out_ref[rows:chunk_rows, :] = jnp.zeros((TAIL, width), jnp.bfloat16)
        out_ref[rows:chunk_rows, :rows] = tile
    out_refs[-1][chunk_rows:, :] = act_ref[...]


def gradient_chunks(place, upstream, passed, others, other_at):
    rows, width = upstream.shape
    replaced = [other for other in others if other is not None]

    def kernel(tp, section, up_ref, act_ref, branch_ref, rms_ref, *refs):
        other_refs, out_refs = list(refs[: len(replaced)]), refs[len(replaced) :]
        store_gradient_chunks(out_refs, up_ref[...], act_ref, branch_ref, rms_ref)
        if replaced:

            @pl.when(section == other_at)
            def _():
                for other, out_ref in zip(others, out_refs):
                    if other is not None:
                        out_ref[...] = other_refs.pop(0)[...]

    shapes = [bf16(rows + TAIL, width)] * len(others) + [bf16(2 * rows + TAIL, width)]
    return local_kernel(kernel, place, [upstream, *passed, *replaced], shapes)


def row_statistics(place, a, back):
    rows, _ = a.shape

    def kernel(tp, section, a_ref, back_ref, out_ref):
        wide = a_ref[...].astype(jnp.float32)
        row_ids = lax.broadcasted_iota(jnp.int32, (8, rows), 0)
        lines = jnp.where(row_ids == 0, as_line(row_sum(wide * wide)), 0.0)
        out_ref[...] = jnp.where(row_ids == 1, as_line(row_sum(wide * back_ref[...])), lines)

    return local_kernel(kernel, place, [a, back], [f32(8, rows)])[0]


def last_gradient(place, cot, back, a, sums, passed, full_width):
    rows, width = a.shape

    def kernel(tp, section, cot_ref, back_ref, a_ref, sums_ref, act_ref, branch_ref, rms_ref, grad_ref, *out_refs):
        squares = as_column(sums_ref[0:1, :])
        row_dot = as_column(sums_ref[1:2, :])
        rms = lax.rsqrt(squares / full_width + EPSILON)
        grad = (
            cot_ref[...].astype(jnp.float32)
            + rms * back_ref[...]
            - (rms * rms * rms / full_width * row_dot) * a_ref[...].astype(jnp.float32)
        ).astype(jnp.bfloat16)
        grad_ref[...] = grad
        store_gradient_chunks(out_refs, grad, act_ref, branch_ref, rms_ref)

    return local_kernel(
        kernel,
        place,
        [cot, back, a, sums, *passed],
        [bf16(rows, width), bf16(rows + TAIL, width), bf16(2 * rows + TAIL, width)],
    )


def block_products(blocks, rows, start, tile):
    total = None
    for w_ref, chunk in blocks:
        product = lax.dot_general(
            w_ref[start : start + tile, :],
            chunk[:rows, :],
            (((1,), (1,)), ((), ())),
            preferred_element_type=jnp.float32,
        )
        total = product if total is None else total + product
    return total


def scaled_back(place, halves, gain_row, only):
    w_far, w_near = halves[0][0], halves[1][0]
    count, width, _ = w_far.shape
    rows = halves[0][1][0].shape[0] - TAIL
    tile = min(width, 256)

    def kernel(tp, section, far_ref, near_ref, gain_ref, *refs):
        blocks = [(far_ref.at[k], refs[k]) for k in range(count)]
        blocks += [(near_ref.at[k], refs[count + k]) for k in range(count)]

        @pl.when(section == only)
        def _():
            for start in range(0, width, tile):
                columns = slice(start, start + tile)
                products = block_products(blocks, rows, start, tile)
                refs[-1][:, columns] = gain_ref[:, columns] * products.T

    return local_kernel(
        kernel,
        place,
        [w_far, w_near, gain_row] + halves[0][1] + halves[1][1],
        [f32(rows, width)],
        cost=matmul_cost(rows, width, 2 * count),
    )[0]


def backward_part(place, chunks, w_half, numbers, rows, before=None):
    width = w_half.shape[1]
    tile = min(width, 256)
    given = [] if before is None else list(before)

    def kernel(tp, section, w_ref, *refs):
        chunk_refs, (out_ref, sum_ref) = refs[: len(chunks)], refs[-2:]
        blocks = [(w_ref.at[k], chunk) for k, chunk in zip(numbers, chunk_refs)]
        for start in range(0, width, tile):
            products = block_products(blocks, rows, start, tile)
            if given:
                products = products + refs[len(chunks)][start : start + tile, :]
            out_ref[start : start + tile, :] = products
        sums = tail_sum(chunk_refs, rows)
        sum_ref[...] = sums + refs[len(chunks) + 1][...] if given else sums

    return local_kernel(
        kernel,
        place,
        [w_half] + chunks + given,
        [f32(width, rows), f32(TAIL, rows)],
        cost=matmul_cost(rows, width, len(chunks)),
    )


def finish_backward(
    place, chunks, w_half, numbers, before, pack, gain_row, a, full_width, results, at, last_output=None, last=None
):
    rows, width = a.shape
    chunk_rows = rows + TAIL
    count = len(chunks)
    tile = min(width, 256)
    given = [] if last_output is None else [last_output]

    def kernel(tp, section, w_ref, *refs):
        chunk_refs = refs[:count]
        half_ref, sum_ref, pack_ref, gain_ref, a_ref, *old_refs = refs[count : count + 7]
        out_ref, *new_refs = refs[-3:]
        row_dot = as_column((sum_ref[...] + tail_sum(chunk_refs, rows))[:1])
        tail = pack_ref[rows:chunk_rows, :rows].astype(jnp.float32)
        rms = as_column(tail[1:2] + tail[2:3])
        scale = rms * rms * rms / full_width * row_dot
        blocks = [(w_ref.at[k], chunk) for k, chunk in zip(numbers, chunk_refs)]
        for start in range(0, width, tile):
            products = block_products(blocks, rows, start, tile)
            back = (products + half_ref[start : start + tile, :]).T
            columns = slice(start, start + tile)
            out_ref[:, columns] = (
                pack_ref[:rows, columns].astype(jnp.float32)
                + rms * gain_ref[:, columns] * back
                - scale * a_ref[:, columns].astype(jnp.float32)
            ).astype(jnp.bfloat16)

        @pl.when(section == at)
        def _():
            new_refs[0][...] = out_ref[...]
            new_refs[1][...] = pack_ref[chunk_rows:, :]

        @pl.when(section != at)
        def _():
            for new, old in zip(new_refs, old_refs):
                new[...] = old[...]

        if given:

            @pl.when(section == last)
            def _():
                new_refs[1][...] = refs[count + 7][...]

    return local_kernel(
        kernel,
        place,
        [w_half, *chunks, *before, pack, gain_row, a, *results] + given,
        [bf16(rows, width)] * 3,
        cost=matmul_cost(rows, width, count),
    )


def on_device(inputs, cotangent, weights, gains):
    section_count = lax.axis_size("section")
    tp_count = lax.axis_size("tp")
    micro_count, row_count, width = inputs.shape
    rows = micro_count * row_count
    full_width = weights.shape[2]
    last = section_count - 1
    place = jnp.stack([lax.axis_index("tp"), lax.axis_index("section")])
    across = tp_count // 2
    near = list(range(across - 1, 0, -1))
    near_codes = [0] + near
    far_codes = [across ^ e for e in near_codes]
    inside = [(last, last)]

    def across_route(beside, riding):
        if beside == last:
            return [(1, 1)] + inside
        return [(beside, beside)] + (inside if riding else [])

    def send(value, routes, step=0):
        pairs = [
            (source * tp_count + t, target * tp_count + (t ^ step))
            for source, target in routes
            for t in range(tp_count)
        ]
        return lax.ppermute(value, ("section", "tp"), pairs)

    cot = cotangent.reshape(rows, width)

    block_in = inputs.reshape(rows, width)
    block_ins = []
    passed = []
    other = None
    cot_found = {}
    for section in range(last):
        beside = section ^ 1
        route = [(section, beside)]
        shared = section < 2
        first_pass = section == 0
        if first_pass:
            w_far, *far, other = first_forward_blocks(
                place, block_in, gains, weights[0], far_codes, other=cot, other_at=last
            )
            w_far = in_vmem(w_far)
            cot_found[0] = other
        else:
            far = forward_blocks(
                place, block_in, gains, w_far, other=other if shared else None, other_at=last
            )
        far_route = route + inside if shared else route
        arrived = [send(chunk, far_route, e) for e, chunk in zip(near, far[1:])]
        if first_pass:
            w_near, *own = first_forward_blocks(
                place, block_in, gains, weights[0], near_codes, pack=True
            )
            w_near = in_vmem(w_near)
        else:
            own = forward_blocks(place, block_in, gains, w_near, pack=True)
        if shared:
            for e, chunk in zip(near, arrived):
                cot_found[e if first_pass else across ^ e] = chunk
        combined = add_chunks(
            place, arrived + [send(far[0], route)], other if first_pass else None, last
        )
        crossed = send(combined, across_route(beside, first_pass), across)
        if first_pass:
            cot_found[across] = other = crossed
        direct = [send(chunk, route, e) for e, chunk in zip(near, own[1:])]
        passed.append(
            finish_forward(place, send(own[0], route), direct + [crossed], None, full_width)
        )
        block_ins.append(block_in)
        output = passed[-1][0]
        block_in = send(output, [(beside, section + 1)]) if section % 2 else output
        if section == 1:
            halves = [
                (half, [cot_found[code] for code in codes])
                for half, codes in ((w_far, far_codes), (w_near, near_codes))
            ]
            last_back = scaled_back(place, halves, gains, last)

    sums = row_statistics(place, block_in, last_back)
    step = 1
    while step < tp_count:
        arriving = send(sums, ([(0, 1)] if step < across else [(1, 1)]) + inside, step)
        sums = add_chunks(place, [sums, arriving])
        step *= 2
    last_in = block_in
    grad, *first_chunks = last_gradient(
        place, cot, last_back, block_in, sums, passed[-1], full_width
    )
    results = (grad, grad)

    last_in, first_chunks = lax.optimization_barrier((last_in, first_chunks))
    last_far = forward_blocks(place, last_in, gains, w_far, only=last)
    last_own = forward_blocks(place, last_in, gains, w_near, only=last)
    last_output = None
    for section in range(last - 1, -1, -1):
        turn = last - 1 - section
        beside = section ^ 1
        route = [(beside, section)]
        if turn == 0:
            chunk, pack = first_chunks
        else:
            upstream = send(grad, [(section + 1, beside)]) if section % 2 else grad
            others = [None]
            if turn == 1:
                others = [None] + last_far[1:]
            if turn == 2:
                others = [last_combined] + last_own[1:]
            chunk, *near_chunks, pack = gradient_chunks(
                place, upstream, passed[section], others, last
            )
        riding = inside if turn in (1, 2) else []
        if not riding:
            near_chunks = [chunk] * len(near)
        crossed = send(chunk, across_route(beside, turn == 2), across)
        pack = send(pack, route)
        direct = [send(chunk, route + riding, e) for e, chunk in zip(near, near_chunks)]
        forwarded = [send(crossed, route, e) for e in near] + [send(crossed, route)]
        numbers = list(range(1, across)) + [0]
        part = backward_part(place, direct + [pack], w_near, numbers, rows)
        middle = across // 2
        part = backward_part(
            place, forwarded[middle - 1 : -1], w_far, numbers[middle - 1 : -1], rows, part
        )
        if turn == 1:
            last_combined = add_chunks(place, [last_far[0]] + direct)
        if turn == 2:
            last_output, _, _ = finish_forward(
                place, last_own[0], direct + [crossed], last_in, full_width
            )
        grad, *results = finish_backward(
            place,
            forwarded[: middle - 1] + forwarded[-1:],
            w_far,
            numbers[: middle - 1] + numbers[-1:],
            part,
            pack,
            gains,
            block_ins[section],
            full_width,
            results,
            section,
            last_output if section == 0 else None,
            last,
        )
    grads, outputs = results
    shape = (1, micro_count, row_count, width)
    return outputs.reshape(shape), grads.reshape(shape)


def solution(mesh):
    placed = (
        P(None, None, "tp"),
        P(None, None, "tp"),
        P("section", "tp", None),
        P("section", "tp"),
    )
    return jax.shard_map(
        on_device,
        mesh=mesh,
        in_specs=placed,
        out_specs=(P("section", None, None, "tp"), P("section", None, None, "tp")),
        check_vma=False,
    )
```

```python
import jax
import jax.numpy as jnp
from jax import lax
from jax.experimental import pallas as pl
from jax.experimental.pallas import tpu as pltpu
from jax.sharding import PartitionSpec as P

EPSILON = 1e-05
MIB = 1 << 20
TAIL = 16
LANES = 128
SMEM_SPEC = pl.BlockSpec(memory_space=pltpu.SMEM)
VMEM_SPEC = pl.BlockSpec(memory_space=pltpu.VMEM)


def local_kernel(kernel, place, operands, out_shapes, limit=12 * MIB, cost=None, **options):
    def body(place_ref, *refs):
        kernel(place_ref[0], place_ref[1], *refs)

    options.setdefault("in_specs", [SMEM_SPEC] + [VMEM_SPEC] * len(operands))
    call = pl.pallas_call(
        body,
        out_shape=out_shapes,
        out_specs=[VMEM_SPEC] * len(out_shapes),
        compiler_params=pltpu.CompilerParams(vmem_limit_bytes=limit),
        cost_estimate=cost,
        **options,
    )
    return list(call(place, *operands))


def bf16(*shape):
    return jax.ShapeDtypeStruct(shape, jnp.bfloat16)


def f32(*shape):
    return jax.ShapeDtypeStruct(shape, jnp.float32)


def as_line(column):
    return jnp.broadcast_to(column, (column.shape[0], LANES)).T[:1]


def as_column(line):
    return jnp.broadcast_to(line, (LANES, line.shape[1])).T[:, :1]


def row_sum(value):
    return jnp.sum(value, axis=1, keepdims=True).astype(jnp.bfloat16).astype(jnp.float32)


def tail_sum(chunk_refs, rows):
    total = chunk_refs[0][rows : rows + TAIL, :rows].astype(jnp.float32)
    for chunk in chunk_refs[1:]:
        total = total + chunk[rows : rows + TAIL, :rows].astype(jnp.float32)
    return total


def matmul_cost(rows, width, count):
    return pl.CostEstimate(
        flops=2 * rows * width * width * count,
        bytes_accessed=2 * width * width * count,
        transcendentals=0,
    )


def in_hbm(array):
    return pltpu.with_memory_space_constraint(array, pltpu.HBM)


def in_vmem(array):
    return pltpu.with_memory_space_constraint(array, pltpu.VMEM)


def partial_chunks(tp, wide, gain_ref, take_block, out_refs):
    rows, width = wide.shape
    tile = min(width, 512)
    scaled = (wide * gain_ref[...]).astype(jnp.bfloat16)
    for number, out_ref in enumerate(out_refs):
        w_ref = take_block(number)
        for start in range(0, width, tile):
            partial = jnp.dot(
                scaled, w_ref[:, start : start + tile], preferred_element_type=jnp.float32
            )
            out_ref[:rows, start : start + tile] = partial.astype(jnp.bfloat16)
    line = as_line(jnp.sum(wide * wide, axis=1, keepdims=True))
    row_ids = lax.broadcasted_iota(jnp.int32, (TAIL, rows), 0)
    own_row = jnp.where(row_ids == tp % TAIL, jnp.broadcast_to(line, (TAIL, rows)), 0.0)
    for out_ref in out_refs:
        out_ref[rows : rows + TAIL, :] = jnp.zeros((TAIL, width), jnp.bfloat16)
        out_ref[rows : rows + TAIL, :rows] = own_row.astype(jnp.bfloat16)


def chunk_shapes(rows, width, count, pack):
    shapes = [bf16(rows + TAIL, width)] * count
    if pack:
        shapes[0] = bf16(2 * rows + TAIL, width)
    return shapes


def first_forward_blocks(place, a, gain_row, weights, codes, pack=False, other=None, other_from=None):
    rows, width = a.shape
    count = len(codes)
    others = [] if other is None else [other]

    def kernel(tp, section, a_hbm, gain_ref, w_hbm, *refs):
        w_ref, out_refs = refs[len(others)], refs[len(others) + 1 : len(others) + 1 + count]
        a_ref, a_done, w_done = refs[-3:]
        a_copy = pltpu.make_async_copy(a_hbm, a_ref, a_done)
        a_copy.start()
        copies = []
        for number, code in enumerate(codes):
            columns = pl.ds(pl.multiple_of((tp ^ code) * width, width), width)
            copies.append(
                pltpu.make_async_copy(w_hbm.at[:, columns], w_ref.at[number], w_done.at[number])
            )
            copies[-1].start()
        if others:
            chunk_ref = refs[len(others) + 1 + count]
            chunk_ref[:rows, :] = refs[0][...]
            chunk_ref[rows:, :] = jnp.zeros((TAIL, width), jnp.bfloat16)
        a_copy.wait()

        def take_block(number):
            copies[number].wait()
            return w_ref.at[number]

        partial_chunks(tp, a_ref[...].astype(jnp.float32), gain_ref, take_block, out_refs)
        if pack:
            out_refs[0][rows + TAIL :, :] = a_ref[...]
        if others:

            @pl.when(section >= other_from)
            def _():
                for out_ref in out_refs:
                    out_ref[...] = chunk_ref[...]

    return local_kernel(
        kernel,
        place,
        [in_hbm(a), gain_row, in_hbm(weights)] + others,
        [pltpu.VMEM((count, width, width), jnp.bfloat16)]
        + chunk_shapes(rows, width, count, pack)
        + [bf16(rows + TAIL, width)] * len(others),
        in_specs=[SMEM_SPEC, pl.BlockSpec(memory_space=pltpu.HBM), VMEM_SPEC]
        + [pl.BlockSpec(memory_space=pltpu.HBM)]
        + [VMEM_SPEC] * len(others),
        scratch_shapes=[
            pltpu.VMEM((rows, width), jnp.bfloat16),
            pltpu.SemaphoreType.DMA,
            pltpu.SemaphoreType.DMA((count,)),
        ],
        cost=matmul_cost(rows, width, count),
    )


def forward_blocks(place, a, gain_row, w_half, pack=False, only=None, other=None, other_from=None):
    rows, width = a.shape
    count = w_half.shape[0]
    others = [] if other is None else [other]

    def kernel(tp, section, a_ref, gain_ref, w_ref, *refs):
        out_refs = refs[len(others) :]

        def work():
            wide = a_ref[...].astype(jnp.float32)
            partial_chunks(tp, wide, gain_ref, lambda number: w_ref.at[number], out_refs)
            if pack:
                out_refs[0][rows + TAIL :, :] = a_ref[...]

        if only is not None:
            pl.when(section == only)(work)
        else:
            work()
        if others:

            @pl.when(section >= other_from)
            def _():
                for out_ref in out_refs:
                    out_ref[...] = refs[0][...]

    return local_kernel(
        kernel,
        place,
        [a, gain_row, w_half] + others,
        chunk_shapes(rows, width, count, pack),
        cost=matmul_cost(rows, width, count),
    )


def add_chunks(place, chunks, other=None, other_from=None):
    def kernel(tp, section, *refs):
        total = refs[0][...].astype(jnp.float32)
        for chunk in refs[1 : len(chunks)]:
            total = total + chunk[...].astype(jnp.float32)
        refs[-1][...] = total.astype(refs[-1].dtype)
        if other is not None:

            @pl.when(section >= other_from)
            def _():
                refs[-1][...] = refs[len(chunks)][...]

    operands = chunks + ([] if other is None else [other])
    shape = jax.ShapeDtypeStruct(chunks[0].shape, chunks[0].dtype)
    return local_kernel(kernel, place, operands, [shape])[0]


def finish_forward(place, first, chunks, a, full_width):
    chunk_rows, width = chunks[0].shape
    rows = chunk_rows - TAIL
    given = [] if a is None else [a]

    def kernel(tp, section, first_ref, *refs):
        chunk_refs, (out_ref, branch_ref, rms_ref) = refs[: len(chunks)], refs[-3:]
        source = first_ref[chunk_rows:, :] if a is None else refs[len(chunks)][...]
        branch = first_ref[:rows, :].astype(jnp.float32)
        for chunk in chunk_refs:
            branch = branch + chunk[:rows, :].astype(jnp.float32)
        squares = jnp.sum(tail_sum((first_ref,) + chunk_refs, rows), axis=0, keepdims=True)
        inv_rms = lax.rsqrt(as_column(squares) / full_width + EPSILON)
        out_ref[...] = (source.astype(jnp.float32) + inv_rms * branch).astype(jnp.bfloat16)
        branch_ref[...] = branch
        rms_ref[...] = jnp.broadcast_to(inv_rms, (rows, LANES))

    return local_kernel(
        kernel,
        place,
        [first] + chunks + given,
        [bf16(rows, width), f32(rows, width), f32(rows, LANES)],
    )


def two_parts(line):
    high = line.astype(jnp.bfloat16).astype(jnp.float32)
    return [high, line - high]


def store_tail(out_ref, rows, lines):
    row_ids = lax.broadcasted_iota(jnp.int32, (TAIL, rows), 0)
    tile = jnp.zeros((TAIL, rows), jnp.float32)
    for number, line in enumerate(lines):
        tile = jnp.where(row_ids == number, line, tile)
    out_ref[rows:, :] = jnp.zeros((TAIL, out_ref.shape[1]), out_ref.dtype)
    out_ref[rows:, :rows] = tile.astype(out_ref.dtype)


def row_line(value):
    return as_line(jnp.sum(value, axis=1, keepdims=True))


def gradient_chunks(place, upstream, branch, inv_rms, others, other_at):
    rows, width = upstream.shape
    replaced = [other for other in others if other is not None]

    def kernel(tp, section, up_ref, branch_ref, rms_ref, *refs):
        other_refs, out_refs = list(refs[: len(replaced)]), refs[len(replaced) :]
        dots = row_line(up_ref[...].astype(jnp.float32) * branch_ref[...])
        lines = [dots] + two_parts(rms_ref[...].T[:1])
        for out_ref in out_refs:
            out_ref[:rows, :] = up_ref[...]
            store_tail(out_ref, rows, lines)
        if replaced:

            @pl.when(section == other_at)
            def _():
                for other, out_ref in zip(others, out_refs):
                    if other is not None:
                        out_ref[...] = other_refs.pop(0)[...]

    shapes = [bf16(rows + TAIL, width)] * len(others)
    return local_kernel(kernel, place, [upstream, branch, inv_rms, *replaced], shapes)


def statistics_chunk(place, a, back_chunk, cot, branch, inv_rms):
    rows, width = a.shape

    def kernel(tp, section, a_ref, back_ref, cot_ref, branch_ref, rms_ref, out_ref):
        wide = a_ref[...].astype(jnp.float32)
        back = back_ref[:rows, :].astype(jnp.float32)
        cot_wide = cot_ref[...].astype(jnp.float32)
        lines = []
        for product in (
            wide * wide,
            wide * back,
            cot_wide * branch_ref[...],
            back * branch_ref[...],
            wide * branch_ref[...],
        ):
            lines += two_parts(row_line(product))
        out_ref[:rows, :] = a_ref[...]
        store_tail(out_ref, rows, lines + two_parts(rms_ref[...].T[:1]))

    return local_kernel(
        kernel, place, [a, back_chunk, cot, branch, inv_rms], [bf16(rows + TAIL, width)]
    )[0]


def block_products(blocks, rows, start, tile):
    total = None
    for w_ref, chunk in blocks:
        product = lax.dot_general(
            w_ref[start : start + tile, :],
            chunk[:rows, :],
            (((1,), (1,)), ((), ())),
            preferred_element_type=jnp.float32,
        )
        total = product if total is None else total + product
    return total


def all_products(place, chunk_sets, w_far, w_near, only, gain_row=None):
    count, width, _ = w_far.shape
    rows = chunk_sets[0][0].shape[0] - TAIL
    tile = min(width, 256)
    given = [] if gain_row is None else [gain_row]

    def kernel(tp, section, far_ref, near_ref, *refs):
        w_refs = [far_ref.at[k] for k in range(count)] + [near_ref.at[k] for k in range(count)]
        chunk_refs = refs[len(given) : -len(chunk_sets)]

        @pl.when(section == only)
        def _():
            for number, out_ref in enumerate(refs[-len(chunk_sets) :]):
                chunks = chunk_refs[2 * count * number : 2 * count * (number + 1)]
                for start in range(0, width, tile):
                    products = block_products(list(zip(w_refs, chunks)), rows, start, tile)
                    columns = slice(start, start + tile)
                    if given:
                        back = refs[0][:, columns] * products.T
                        out_ref[:rows, columns] = back.astype(jnp.bfloat16)
                    else:
                        out_ref[columns, :] = products
                if given:
                    out_ref[rows:, :] = jnp.zeros((TAIL, width), jnp.bfloat16)

    shape = f32(width, rows) if gain_row is None else bf16(rows + TAIL, width)
    return local_kernel(
        kernel,
        place,
        [w_far, w_near] + given + [chunk for chunks in chunk_sets for chunk in chunks],
        [shape] * len(chunk_sets),
        cost=matmul_cost(rows, width, 2 * count * len(chunk_sets)),
    )


def backward_part(place, chunks, w_half, numbers, rows, before=None):
    width = w_half.shape[1]
    tile = min(width, 256)
    given = [] if before is None else list(before)

    def kernel(tp, section, w_ref, *refs):
        chunk_refs, (out_ref, sum_ref) = refs[: len(chunks)], refs[-2:]
        blocks = [(w_ref.at[k], chunk) for k, chunk in zip(numbers, chunk_refs)]
        for start in range(0, width, tile):
            products = block_products(blocks, rows, start, tile)
            if given:
                products = products + refs[len(chunks)][start : start + tile, :]
            out_ref[start : start + tile, :] = products
        sums = tail_sum(chunk_refs, rows)
        sum_ref[...] = sums + refs[len(chunks) + 1][...] if given else sums

    return local_kernel(
        kernel,
        place,
        [w_half] + chunks + given,
        [f32(width, rows), f32(TAIL, rows)],
        cost=matmul_cost(rows, width, len(chunks)),
    )


def finish_backward(place, chunks, w_half, numbers, before, own, gain_row, a, full_width, last_block=None, finals=()):
    rows, width = a.shape
    chunk_rows = rows + TAIL
    count = len(chunks)
    tile = min(width, 256)
    extra = [] if last_block is None else list(last_block)
    chosen = [[array for array in arrays if array is not None] for arrays in finals]

    def kernel(tp, section, w_ref, *refs):
        chunk_refs = refs[:count]
        before_ref, sum_ref, own_ref, gain_ref, a_ref = refs[count : count + 5]
        rest = list(refs[count + 5 :])
        out_refs = rest[len(extra) + sum(len(arrays) for arrays in chosen) :]
        out_ref = out_refs[0]
        sums = sum_ref[...] + tail_sum(chunk_refs, rows)
        tail = own_ref[rows:chunk_rows, :rows].astype(jnp.float32)

        def pair(lines, number):
            return lines[number : number + 1] + lines[number + 1 : number + 2]

        if extra:
            cot_ref, gained_ref, cot_products, gained_products = rest[:4]
            last_rms = lax.rsqrt(pair(sums, 0) / full_width + EPSILON)
            last_scale = last_rms * last_rms * last_rms / full_width * pair(sums, 2)
            dots = pair(sums, 4) + last_rms * pair(sums, 6) - last_scale * pair(sums, 8)
            rms = as_column(pair(tail, 10))
            rms_column, scale_column = as_column(last_rms), as_column(last_scale)
            out_refs[1][...] = (
                cot_ref[...].astype(jnp.float32)
                + rms_column * gained_ref[:rows, :].astype(jnp.float32)
                - scale_column * own_ref[:rows, :].astype(jnp.float32)
            ).astype(jnp.bfloat16)
            up_ref = out_refs[1]
        else:
            dots = sums[:1]
            rms = as_column(pair(tail, 1))
            up_ref = own_ref
        scale = rms * rms * rms / full_width * as_column(dots)
        blocks = [(w_ref.at[k], chunk) for k, chunk in zip(numbers, chunk_refs)]
        for start in range(0, width, tile):
            columns = slice(start, start + tile)
            products = block_products(blocks, rows, start, tile) + before_ref[columns, :]
            if extra:
                products = (
                    cot_products[columns, :]
                    + last_rms * gained_products[columns, :]
                    - last_scale * products
                )
            out_ref[:, columns] = (
                up_ref[:rows, columns].astype(jnp.float32)
                + rms * gain_ref[:, columns] * products.T
                - scale * a_ref[:, columns].astype(jnp.float32)
            ).astype(jnp.bfloat16)
        final_refs = rest[len(extra) :]
        for arrays, final_ref in zip(finals, out_refs[1 + bool(extra) :]):
            for number, array in enumerate(arrays):
                source = out_ref if array is None else final_refs.pop(0)

                @pl.when(section == number)
                def _(source=source, final_ref=final_ref):
                    final_ref[...] = source[...]

    return local_kernel(
        kernel,
        place,
        [w_half, *chunks, *before, own, gain_row, a, *extra]
        + [array for arrays in chosen for array in arrays],
        [bf16(rows, width)] * (1 + bool(extra) + len(finals)),
        cost=matmul_cost(rows, width, count),
    )


def on_device(inputs, cotangent, weights, gains):
    section_count = lax.axis_size("section")
    tp_count = lax.axis_size("tp")
    micro_count, row_count, width = inputs.shape
    rows = micro_count * row_count
    full_width = weights.shape[2]
    last = section_count - 1
    below = last - 1
    place = jnp.stack([lax.axis_index("tp"), lax.axis_index("section")])
    across = tp_count // 2
    near = list(range(across - 1, 0, -1))
    near_codes = [0] + near
    far_codes = [across ^ e for e in near_codes]
    numbers = {code: number for number, code in enumerate(near_codes)}
    inside = [(below, below), (last, last)]

    def send(value, routes, step=0):
        pairs = [
            (source * tp_count + t, target * tp_count + (t ^ step))
            for source, target in routes
            for t in range(tp_count)
        ]
        return lax.ppermute(value, ("section", "tp"), pairs)

    def across_route(section, riding=False):
        if section == 1 or riding:
            return [(section, section)] + inside
        return [(section, section)]

    def gather(chunk, source, target, near_chunks=None, riding=(), across_riding=False):
        route = [(source, target)]
        crossed = send(chunk, across_route(source, across_riding), across)
        found = [send(chunk, route)]
        for e in reversed(near):
            near_chunk = near_chunks[e] if near_chunks else chunk
            found.append(send(near_chunk, route + list(riding), e))
        forwarded = [send(crossed, route)]
        forwarded += [send(crossed, route, e) for e in reversed(near)]
        return found, forwarded, crossed

    cot = cotangent.reshape(rows, width)

    block_in = inputs.reshape(rows, width)
    block_ins = []
    passed = []
    other = None
    cot_found = {}
    for section in range(last):
        beside = section ^ 1
        route = [(section, beside)]
        shared = section < 2
        first_pass = section == 0
        if first_pass:
            w_far, *far, other = first_forward_blocks(
                place, block_in, gains, weights[0], far_codes, other=cot, other_from=below
            )
            w_far = in_vmem(w_far)
            cot_found[0] = other
        else:
            far = forward_blocks(
                place, block_in, gains, w_far, other=other if shared else None, other_from=below
            )
        far_route = route + inside if shared else route
        arrived = [send(chunk, far_route, e) for e, chunk in zip(near, far[1:])]
        if first_pass:
            w_near, *own = first_forward_blocks(
                place, block_in, gains, weights[0], near_codes, pack=True
            )
            w_near = in_vmem(w_near)
        else:
            own = forward_blocks(place, block_in, gains, w_near, pack=True)
        if shared:
            for e, chunk in zip(near, arrived):
                cot_found[e if first_pass else across ^ e] = chunk
        far_own = send(far[0], route)
        combined = add_chunks(
            place, arrived + [far_own], other if first_pass else None, below
        )
        pack, _ = lax.optimization_barrier((own[0], far_own))
        crossed = send(combined, across_route(beside), across)
        if first_pass:
            cot_found[across] = other = crossed
        direct = [send(chunk, route, e) for e, chunk in zip(near, own[1:])]
        passed.append(
            finish_forward(place, send(pack, route), direct + [crossed], None, full_width)
        )
        block_ins.append(block_in)
        output = passed[-1][0]
        block_in = send(output, [(beside, section + 1)]) if section % 2 else output
        if section == 1:
            cot_chunks = [cot_found[code] for code in far_codes + near_codes]
            cot_chunks, output = lax.optimization_barrier((cot_chunks, output))
            gained = all_products(place, [cot_chunks], w_far, w_near, last, gains)[0]
            found, forwarded, _ = gather(gained, last, below)
            block_in, found, forwarded = lax.optimization_barrier((block_in, found, forwarded))
            gained_own = found[0]
            order = [0] + list(reversed(near))
            gained_found = {code: chunk for code, chunk in zip(order, found)}
            gained_found.update({across ^ code: chunk for code, chunk in zip(order, forwarded)})
            gained_chunks = [gained_found[code] for code in far_codes + near_codes]

    products = all_products(place, [cot_chunks, gained_chunks], w_far, w_near, below)
    last_in = block_in
    chunk = statistics_chunk(place, block_in, gained, cot, *passed[below][1:])
    grads = [None] * section_count
    acts = [None] * section_count
    for section in range(below, -1, -1):
        turn = below - section
        beside = section ^ 1
        near_chunks, riding = None, ()
        if turn:
            upstream = send(grad, [(section + 1, beside)]) if section % 2 else grad
            others = [None]
            if turn == 1:
                others += last_far[1:]
            if turn == 2:
                others = [last_combined] + last_own[1:]
            chunk, *rest = gradient_chunks(place, upstream, *passed[section][1:], others, last)
            if turn <= 2:
                near_chunks, riding = dict(zip(near, rest)), inside
        found, forwarded, crossed = gather(
            chunk, beside, section, near_chunks, riding, across_riding=turn == 2
        )
        part = backward_part(
            place, found, w_near, [numbers[e] for e in [0] + list(reversed(near))], rows
        )
        early = [0] + near[: max(1, across // 4)]
        late = [e for e in reversed(near) if e not in early]
        by_code = dict(zip([0] + list(reversed(near)), forwarded))
        part = backward_part(
            place, [by_code[e] for e in early], w_far, [numbers[e] for e in early], rows, part
        )
        if turn == 1:
            last_combined = add_chunks(place, [last_far[0]] + found[1:])
        if turn == 2:
            last_output, _, _ = finish_forward(
                place, last_own[0], found[1:] + [crossed], last_in, full_width
            )
            acts[last] = last_output
        finish = [
            place,
            [by_code[e] for e in late],
            w_far,
            [numbers[e] for e in late],
            part,
            found[0],
            gains,
            block_ins[section],
            full_width,
        ]
        if turn == 0:
            grad, last_grad = finish_backward(*finish, [cot, gained_own, *products])
            acts[:below] = [
                send(passed[number][0], [(number ^ 1, number)]) for number in range(below)
            ]
            grad, last_grad, last_in, acts[:below] = lax.optimization_barrier(
                (grad, last_grad, last_in, acts[:below])
            )
            last_far = forward_blocks(place, last_in, gains, w_far, only=last)
            last_own = forward_blocks(place, last_in, gains, w_near, only=last)
        elif section:
            (grad,) = finish_backward(*finish)
        else:
            grad, own_grad, own_output = finish_backward(*finish, None, [grads, acts])
        if turn == 1:
            grads[last] = send(last_grad, [(below, last)])
            acts[below] = send(passed[below][0], [(last, below)])
            grad, grads[last], acts[below] = lax.optimization_barrier(
                (grad, grads[last], acts[below])
            )
        if section:
            grads[section] = grad
    shape = (1, micro_count, row_count, width)
    return own_output.reshape(shape), own_grad.reshape(shape)


def solution(mesh):
    placed = (
        P(None, None, "tp"),
        P(None, None, "tp"),
        P("section", "tp", None),
        P("section", "tp"),
    )
    return jax.shard_map(
        on_device,
        mesh=mesh,
        in_specs=placed,
        out_specs=(P("section", None, None, "tp"), P("section", None, None, "tp")),
        check_vma=False,
    )
```

```python
import jax
import jax.numpy as jnp
from jax import lax
from jax.experimental import pallas as pl
from jax.experimental.pallas import tpu as pltpu
from jax.sharding import PartitionSpec as P

EPSILON = 1e-05
MIB = 1 << 20
TAIL = 16
LANES = 128
SMEM_SPEC = pl.BlockSpec(memory_space=pltpu.SMEM)
VMEM_SPEC = pl.BlockSpec(memory_space=pltpu.VMEM)


def local_kernel(kernel, place, operands, out_shapes, limit=12 * MIB, cost=None, **options):
    def body(place_ref, *refs):
        kernel(place_ref[0], place_ref[1], *refs)

    options.setdefault("in_specs", [SMEM_SPEC] + [VMEM_SPEC] * len(operands))
    call = pl.pallas_call(
        body,
        out_shape=out_shapes,
        out_specs=[VMEM_SPEC] * len(out_shapes),
        compiler_params=pltpu.CompilerParams(vmem_limit_bytes=limit),
        cost_estimate=cost,
        **options,
    )
    return list(call(place, *operands))


def bf16(*shape):
    return jax.ShapeDtypeStruct(shape, jnp.bfloat16)


def f32(*shape):
    return jax.ShapeDtypeStruct(shape, jnp.float32)


def as_line(column):
    return jnp.broadcast_to(column, (column.shape[0], LANES)).T[:1]


def as_column(line):
    return jnp.broadcast_to(line, (LANES, line.shape[1])).T[:, :1]


def row_sum(value):
    return jnp.sum(value, axis=1, keepdims=True).astype(jnp.bfloat16).astype(jnp.float32)


def tail_sum(chunk_refs, rows):
    total = chunk_refs[0][rows : rows + TAIL, :rows].astype(jnp.float32)
    for chunk in chunk_refs[1:]:
        total = total + chunk[rows : rows + TAIL, :rows].astype(jnp.float32)
    return total


def matmul_cost(rows, width, count):
    return pl.CostEstimate(
        flops=2 * rows * width * width * count,
        bytes_accessed=2 * width * width * count,
        transcendentals=0,
    )


def in_hbm(array):
    return pltpu.with_memory_space_constraint(array, pltpu.HBM)


def in_vmem(array):
    return pltpu.with_memory_space_constraint(array, pltpu.VMEM)


def partial_chunks(tp, wide, gain_ref, take_block, out_refs):
    rows, width = wide.shape
    tile = min(width, 512)
    scaled = (wide * gain_ref[...]).astype(jnp.bfloat16)
    for number, out_ref in enumerate(out_refs):
        w_ref = take_block(number)
        for start in range(0, width, tile):
            partial = jnp.dot(
                scaled, w_ref[:, start : start + tile], preferred_element_type=jnp.float32
            )
            out_ref[:rows, start : start + tile] = partial.astype(jnp.bfloat16)
    line = as_line(jnp.sum(wide * wide, axis=1, keepdims=True))
    row_ids = lax.broadcasted_iota(jnp.int32, (TAIL, rows), 0)
    own_row = jnp.where(row_ids == tp % TAIL, jnp.broadcast_to(line, (TAIL, rows)), 0.0)
    for out_ref in out_refs:
        out_ref[rows : rows + TAIL, :] = jnp.zeros((TAIL, width), jnp.bfloat16)
        out_ref[rows : rows + TAIL, :rows] = own_row.astype(jnp.bfloat16)


def chunk_shapes(rows, width, count, pack):
    shapes = [bf16(rows + TAIL, width)] * count
    if pack:
        shapes[0] = bf16(2 * rows + TAIL, width)
    return shapes


def first_forward_blocks(place, a, gain_row, weights, codes, pack=False, other=None, other_from=None):
    rows, width = a.shape
    count = len(codes)
    others = [] if other is None else [other]

    def kernel(tp, section, a_hbm, gain_ref, w_hbm, *refs):
        w_ref, out_refs = refs[len(others)], refs[len(others) + 1 : len(others) + 1 + count]
        a_ref, a_done, w_done = refs[-3:]
        a_copy = pltpu.make_async_copy(a_hbm, a_ref, a_done)
        a_copy.start()
        copies = []
        for number, code in enumerate(codes):
            columns = pl.ds(pl.multiple_of((tp ^ code) * width, width), width)
            copies.append(
                pltpu.make_async_copy(w_hbm.at[:, columns], w_ref.at[number], w_done.at[number])
            )
            copies[-1].start()
        if others:
            chunk_ref = refs[len(others) + 1 + count]
            chunk_ref[:rows, :] = refs[0][...]
            chunk_ref[rows:, :] = jnp.zeros((TAIL, width), jnp.bfloat16)
        a_copy.wait()

        def take_block(number):
            copies[number].wait()
            return w_ref.at[number]

        partial_chunks(tp, a_ref[...].astype(jnp.float32), gain_ref, take_block, out_refs)
        if pack:
            out_refs[0][rows + TAIL :, :] = a_ref[...]
        if others:

            @pl.when(section >= other_from)
            def _():
                for out_ref in out_refs:
                    out_ref[...] = chunk_ref[...]

    return local_kernel(
        kernel,
        place,
        [in_hbm(a), gain_row, in_hbm(weights)] + others,
        [pltpu.VMEM((count, width, width), jnp.bfloat16)]
        + chunk_shapes(rows, width, count, pack)
        + [bf16(rows + TAIL, width)] * len(others),
        in_specs=[SMEM_SPEC, pl.BlockSpec(memory_space=pltpu.HBM), VMEM_SPEC]
        + [pl.BlockSpec(memory_space=pltpu.HBM)]
        + [VMEM_SPEC] * len(others),
        scratch_shapes=[
            pltpu.VMEM((rows, width), jnp.bfloat16),
            pltpu.SemaphoreType.DMA,
            pltpu.SemaphoreType.DMA((count,)),
        ],
        cost=matmul_cost(rows, width, count),
    )


def forward_blocks(place, a, gain_row, w_half, pack=False, only=None, other=None, other_from=None):
    rows, width = a.shape
    count = w_half.shape[0]
    others = [] if other is None else [other]

    def kernel(tp, section, a_ref, gain_ref, w_ref, *refs):
        out_refs = refs[len(others) :]

        def work():
            wide = a_ref[...].astype(jnp.float32)
            partial_chunks(tp, wide, gain_ref, lambda number: w_ref.at[number], out_refs)
            if pack:
                out_refs[0][rows + TAIL :, :] = a_ref[...]

        if only is not None:
            pl.when(section == only)(work)
        else:
            work()
        if others:

            @pl.when(section >= other_from)
            def _():
                for out_ref in out_refs:
                    out_ref[...] = refs[0][...]

    return local_kernel(
        kernel,
        place,
        [a, gain_row, w_half] + others,
        chunk_shapes(rows, width, count, pack),
        cost=matmul_cost(rows, width, count),
    )


def add_chunks(place, chunks, other=None, other_from=None, only=None):
    def kernel(tp, section, *refs):
        def work():
            total = refs[0][...].astype(jnp.float32)
            for chunk in refs[1 : len(chunks)]:
                total = total + chunk[...].astype(jnp.float32)
            refs[-1][...] = total.astype(refs[-1].dtype)

        if only is not None:
            pl.when(section == only)(work)
        else:
            work()
        if other is not None:

            @pl.when(section >= other_from)
            def _():
                refs[-1][...] = refs[len(chunks)][...]

    operands = chunks + ([] if other is None else [other])
    shape = jax.ShapeDtypeStruct(chunks[0].shape, chunks[0].dtype)
    return local_kernel(kernel, place, operands, [shape])[0]


def finish_forward(place, first, chunks, a, full_width, only=None):
    chunk_rows, width = chunks[0].shape
    rows = chunk_rows - TAIL
    given = [] if a is None else [a]

    def kernel(tp, section, first_ref, *refs):
        chunk_refs, (out_ref, branch_ref, rms_ref) = refs[: len(chunks)], refs[-3:]
        def work():
            source = first_ref[chunk_rows:, :] if a is None else refs[len(chunks)][...]
            branch = first_ref[:rows, :].astype(jnp.float32)
            for chunk in chunk_refs:
                branch = branch + chunk[:rows, :].astype(jnp.float32)
            squares = jnp.sum(tail_sum((first_ref,) + chunk_refs, rows), axis=0, keepdims=True)
            inv_rms = lax.rsqrt(as_column(squares) / full_width + EPSILON)
            out_ref[...] = (source.astype(jnp.float32) + inv_rms * branch).astype(jnp.bfloat16)
            branch_ref[...] = branch
            rms_ref[...] = jnp.broadcast_to(inv_rms, (rows, LANES))

        if only is not None:
            pl.when(section == only)(work)
        else:
            work()

    return local_kernel(
        kernel,
        place,
        [first] + chunks + given,
        [bf16(rows, width), f32(rows, width), f32(rows, LANES)],
    )


def two_parts(line):
    high = line.astype(jnp.bfloat16).astype(jnp.float32)
    return [high, line - high]


def store_tail(out_ref, rows, lines):
    row_ids = lax.broadcasted_iota(jnp.int32, (TAIL, rows), 0)
    tile = jnp.zeros((TAIL, rows), jnp.float32)
    for number, line in enumerate(lines):
        tile = jnp.where(row_ids == number, line, tile)
    out_ref[rows:, :] = jnp.zeros((TAIL, out_ref.shape[1]), out_ref.dtype)
    out_ref[rows:, :rows] = tile.astype(out_ref.dtype)


def row_line(value):
    return as_line(jnp.sum(value, axis=1, keepdims=True))


def gradient_chunks(place, upstream, branch, inv_rms, others, other_at):
    rows, width = upstream.shape
    replaced = [other for other in others if other is not None]

    def kernel(tp, section, up_ref, branch_ref, rms_ref, *refs):
        other_refs, out_refs = list(refs[: len(replaced)]), refs[len(replaced) :]
        dots = row_line(up_ref[...].astype(jnp.float32) * branch_ref[...])
        lines = [dots] + two_parts(rms_ref[...].T[:1])
        for out_ref in out_refs:
            out_ref[:rows, :] = up_ref[...]
            store_tail(out_ref, rows, lines)
        if replaced:

            @pl.when(section == other_at)
            def _():
                for other, out_ref in zip(others, out_refs):
                    if other is not None:
                        out_ref[...] = other_refs.pop(0)[...]

    shapes = [bf16(rows + TAIL, width)] * len(others)
    return local_kernel(kernel, place, [upstream, branch, inv_rms, *replaced], shapes)


def statistics_chunk(place, a, back_chunk, cot, branch, inv_rms):
    rows, width = a.shape

    def kernel(tp, section, a_ref, back_ref, cot_ref, branch_ref, rms_ref, out_ref):
        wide = a_ref[...].astype(jnp.float32)
        back = back_ref[:rows, :].astype(jnp.float32)
        cot_wide = cot_ref[...].astype(jnp.float32)
        lines = []
        for product in (
            wide * wide,
            wide * back,
            cot_wide * branch_ref[...],
            back * branch_ref[...],
            wide * branch_ref[...],
        ):
            lines += two_parts(row_line(product))
        out_ref[:rows, :] = a_ref[...]
        store_tail(out_ref, rows, lines + two_parts(rms_ref[...].T[:1]))

    return local_kernel(
        kernel, place, [a, back_chunk, cot, branch, inv_rms], [bf16(rows + TAIL, width)]
    )[0]


def block_products(blocks, rows, start, tile):
    total = None
    for w_ref, chunk in blocks:
        product = lax.dot_general(
            w_ref[start : start + tile, :],
            chunk[:rows, :],
            (((1,), (1,)), ((), ())),
            preferred_element_type=jnp.float32,
        )
        total = product if total is None else total + product
    return total


def gained_chunks(place, chunks, w_far, w_near, gain_row, only):
    count, width, _ = w_far.shape
    chunk_rows = chunks[0].shape[0]
    rows = chunk_rows - TAIL
    tile = min(width, 256)

    def kernel(tp, section, far_ref, near_ref, gain_ref, *refs):
        w_refs = [far_ref.at[k] for k in range(count)] + [near_ref.at[k] for k in range(count)]
        chunk_refs, (out_ref, pack_ref) = refs[:-2], refs[-2:]

        @pl.when(section == only)
        def _():
            for start in range(0, width, tile):
                columns = slice(start, start + tile)
                products = block_products(list(zip(w_refs, chunk_refs)), rows, start, tile)
                back = gain_ref[:, columns] * products.T
                out_ref[:rows, columns] = back.astype(jnp.bfloat16)
            out_ref[rows:, :] = jnp.zeros((TAIL, width), jnp.bfloat16)
            for number, chunk in enumerate([out_ref] + list(chunk_refs)):
                pack_ref[number * chunk_rows : (number + 1) * chunk_rows, :] = chunk[...]

    return local_kernel(
        kernel,
        place,
        [w_far, w_near, gain_row] + chunks,
        [bf16(chunk_rows, width), bf16((1 + len(chunks)) * chunk_rows, width)],
        cost=matmul_cost(rows, width, 2 * count),
    )


def early_products(place, pack, gained, w_far, w_near, only):
    count, width, _ = w_far.shape
    given = [chunk for chunk in gained if chunk is not None]
    chunk_rows = given[0].shape[0]
    rows = chunk_rows - TAIL
    tile = min(width, 256)

    def kernel(tp, section, far_ref, near_ref, pack_ref, *refs):
        w_refs = [far_ref.at[k] for k in range(count)] + [near_ref.at[k] for k in range(count)]
        packed = [pack_ref.at[pl.ds(k * chunk_rows, chunk_rows), :] for k in range(1 + 2 * count)]
        gained_refs = list(refs[:-2])
        gained_refs = [packed[0] if chunk is None else gained_refs.pop(0) for chunk in gained]

        @pl.when(section == only)
        def _():
            for chunk_refs, out_ref in zip((packed[1:], gained_refs), refs[-2:]):
                for start in range(0, width, tile):
                    out_ref[start : start + tile, :] = block_products(
                        list(zip(w_refs, chunk_refs)), rows, start, tile
                    )

    return local_kernel(
        kernel,
        place,
        [w_far, w_near, pack] + given,
        [f32(width, rows)] * 2,
        cost=matmul_cost(rows, width, 4 * count),
    )


def backward_part(place, chunks, w_half, numbers, rows, before=None):
    width = w_half.shape[1]
    tile = min(width, 256)
    given = [] if before is None else list(before)

    def kernel(tp, section, w_ref, *refs):
        chunk_refs, (out_ref, sum_ref) = refs[: len(chunks)], refs[-2:]
        blocks = [(w_ref.at[k], chunk) for k, chunk in zip(numbers, chunk_refs)]
        for start in range(0, width, tile):
            products = block_products(blocks, rows, start, tile)
            if given:
                products = products + refs[len(chunks)][start : start + tile, :]
            out_ref[start : start + tile, :] = products
        sums = tail_sum(chunk_refs, rows)
        sum_ref[...] = sums + refs[len(chunks) + 1][...] if given else sums

    return local_kernel(
        kernel,
        place,
        [w_half] + chunks + given,
        [f32(width, rows), f32(TAIL, rows)],
        cost=matmul_cost(rows, width, len(chunks)),
    )


def finish_backward(place, chunks, w_half, numbers, before, own, gain_row, a, full_width, last_block=None, finals=()):
    rows, width = a.shape
    chunk_rows = rows + TAIL
    count = len(chunks)
    tile = min(width, 256)
    extra = [] if last_block is None else list(last_block)
    chosen = [[array for array in arrays if array is not None] for arrays in finals]

    def kernel(tp, section, w_ref, *refs):
        chunk_refs = refs[:count]
        before_ref, sum_ref, own_ref, gain_ref, a_ref = refs[count : count + 5]
        rest = list(refs[count + 5 :])
        out_refs = rest[len(extra) + sum(len(arrays) for arrays in chosen) :]
        out_ref = out_refs[0]
        sums = sum_ref[...] + tail_sum(chunk_refs, rows)
        tail = own_ref[rows:chunk_rows, :rows].astype(jnp.float32)

        def pair(lines, number):
            return lines[number : number + 1] + lines[number + 1 : number + 2]

        if extra:
            cot_ref, gained_ref, cot_products, gained_products = rest[:4]
            last_rms = lax.rsqrt(pair(sums, 0) / full_width + EPSILON)
            last_scale = last_rms * last_rms * last_rms / full_width * pair(sums, 2)
            dots = pair(sums, 4) + last_rms * pair(sums, 6) - last_scale * pair(sums, 8)
            rms = as_column(pair(tail, 10))
            rms_column, scale_column = as_column(last_rms), as_column(last_scale)
            out_refs[1][...] = (
                cot_ref[...].astype(jnp.float32)
                + rms_column * gained_ref[:rows, :].astype(jnp.float32)
                - scale_column * own_ref[:rows, :].astype(jnp.float32)
            ).astype(jnp.bfloat16)
            up_ref = out_refs[1]
        else:
            dots = sums[:1]
            rms = as_column(pair(tail, 1))
            up_ref = own_ref
        scale = rms * rms * rms / full_width * as_column(dots)
        blocks = [(w_ref.at[k], chunk) for k, chunk in zip(numbers, chunk_refs)]
        for start in range(0, width, tile):
            columns = slice(start, start + tile)
            products = block_products(blocks, rows, start, tile) + before_ref[columns, :]
            if extra:
                products = (
                    cot_products[columns, :]
                    + last_rms * gained_products[columns, :]
                    - last_scale * products
                )
            out_ref[:, columns] = (
                up_ref[:rows, columns].astype(jnp.float32)
                + rms * gain_ref[:, columns] * products.T
                - scale * a_ref[:, columns].astype(jnp.float32)
            ).astype(jnp.bfloat16)
        final_refs = rest[len(extra) :]
        for arrays, final_ref in zip(finals, out_refs[1 + bool(extra) :]):
            for number, array in enumerate(arrays):
                source = out_ref if array is None else final_refs.pop(0)

                @pl.when(section == number)
                def _(source=source, final_ref=final_ref):
                    final_ref[...] = source[...]

    return local_kernel(
        kernel,
        place,
        [w_half, *chunks, *before, own, gain_row, a, *extra]
        + [array for arrays in chosen for array in arrays],
        [bf16(rows, width)] * (1 + bool(extra) + len(finals)),
        cost=matmul_cost(rows, width, count),
    )


def on_device(inputs, cotangent, weights, gains):
    section_count = lax.axis_size("section")
    tp_count = lax.axis_size("tp")
    micro_count, row_count, width = inputs.shape
    rows = micro_count * row_count
    full_width = weights.shape[2]
    last = section_count - 1
    below = last - 1
    place = jnp.stack([lax.axis_index("tp"), lax.axis_index("section")])
    across = tp_count // 2
    near = list(range(across - 1, 0, -1))
    near_codes = [0] + near
    far_codes = [across ^ e for e in near_codes]
    numbers = {code: number for number, code in enumerate(near_codes)}
    inside = [(last, last)]

    def send(value, routes, step=0):
        pairs = [
            (source * tp_count + t, target * tp_count + (t ^ step))
            for source, target in routes
            for t in range(tp_count)
        ]
        return lax.ppermute(value, ("section", "tp"), pairs)

    def across_route(section, riding=False):
        if section == 1 or riding:
            return [(section, section)] + inside
        return [(section, section)]

    def gather(chunk, source, target, near_chunks=None, riding=(), across_riding=False, pack=None):
        route = [(source, target)]
        crossed = send(chunk, across_route(source, across_riding), across)
        found = [send(chunk if pack is None else pack, route)]
        for e in reversed(near):
            near_chunk = near_chunks[e] if near_chunks else chunk
            found.append(send(near_chunk, route + list(riding), e))
        forwarded = [send(crossed, route)]
        forwarded += [send(crossed, route, e) for e in reversed(near)]
        return found, forwarded, crossed

    cot = cotangent.reshape(rows, width)

    block_in = inputs.reshape(rows, width)
    block_ins = []
    passed = []
    other = None
    cot_found = {}
    for section in range(last):
        beside = section ^ 1
        route = [(section, beside)]
        shared = section < 2
        first_pass = section == 0
        if first_pass:
            w_far, *far, other = first_forward_blocks(
                place, block_in, gains, weights[0], far_codes, other=cot, other_from=last
            )
            w_far = in_vmem(w_far)
            cot_found[0] = other
        else:
            far = forward_blocks(
                place, block_in, gains, w_far, other=other if shared else None, other_from=last
            )
        far_route = route + inside if shared else route
        arrived = [send(chunk, far_route, e) for e, chunk in zip(near, far[1:])]
        if first_pass:
            w_near, *own = first_forward_blocks(
                place, block_in, gains, weights[0], near_codes, pack=True
            )
            w_near = in_vmem(w_near)
        else:
            own = forward_blocks(place, block_in, gains, w_near, pack=True)
        if shared:
            for e, chunk in zip(near, arrived):
                cot_found[e if first_pass else across ^ e] = chunk
        far_own = send(far[0], route)
        combined = add_chunks(
            place, arrived + [far_own], other if first_pass else None, last
        )
        pack, _ = lax.optimization_barrier((own[0], far_own))
        crossed = send(combined, across_route(beside), across)
        if first_pass:
            cot_found[across] = other = crossed
        direct = [send(chunk, route, e) for e, chunk in zip(near, own[1:])]
        if section == below:
            gained_pack, combined = lax.optimization_barrier((gained_pack, combined))
            products = early_products(
                place,
                gained_pack,
                [gained_found[code] for code in far_codes + near_codes],
                w_far,
                w_near,
                below,
            )
            crossed, products = lax.optimization_barrier((crossed, products))
        passed.append(
            finish_forward(place, send(pack, route), direct + [crossed], None, full_width)
        )
        block_ins.append(block_in)
        output = passed[-1][0]
        if section == 1:
            order = [0] + list(reversed(near))
            cot_chunks = [cot_found[code] for code in far_codes + near_codes]
            cot_chunks, output = lax.optimization_barrier((cot_chunks, output))
            gained, gained_pack = gained_chunks(place, cot_chunks, w_far, w_near, gains, last)
            found, forwarded, far_chunk = gather(gained, last, below, pack=gained_pack)
            output, found, _ = lax.optimization_barrier((output, found, far_chunk))
            gained_found = dict(zip(order, found))
            gained_pack = gained_found[0]
            gained_found[0] = None
        block_in = send(output, [(beside, section + 1)]) if section % 2 else output
        if section == 1:
            block_in, forwarded, gained_pack = lax.optimization_barrier(
                (block_in, forwarded, gained_pack)
            )
            gained_found.update({across ^ code: chunk for code, chunk in zip(order, forwarded)})
    last_in = block_in
    chunk = statistics_chunk(place, block_in, gained, cot, *passed[below][1:])
    grads = [None] * section_count
    acts = [None] * section_count
    for section in range(below, -1, -1):
        turn = below - section
        beside = section ^ 1
        near_chunks, riding = None, ()
        if turn:
            upstream = send(grad, [(section + 1, beside)]) if section % 2 else grad
            others = [None]
            if turn == 1:
                others += last_far[1:]
            if turn == 2:
                others = [last_combined] + last_own[1:]
            chunk, *rest = gradient_chunks(place, upstream, *passed[section][1:], others, last)
            if turn <= 2:
                near_chunks, riding = dict(zip(near, rest)), inside
        found, forwarded, crossed = gather(
            chunk, beside, section, near_chunks, riding, across_riding=turn == 2
        )
        part = backward_part(
            place, found, w_near, [numbers[e] for e in [0] + list(reversed(near))], rows
        )
        early = [0] + near[: max(1, across // 4)]
        late = [e for e in reversed(near) if e not in early]
        by_code = dict(zip([0] + list(reversed(near)), forwarded))
        part = backward_part(
            place, [by_code[e] for e in early], w_far, [numbers[e] for e in early], rows, part
        )
        if turn == 1:
            last_combined = add_chunks(place, [last_far[0]] + found[1:], only=last)
        if turn == 2:
            last_output, _, _ = finish_forward(
                place, last_own[0], found[1:] + [crossed], last_in, full_width, only=last
            )
            acts[last] = last_output
        finish = [
            place,
            [by_code[e] for e in late],
            w_far,
            [numbers[e] for e in late],
            part,
            found[0],
            gains,
            block_ins[section],
            full_width,
        ]
        if turn == 0:
            grad, last_grad = finish_backward(*finish, [cot, gained_pack, *products])
            acts[:below] = [
                send(passed[number][0], [(number ^ 1, number)]) for number in range(below)
            ]
            grad, last_grad, last_in, acts[:below] = lax.optimization_barrier(
                (grad, last_grad, last_in, acts[:below])
            )
            last_far = forward_blocks(place, last_in, gains, w_far, only=last)
            last_own = forward_blocks(place, last_in, gains, w_near, only=last)
        elif section:
            (grad,) = finish_backward(*finish)
        else:
            grad, own_grad, own_output = finish_backward(*finish, None, [grads, acts])
        if turn == 1:
            grads[last] = send(last_grad, [(below, last)])
            acts[below] = send(passed[below][0], [(last, below)])
            grad, grads[last], acts[below] = lax.optimization_barrier(
                (grad, grads[last], acts[below])
            )
        if section:
            grads[section] = grad
    shape = (1, micro_count, row_count, width)
    return own_output.reshape(shape), own_grad.reshape(shape)


def solution(mesh):
    placed = (
        P(None, None, "tp"),
        P(None, None, "tp"),
        P("section", "tp", None),
        P("section", "tp"),
    )
    return jax.shard_map(
        on_device,
        mesh=mesh,
        in_specs=placed,
        out_specs=(P("section", None, None, "tp"), P("section", None, None, "tp")),
        check_vma=False,
    )
```

```python
import jax
import jax.numpy as jnp
from jax import lax
from jax.experimental import pallas as pl
from jax.experimental.pallas import tpu as pltpu
from jax.sharding import PartitionSpec as P

EPSILON = 1e-05
MIB = 1 << 20
TAIL = 16
LANES = 128
SMEM_SPEC = pl.BlockSpec(memory_space=pltpu.SMEM)
VMEM_SPEC = pl.BlockSpec(memory_space=pltpu.VMEM)


def local_kernel(kernel, place, operands, out_shapes, limit=12 * MIB, cost=None, **options):
    def body(place_ref, *refs):
        kernel(place_ref[0], place_ref[1], *refs)

    options.setdefault("in_specs", [SMEM_SPEC] + [VMEM_SPEC] * len(operands))
    call = pl.pallas_call(
        body,
        out_shape=out_shapes,
        out_specs=[VMEM_SPEC] * len(out_shapes),
        compiler_params=pltpu.CompilerParams(vmem_limit_bytes=limit),
        cost_estimate=cost,
        **options,
    )
    return list(call(place, *operands))


def bf16(*shape):
    return jax.ShapeDtypeStruct(shape, jnp.bfloat16)


def f32(*shape):
    return jax.ShapeDtypeStruct(shape, jnp.float32)


def as_line(column):
    return jnp.broadcast_to(column, (column.shape[0], LANES)).T[:1]


def as_column(line):
    return jnp.broadcast_to(line, (LANES, line.shape[1])).T[:, :1]


def row_sum(value):
    return jnp.sum(value, axis=1, keepdims=True).astype(jnp.bfloat16).astype(jnp.float32)


def tail_sum(chunk_refs, rows):
    total = chunk_refs[0][rows : rows + TAIL, :rows].astype(jnp.float32)
    for chunk in chunk_refs[1:]:
        total = total + chunk[rows : rows + TAIL, :rows].astype(jnp.float32)
    return total


def matmul_cost(rows, width, count):
    return pl.CostEstimate(
        flops=2 * rows * width * width * count,
        bytes_accessed=2 * width * width * count,
        transcendentals=0,
    )


def in_hbm(array):
    return pltpu.with_memory_space_constraint(array, pltpu.HBM)


def in_vmem(array):
    return pltpu.with_memory_space_constraint(array, pltpu.VMEM)


def for_tiles(width, tile, body):
    def step(number, carry):
        body(pl.multiple_of(number * tile, tile))
        return carry

    lax.fori_loop(0, width // tile, step, 0)


def partial_chunks(tp, wide, gain_ref, take_block, out_refs, looped=False):
    rows, width = wide.shape
    tile = min(width, 256 if looped else 512)
    scaled = (wide * gain_ref[...]).astype(jnp.bfloat16)
    for number, out_ref in enumerate(out_refs):
        w_ref = take_block(number)

        def work(start, w_ref=w_ref, out_ref=out_ref):
            columns = pl.ds(start, tile)
            partial = jnp.dot(scaled, w_ref[:, columns], preferred_element_type=jnp.float32)
            out_ref[:rows, columns] = partial.astype(jnp.bfloat16)

        if looped:
            for_tiles(width, tile, work)
        else:
            for start in range(0, width, tile):
                work(start)
    line = as_line(jnp.sum(wide * wide, axis=1, keepdims=True))
    row_ids = lax.broadcasted_iota(jnp.int32, (TAIL, rows), 0)
    own_row = jnp.where(row_ids == tp % TAIL, jnp.broadcast_to(line, (TAIL, rows)), 0.0)
    for out_ref in out_refs:
        out_ref[rows : rows + TAIL, :] = jnp.zeros((TAIL, width), jnp.bfloat16)
        out_ref[rows : rows + TAIL, :rows] = own_row.astype(jnp.bfloat16)


def chunk_shapes(rows, width, count, pack):
    shapes = [bf16(rows + TAIL, width)] * count
    if pack:
        shapes[0] = bf16(2 * rows + TAIL, width)
    return shapes


def first_forward_blocks(place, a, gain_row, weights, codes, pack=False, other=None, other_from=None):
    rows, width = a.shape
    count = len(codes)
    others = [] if other is None else [other]

    def kernel(tp, section, a_hbm, gain_ref, w_hbm, *refs):
        w_ref, out_refs = refs[len(others)], refs[len(others) + 1 : len(others) + 1 + count]
        a_ref, a_done, w_done = refs[-3:]
        a_copy = pltpu.make_async_copy(a_hbm, a_ref, a_done)
        a_copy.start()
        copies = []
        for number, code in enumerate(codes):
            columns = pl.ds(pl.multiple_of((tp ^ code) * width, width), width)
            copies.append(
                pltpu.make_async_copy(w_hbm.at[:, columns], w_ref.at[number], w_done.at[number])
            )
            copies[-1].start()
        if others:
            chunk_ref = refs[len(others) + 1 + count]
            chunk_ref[:rows, :] = refs[0][...]
            chunk_ref[rows:, :] = jnp.zeros((TAIL, width), jnp.bfloat16)
        a_copy.wait()

        def take_block(number):
            copies[number].wait()
            return w_ref.at[number]

        partial_chunks(tp, a_ref[...].astype(jnp.float32), gain_ref, take_block, out_refs)
        if pack:
            out_refs[0][rows + TAIL :, :] = a_ref[...]
        if others:

            @pl.when(section >= other_from)
            def _():
                for out_ref in out_refs:
                    out_ref[: rows + TAIL, :] = chunk_ref[...]

    return local_kernel(
        kernel,
        place,
        [in_hbm(a), gain_row, in_hbm(weights)] + others,
        [pltpu.VMEM((count, width, width), jnp.bfloat16)]
        + chunk_shapes(rows, width, count, pack)
        + [bf16(rows + TAIL, width)] * len(others),
        in_specs=[SMEM_SPEC, pl.BlockSpec(memory_space=pltpu.HBM), VMEM_SPEC]
        + [pl.BlockSpec(memory_space=pltpu.HBM)]
        + [VMEM_SPEC] * len(others),
        scratch_shapes=[
            pltpu.VMEM((rows, width), jnp.bfloat16),
            pltpu.SemaphoreType.DMA,
            pltpu.SemaphoreType.DMA((count,)),
        ],
        cost=matmul_cost(rows, width, count),
    )


def forward_blocks(place, a, gain_row, w_half, pack=False, only=None, other=None, other_from=None):
    rows, width = a.shape
    count = w_half.shape[0]
    others = [] if other is None else [other]

    def kernel(tp, section, a_ref, gain_ref, w_ref, *refs):
        out_refs = refs[len(others) :]

        def work():
            wide = a_ref[...].astype(jnp.float32)
            partial_chunks(
                tp, wide, gain_ref, lambda number: w_ref.at[number], out_refs, only is not None
            )
            if pack:
                out_refs[0][rows + TAIL :, :] = a_ref[...]

        if only is not None:
            pl.when(section == only)(work)
        else:
            work()
        if others:

            @pl.when(section >= other_from)
            def _():
                for out_ref in out_refs:
                    out_ref[...] = refs[0][...]

    return local_kernel(
        kernel,
        place,
        [a, gain_row, w_half] + others,
        chunk_shapes(rows, width, count, pack),
        cost=matmul_cost(rows, width, count),
    )


def add_chunks(place, chunks, other=None, other_from=None, only=None):
    def kernel(tp, section, *refs):
        def work():
            total = refs[0][...].astype(jnp.float32)
            for chunk in refs[1 : len(chunks)]:
                total = total + chunk[...].astype(jnp.float32)
            refs[-1][...] = total.astype(refs[-1].dtype)

        if only is not None:
            pl.when(section == only)(work)
        else:
            work()
        if other is not None:

            @pl.when(section >= other_from)
            def _():
                refs[-1][...] = refs[len(chunks)][...]

    operands = chunks + ([] if other is None else [other])
    shape = jax.ShapeDtypeStruct(chunks[0].shape, chunks[0].dtype)
    return local_kernel(kernel, place, operands, [shape])[0]


def finish_forward(place, first, chunks, a, full_width, only=None):
    chunk_rows, width = chunks[0].shape
    rows = chunk_rows - TAIL
    given = [] if a is None else [a]

    def kernel(tp, section, first_ref, *refs):
        chunk_refs, (out_ref, branch_ref, rms_ref) = refs[: len(chunks)], refs[-3:]
        def work():
            source = first_ref[chunk_rows:, :] if a is None else refs[len(chunks)][...]
            branch = first_ref[:rows, :].astype(jnp.float32)
            for chunk in chunk_refs:
                branch = branch + chunk[:rows, :].astype(jnp.float32)
            squares = jnp.sum(tail_sum((first_ref,) + chunk_refs, rows), axis=0, keepdims=True)
            inv_rms = lax.rsqrt(as_column(squares) / full_width + EPSILON)
            out_ref[...] = (source.astype(jnp.float32) + inv_rms * branch).astype(jnp.bfloat16)
            branch_ref[...] = branch
            rms_ref[...] = jnp.broadcast_to(inv_rms, (rows, LANES))

        if only is not None:
            pl.when(section == only)(work)
        else:
            work()

    return local_kernel(
        kernel,
        place,
        [first] + chunks + given,
        [bf16(rows, width), f32(rows, width), f32(rows, LANES)],
    )


def two_parts(line):
    high = line.astype(jnp.bfloat16).astype(jnp.float32)
    return [high, line - high]


def store_tail(out_ref, rows, lines):
    row_ids = lax.broadcasted_iota(jnp.int32, (TAIL, rows), 0)
    tile = jnp.zeros((TAIL, rows), jnp.float32)
    for number, line in enumerate(lines):
        tile = jnp.where(row_ids == number, line, tile)
    out_ref[rows:, :] = jnp.zeros((TAIL, out_ref.shape[1]), out_ref.dtype)
    out_ref[rows:, :rows] = tile.astype(out_ref.dtype)


def row_line(value):
    return as_line(jnp.sum(value, axis=1, keepdims=True))


def gradient_chunks(place, upstream, branch, inv_rms, others, other_at):
    rows, width = upstream.shape
    replaced = [other for other in others if other is not None]

    def kernel(tp, section, up_ref, branch_ref, rms_ref, *refs):
        other_refs, out_refs = list(refs[: len(replaced)]), refs[len(replaced) :]
        dots = row_line(up_ref[...].astype(jnp.float32) * branch_ref[...])
        lines = [dots] + two_parts(rms_ref[...].T[:1])
        for out_ref in out_refs:
            out_ref[:rows, :] = up_ref[...]
            store_tail(out_ref, rows, lines)
        if replaced:

            @pl.when(section == other_at)
            def _():
                for other, out_ref in zip(others, out_refs):
                    if other is not None:
                        out_ref[...] = other_refs.pop(0)[...]

    shapes = [bf16(rows + TAIL, width)] * len(others)
    return local_kernel(kernel, place, [upstream, branch, inv_rms, *replaced], shapes)


def statistics_chunk(place, a, back_chunk, cot, branch, inv_rms):
    rows, width = a.shape

    def kernel(tp, section, a_ref, back_ref, cot_ref, branch_ref, rms_ref, out_ref):
        wide = a_ref[...].astype(jnp.float32)
        back = back_ref[:rows, :].astype(jnp.float32)
        cot_wide = cot_ref[...].astype(jnp.float32)
        lines = []
        for product in (
            wide * wide,
            wide * back,
            cot_wide * branch_ref[...],
            back * branch_ref[...],
            wide * branch_ref[...],
        ):
            lines += two_parts(row_line(product))
        out_ref[:rows, :] = a_ref[...]
        store_tail(out_ref, rows, lines + two_parts(rms_ref[...].T[:1]))

    return local_kernel(
        kernel, place, [a, back_chunk, cot, branch, inv_rms], [bf16(rows + TAIL, width)]
    )[0]


def block_products(blocks, rows, start, tile):
    total = None
    for w_ref, chunk in blocks:
        product = lax.dot_general(
            w_ref[pl.ds(start, tile), :],
            chunk[:rows, :],
            (((1,), (1,)), ((), ())),
            preferred_element_type=jnp.float32,
        )
        total = product if total is None else total + product
    return total


def gained_chunks(place, chunks, w_far, w_near, gain_row, only):
    count, width, _ = w_far.shape
    chunk_rows = chunks[0].shape[0]
    rows = chunk_rows - TAIL
    tile = min(width, 256)

    def kernel(tp, section, far_ref, near_ref, gain_ref, *refs):
        w_refs = [far_ref.at[k] for k in range(count)] + [near_ref.at[k] for k in range(count)]
        chunk_refs, (out_ref, pack_ref) = refs[:-2], refs[-2:]

        @pl.when(section == only)
        def _():
            def work(start):
                columns = pl.ds(start, tile)
                products = block_products(list(zip(w_refs, chunk_refs)), rows, start, tile)
                back = gain_ref[:, columns] * products.T
                out_ref[:rows, columns] = back.astype(jnp.bfloat16)

            for_tiles(width, tile, work)
            out_ref[rows:, :] = jnp.zeros((TAIL, width), jnp.bfloat16)
            for number, chunk in enumerate([out_ref] + list(chunk_refs)):
                pack_ref[number * chunk_rows : (number + 1) * chunk_rows, :] = chunk[...]

    return local_kernel(
        kernel,
        place,
        [w_far, w_near, gain_row] + chunks,
        [bf16(chunk_rows, width), bf16((1 + len(chunks)) * chunk_rows, width)],
        cost=matmul_cost(rows, width, 2 * count),
    )


def early_products(place, pack, gained, w_far, w_near, only):
    count, width, _ = w_far.shape
    given = [chunk for chunk in gained if chunk is not None]
    chunk_rows = given[0].shape[0]
    rows = chunk_rows - TAIL
    tile = min(width, 256)

    def kernel(tp, section, far_ref, near_ref, pack_ref, *refs):
        w_refs = [far_ref.at[k] for k in range(count)] + [near_ref.at[k] for k in range(count)]
        packed = [pack_ref.at[pl.ds(k * chunk_rows, chunk_rows), :] for k in range(1 + 2 * count)]
        gained_refs = list(refs[:-2])
        gained_refs = [packed[0] if chunk is None else gained_refs.pop(0) for chunk in gained]

        @pl.when(section == only)
        def _():
            def work(start):
                for chunk_refs, out_ref in zip((packed[1:], gained_refs), refs[-2:]):
                    out_ref[pl.ds(start, tile), :] = block_products(
                        list(zip(w_refs, chunk_refs)), rows, start, tile
                    )

            for_tiles(width, tile, work)

    return local_kernel(
        kernel,
        place,
        [w_far, w_near, pack] + given,
        [f32(width, rows)] * 2,
        cost=matmul_cost(rows, width, 4 * count),
    )


def backward_part(place, chunks, w_half, numbers, rows, before=None):
    width = w_half.shape[1]
    tile = min(width, 256)
    given = [] if before is None else list(before)

    def kernel(tp, section, w_ref, *refs):
        chunk_refs, (out_ref, sum_ref) = refs[: len(chunks)], refs[-2:]
        blocks = [(w_ref.at[k], chunk) for k, chunk in zip(numbers, chunk_refs)]

        def work(start):
            products = block_products(blocks, rows, start, tile)
            if given:
                products = products + refs[len(chunks)][pl.ds(start, tile), :]
            out_ref[pl.ds(start, tile), :] = products

        if given:
            for start in range(0, width, tile):
                work(start)
        else:
            for_tiles(width, tile, work)
        sums = tail_sum(chunk_refs, rows)
        sum_ref[...] = sums + refs[len(chunks) + 1][...] if given else sums

    return local_kernel(
        kernel,
        place,
        [w_half] + chunks + given,
        [f32(width, rows), f32(TAIL, rows)],
        cost=matmul_cost(rows, width, len(chunks)),
    )


def finish_backward(place, chunks, w_half, numbers, before, own, gain_row, a, full_width, last_block=None, finals=()):
    rows, width = a.shape
    chunk_rows = rows + TAIL
    count = len(chunks)
    tile = min(width, 256)
    extra = [] if last_block is None else list(last_block)
    chosen = [[array for array in arrays if array is not None] for arrays in finals]

    def kernel(tp, section, w_ref, *refs):
        chunk_refs = refs[:count]
        before_ref, sum_ref, own_ref, gain_ref, a_ref = refs[count : count + 5]
        rest = list(refs[count + 5 :])
        out_refs = rest[len(extra) + sum(len(arrays) for arrays in chosen) :]
        out_ref = out_refs[0]
        sums = sum_ref[...] + tail_sum(chunk_refs, rows)
        tail = own_ref[rows:chunk_rows, :rows].astype(jnp.float32)

        def pair(lines, number):
            return lines[number : number + 1] + lines[number + 1 : number + 2]

        if extra:
            cot_ref, gained_ref, cot_products, gained_products = rest[:4]
            last_rms = lax.rsqrt(pair(sums, 0) / full_width + EPSILON)
            last_scale = last_rms * last_rms * last_rms / full_width * pair(sums, 2)
            dots = pair(sums, 4) + last_rms * pair(sums, 6) - last_scale * pair(sums, 8)
            rms = as_column(pair(tail, 10))
            rms_column, scale_column = as_column(last_rms), as_column(last_scale)
            out_refs[1][...] = (
                cot_ref[...].astype(jnp.float32)
                + rms_column * gained_ref[:rows, :].astype(jnp.float32)
                - scale_column * own_ref[:rows, :].astype(jnp.float32)
            ).astype(jnp.bfloat16)
            up_ref = out_refs[1]
        else:
            dots = sums[:1]
            rms = as_column(pair(tail, 1))
            up_ref = own_ref
        scale = rms * rms * rms / full_width * as_column(dots)
        blocks = [(w_ref.at[k], chunk) for k, chunk in zip(numbers, chunk_refs)]
        for start in range(0, width, tile):
            columns = slice(start, start + tile)
            products = block_products(blocks, rows, start, tile) + before_ref[columns, :]
            if extra:
                products = (
                    cot_products[columns, :]
                    + last_rms * gained_products[columns, :]
                    - last_scale * products
                )
            out_ref[:, columns] = (
                up_ref[:rows, columns].astype(jnp.float32)
                + rms * gain_ref[:, columns] * products.T
                - scale * a_ref[:, columns].astype(jnp.float32)
            ).astype(jnp.bfloat16)
        final_refs = rest[len(extra) :]
        for arrays, final_ref in zip(finals, out_refs[1 + bool(extra) :]):
            for number, array in enumerate(arrays):
                source = out_ref if array is None else final_refs.pop(0)

                @pl.when(section == number)
                def _(source=source, final_ref=final_ref):
                    final_ref[...] = source[...]

    return local_kernel(
        kernel,
        place,
        [w_half, *chunks, *before, own, gain_row, a, *extra]
        + [array for arrays in chosen for array in arrays],
        [bf16(rows, width)] * (1 + bool(extra) + len(finals)),
        cost=matmul_cost(rows, width, count),
    )


def on_device(inputs, cotangent, weights, gains):
    section_count = lax.axis_size("section")
    tp_count = lax.axis_size("tp")
    micro_count, row_count, width = inputs.shape
    rows = micro_count * row_count
    full_width = weights.shape[2]
    last = section_count - 1
    below = last - 1
    place = jnp.stack([lax.axis_index("tp"), lax.axis_index("section")])
    across = tp_count // 2
    near = list(range(1, across))
    near_codes = [0] + near
    far_codes = [across ^ e for e in near_codes]
    numbers = {code: number for number, code in enumerate(near_codes)}
    inside = [(last, last)]

    def send(value, routes, step=0):
        pairs = [
            (source * tp_count + t, target * tp_count + (t ^ step))
            for source, target in routes
            for t in range(tp_count)
        ]
        return lax.ppermute(value, ("section", "tp"), pairs)

    def gather(chunk, source, target, near_chunks=None, riding=(), forward_riding=(), pack=None):
        route = [(source, target)]
        crossed = send(chunk, [(source, source)], across)
        found = [send(chunk if pack is None else pack, route)]
        for e in near:
            near_chunk = near_chunks[e] if near_chunks else chunk
            found.append(send(near_chunk, route + list(riding), e))
        forwarded = [send(crossed, route)]
        forwarded += [send(crossed, route + list(forward_riding), e) for e in near]
        return found, forwarded, crossed

    cot = cotangent.reshape(rows, width)

    block_in = inputs.reshape(rows, width)
    block_ins = []
    passed = []
    cot_far = send(cot, inside, across)
    for section in range(last):
        beside = section ^ 1
        route = [(section, beside)]
        first_pass = section == 0
        if first_pass:
            w_far, *far, cot_chunk = first_forward_blocks(
                place, block_in, gains, weights[0], far_codes, other=cot, other_from=last
            )
            w_far = in_vmem(w_far)
        else:
            far = forward_blocks(place, block_in, gains, w_far)
        near_route = route + inside if first_pass else route
        arrived = [send(chunk, near_route, e) for e, chunk in zip(near, far[1:])]
        if first_pass:
            w_near, *own, cot_far = first_forward_blocks(
                place, block_in, gains, weights[0], near_codes, pack=True, other=cot_far, other_from=last
            )
            w_near = in_vmem(w_near)
        else:
            own = forward_blocks(place, block_in, gains, w_near, pack=True)
        far_own = send(far[0], route)
        combined = add_chunks(place, arrived + [far_own])
        pack, _ = lax.optimization_barrier((own[0], far_own))
        crossed = send(combined, [(beside, beside)], across)
        if section == below:
            own[1], _ = lax.optimization_barrier((own[1], arrived[0]))
        direct = [send(chunk, near_route, e) for e, chunk in zip(near, own[1:])]
        if first_pass:
            cot_chunks = [cot_far] + direct + [cot_chunk] + arrived
        if section == below:
            gained_pack, combined = lax.optimization_barrier((gained_pack, combined))
            products = early_products(
                place,
                gained_pack,
                [gained_found[code] for code in far_codes + near_codes],
                w_far,
                w_near,
                below,
            )
            crossed, products = lax.optimization_barrier((crossed, products))
        passed.append(
            finish_forward(place, send(pack, route), direct + [crossed], None, full_width)
        )
        block_ins.append(block_in)
        output = passed[-1][0]
        if section == 1:
            order = near_codes
            cot_chunks, output = lax.optimization_barrier((cot_chunks, output))
            gained, gained_pack = gained_chunks(place, cot_chunks, w_far, w_near, gains, last)
            found, forwarded, far_chunk = gather(gained, last, below, pack=gained_pack)
            output, found, _ = lax.optimization_barrier((output, found, far_chunk))
            gained_found = dict(zip(order, found))
            gained_pack = gained_found[0]
            gained_found[0] = None
        block_in = send(output, [(beside, section + 1)]) if section % 2 else output
        if section == 1:
            block_in, forwarded, gained_pack = lax.optimization_barrier(
                (block_in, forwarded, gained_pack)
            )
            gained_found.update({across ^ code: chunk for code, chunk in zip(order, forwarded)})
    last_in = block_in
    chunk = statistics_chunk(place, block_in, gained, cot, *passed[below][1:])
    grads = [None] * section_count
    acts = [None] * section_count
    for section in range(below, -1, -1):
        turn = below - section
        beside = section ^ 1
        near_chunks, riding = None, ()
        if turn:
            upstream = send(grad, [(section + 1, beside)]) if section % 2 else grad
            others = [None]
            if turn == 1:
                others += last_far[1:]
            if turn == 2:
                others += last_own[1:]
            chunk, *rest = gradient_chunks(place, upstream, *passed[section][1:], others, last)
            if turn <= 2:
                near_chunks, riding = dict(zip(near, rest)), inside
        found, forwarded, _ = gather(
            chunk, beside, section, near_chunks, riding, inside if turn == 1 else ()
        )
        part = backward_part(
            place, found, w_near, [numbers[e] for e in [0] + near], rows
        )
        early = [0] + near[-max(1, across // 4) :]
        late = [e for e in near if e not in early]
        by_code = dict(zip([0] + near, forwarded))
        part = backward_part(
            place, [by_code[e] for e in early], w_far, [numbers[e] for e in early], rows, part
        )
        if turn == 1:
            last_combined = add_chunks(place, [last_far[0]] + found[1:], only=last)
            last_crossed = send(last_combined, inside, across)
        if turn == 2:
            last_output, _, _ = finish_forward(
                place, last_own[0], found[1:] + [last_crossed], last_in, full_width, only=last
            )
            acts[last] = last_output
        finish = [
            place,
            [by_code[e] for e in late],
            w_far,
            [numbers[e] for e in late],
            part,
            found[0],
            gains,
            block_ins[section],
            full_width,
        ]
        if turn == 0:
            grad, last_grad = finish_backward(*finish, [cot, gained_pack, *products])
            acts[:below] = [
                send(passed[number][0], [(number ^ 1, number)]) for number in range(below)
            ]
            grad, last_grad, last_in, acts[:below] = lax.optimization_barrier(
                (grad, last_grad, last_in, acts[:below])
            )
            last_far = forward_blocks(place, last_in, gains, w_far, only=last)
            last_own = forward_blocks(place, last_in, gains, w_near, only=last)
        elif section:
            (grad,) = finish_backward(*finish)
        else:
            grad, own_grad, own_output = finish_backward(*finish, None, [grads, acts])
        if turn == 1:
            grads[last] = send(last_grad, [(below, last)])
            acts[below] = send(passed[below][0], [(last, below)])
            grad, grads[last], acts[below] = lax.optimization_barrier(
                (grad, grads[last], acts[below])
            )
        if section:
            grads[section] = grad
    shape = (1, micro_count, row_count, width)
    return own_output.reshape(shape), own_grad.reshape(shape)


def solution(mesh):
    placed = (
        P(None, None, "tp"),
        P(None, None, "tp"),
        P("section", "tp", None),
        P("section", "tp"),
    )
    return jax.shard_map(
        on_device,
        mesh=mesh,
        in_specs=placed,
        out_specs=(P("section", None, None, "tp"), P("section", None, None, "tp")),
        check_vma=False,
    )
```

```python
import jax
import jax.numpy as jnp
from jax import lax
from jax.experimental import pallas as pl
from jax.experimental.pallas import tpu as pltpu
from jax.sharding import PartitionSpec as P

EPSILON = 1e-05
MIB = 1 << 20
TAIL = 16
LANES = 128
SMEM_SPEC = pl.BlockSpec(memory_space=pltpu.SMEM)
VMEM_SPEC = pl.BlockSpec(memory_space=pltpu.VMEM)


def local_kernel(kernel, place, operands, out_shapes, limit=12 * MIB, cost=None, **options):
    def body(place_ref, *refs):
        kernel(place_ref[0], place_ref[1], *refs)

    options.setdefault("in_specs", [SMEM_SPEC] + [VMEM_SPEC] * len(operands))
    call = pl.pallas_call(
        body,
        out_shape=out_shapes,
        out_specs=[VMEM_SPEC] * len(out_shapes),
        compiler_params=pltpu.CompilerParams(vmem_limit_bytes=limit),
        cost_estimate=cost,
        **options,
    )
    return list(call(place, *operands))


def bf16(*shape):
    return jax.ShapeDtypeStruct(shape, jnp.bfloat16)


def f32(*shape):
    return jax.ShapeDtypeStruct(shape, jnp.float32)


def as_line(column):
    return jnp.broadcast_to(column, (column.shape[0], LANES)).T[:1]


def as_column(line):
    return jnp.broadcast_to(line, (LANES, line.shape[1])).T[:, :1]


def row_sum(value):
    return jnp.sum(value, axis=1, keepdims=True).astype(jnp.bfloat16).astype(jnp.float32)


def tail_sum(chunk_refs, rows):
    total = chunk_refs[0][rows : rows + TAIL, :rows].astype(jnp.float32)
    for chunk in chunk_refs[1:]:
        total = total + chunk[rows : rows + TAIL, :rows].astype(jnp.float32)
    return total


def matmul_cost(rows, width, count):
    return pl.CostEstimate(
        flops=2 * rows * width * width * count,
        bytes_accessed=2 * width * width * count,
        transcendentals=0,
    )


def in_hbm(array):
    return pltpu.with_memory_space_constraint(array, pltpu.HBM)


def in_vmem(array):
    return pltpu.with_memory_space_constraint(array, pltpu.VMEM)


def for_tiles(width, tile, body):
    def step(number, carry):
        body(pl.multiple_of(number * tile, tile))
        return carry

    lax.fori_loop(0, width // tile, step, 0)


def partial_chunks(tp, wide, gain_ref, take_block, out_refs, looped=False):
    rows, width = wide.shape
    tile = min(width, 256 if looped else 512)
    scaled = (wide * gain_ref[...]).astype(jnp.bfloat16)
    for number, out_ref in enumerate(out_refs):
        w_ref = take_block(number)

        def work(start, w_ref=w_ref, out_ref=out_ref):
            columns = pl.ds(start, tile)
            partial = jnp.dot(scaled, w_ref[:, columns], preferred_element_type=jnp.float32)
            out_ref[:rows, columns] = partial.astype(jnp.bfloat16)

        if looped:
            for_tiles(width, tile, work)
        else:
            for start in range(0, width, tile):
                work(start)
    line = as_line(jnp.sum(wide * wide, axis=1, keepdims=True))
    row_ids = lax.broadcasted_iota(jnp.int32, (TAIL, rows), 0)
    own_row = jnp.where(row_ids == tp % TAIL, jnp.broadcast_to(line, (TAIL, rows)), 0.0)
    for out_ref in out_refs:
        out_ref[rows : rows + TAIL, :] = jnp.zeros((TAIL, width), jnp.bfloat16)
        out_ref[rows : rows + TAIL, :rows] = own_row.astype(jnp.bfloat16)


def chunk_shapes(rows, width, count, pack):
    shapes = [bf16(rows + TAIL, width)] * count
    if pack:
        shapes[0] = bf16(2 * rows + TAIL, width)
    return shapes


def first_forward_blocks(place, a, gain_row, weights, codes, pack=False, other=None, other_from=None):
    rows, width = a.shape
    count = len(codes)
    others = [] if other is None else [other]

    def kernel(tp, section, a_hbm, gain_ref, w_hbm, *refs):
        w_ref, out_refs = refs[len(others)], refs[len(others) + 1 : len(others) + 1 + count]
        a_ref, a_done, w_done = refs[-3:]
        a_copy = pltpu.make_async_copy(a_hbm, a_ref, a_done)
        a_copy.start()
        copies = []
        for number, code in enumerate(codes):
            columns = pl.ds(pl.multiple_of((tp ^ code) * width, width), width)
            copies.append(
                pltpu.make_async_copy(w_hbm.at[:, columns], w_ref.at[number], w_done.at[number])
            )
            copies[-1].start()
        if others:
            chunk_ref = refs[len(others) + 1 + count]
            chunk_ref[:rows, :] = refs[0][...]
            chunk_ref[rows:, :] = jnp.zeros((TAIL, width), jnp.bfloat16)
        a_copy.wait()

        def take_block(number):
            copies[number].wait()
            return w_ref.at[number]

        partial_chunks(tp, a_ref[...].astype(jnp.float32), gain_ref, take_block, out_refs)
        if pack:
            out_refs[0][rows + TAIL :, :] = a_ref[...]
        if others:

            @pl.when(section >= other_from)
            def _():
                for out_ref in out_refs:
                    out_ref[: rows + TAIL, :] = chunk_ref[...]

    return local_kernel(
        kernel,
        place,
        [in_hbm(a), gain_row, in_hbm(weights)] + others,
        [pltpu.VMEM((count, width, width), jnp.bfloat16)]
        + chunk_shapes(rows, width, count, pack)
        + [bf16(rows + TAIL, width)] * len(others),
        in_specs=[SMEM_SPEC, pl.BlockSpec(memory_space=pltpu.HBM), VMEM_SPEC]
        + [pl.BlockSpec(memory_space=pltpu.HBM)]
        + [VMEM_SPEC] * len(others),
        scratch_shapes=[
            pltpu.VMEM((rows, width), jnp.bfloat16),
            pltpu.SemaphoreType.DMA,
            pltpu.SemaphoreType.DMA((count,)),
        ],
        cost=matmul_cost(rows, width, count),
    )


def forward_blocks(place, a, gain_row, w_half, pack=False, only=None, looped=False):
    rows, width = a.shape
    count = w_half.shape[0]

    def kernel(tp, section, a_ref, gain_ref, w_ref, *out_refs):
        def work():
            wide = a_ref[...].astype(jnp.float32)
            partial_chunks(
                tp, wide, gain_ref, lambda number: w_ref.at[number], out_refs, looped
            )
            if pack:
                out_refs[0][rows + TAIL :, :] = a_ref[...]

        if only is not None:
            pl.when(section == only)(work)
        else:
            work()

    return local_kernel(
        kernel,
        place,
        [a, gain_row, w_half],
        chunk_shapes(rows, width, count, pack),
        cost=matmul_cost(rows, width, count),
    )


def add_chunks(place, chunks, only=None):
    def kernel(tp, section, *refs):
        def work():
            total = refs[0][...].astype(jnp.float32)
            for chunk in refs[1:-1]:
                total = total + chunk[...].astype(jnp.float32)
            refs[-1][...] = total.astype(refs[-1].dtype)

        if only is not None:
            pl.when(section == only)(work)
        else:
            work()

    return local_kernel(kernel, place, chunks, [bf16(*chunks[0].shape)])[0]


def finish_forward(place, first, chunks, a, full_width, only=None):
    chunk_rows, width = chunks[0].shape
    rows = chunk_rows - TAIL
    given = [] if a is None else [a]

    def kernel(tp, section, first_ref, *refs):
        chunk_refs, (out_ref, branch_ref, rms_ref) = refs[: len(chunks)], refs[-3:]
        def work():
            source = first_ref[chunk_rows:, :] if a is None else refs[len(chunks)][...]
            branch = first_ref[:rows, :].astype(jnp.float32)
            for chunk in chunk_refs:
                branch = branch + chunk[:rows, :].astype(jnp.float32)
            squares = jnp.sum(tail_sum((first_ref,) + chunk_refs, rows), axis=0, keepdims=True)
            inv_rms = lax.rsqrt(as_column(squares) / full_width + EPSILON)
            out_ref[...] = (source.astype(jnp.float32) + inv_rms * branch).astype(jnp.bfloat16)
            branch_ref[...] = branch
            rms_ref[...] = jnp.broadcast_to(inv_rms, (rows, LANES))

        if only is not None:
            pl.when(section == only)(work)
        else:
            work()

    return local_kernel(
        kernel,
        place,
        [first] + chunks + given,
        [bf16(rows, width), f32(rows, width), f32(rows, LANES)],
    )


def two_parts(line):
    high = line.astype(jnp.bfloat16).astype(jnp.float32)
    return [high, line - high]


def store_tail(out_ref, rows, lines):
    row_ids = lax.broadcasted_iota(jnp.int32, (TAIL, rows), 0)
    tile = jnp.zeros((TAIL, rows), jnp.float32)
    for number, line in enumerate(lines):
        tile = jnp.where(row_ids == number, line, tile)
    out_ref[rows:, :] = jnp.zeros((TAIL, out_ref.shape[1]), out_ref.dtype)
    out_ref[rows:, :rows] = tile.astype(out_ref.dtype)


def row_line(value):
    return as_line(jnp.sum(value, axis=1, keepdims=True))


def gradient_chunks(place, upstream, branch, inv_rms, others, other_at):
    rows, width = upstream.shape
    replaced = [other for other in others if other is not None]

    def kernel(tp, section, up_ref, branch_ref, rms_ref, *refs):
        other_refs, out_refs = list(refs[: len(replaced)]), refs[len(replaced) :]
        dots = row_line(up_ref[...].astype(jnp.float32) * branch_ref[...])
        lines = [dots] + two_parts(rms_ref[...].T[:1])
        for out_ref in out_refs:
            out_ref[:rows, :] = up_ref[...]
            store_tail(out_ref, rows, lines)
        if replaced:

            @pl.when(section == other_at)
            def _():
                for other, out_ref in zip(others, out_refs):
                    if other is not None:
                        out_ref[...] = other_refs.pop(0)[...]

    shapes = [bf16(rows + TAIL, width)] * len(others)
    return local_kernel(kernel, place, [upstream, branch, inv_rms, *replaced], shapes)


def statistics_chunk(place, a, back_chunk, cot, branch, inv_rms):
    rows, width = a.shape

    def kernel(tp, section, a_ref, back_ref, cot_ref, branch_ref, rms_ref, out_ref):
        wide = a_ref[...].astype(jnp.float32)
        back = back_ref[:rows, :].astype(jnp.float32)
        cot_wide = cot_ref[...].astype(jnp.float32)
        lines = []
        for product in (
            wide * wide,
            wide * back,
            cot_wide * branch_ref[...],
            back * branch_ref[...],
            wide * branch_ref[...],
        ):
            lines += two_parts(row_line(product))
        out_ref[:rows, :] = a_ref[...]
        store_tail(out_ref, rows, lines + two_parts(rms_ref[...].T[:1]))

    return local_kernel(
        kernel, place, [a, back_chunk, cot, branch, inv_rms], [bf16(rows + TAIL, width)]
    )[0]


def block_products(blocks, rows, start, tile):
    total = None
    for w_ref, chunk in blocks:
        product = lax.dot_general(
            w_ref[pl.ds(start, tile), :],
            chunk[:rows, :],
            (((1,), (1,)), ((), ())),
            preferred_element_type=jnp.float32,
        )
        total = product if total is None else total + product
    return total


def gained_chunks(place, chunks, w_far, w_near, gain_row, only):
    count, width, _ = w_far.shape
    chunk_rows = chunks[0].shape[0]
    rows = chunk_rows - TAIL
    tile = min(width, 256)

    def kernel(tp, section, far_ref, near_ref, gain_ref, *refs):
        w_refs = [far_ref.at[k] for k in range(count)] + [near_ref.at[k] for k in range(count)]
        chunk_refs, (out_ref, pack_ref) = refs[:-2], refs[-2:]

        @pl.when(section == only)
        def _():
            def work(start):
                columns = pl.ds(start, tile)
                products = block_products(list(zip(w_refs, chunk_refs)), rows, start, tile)
                back = gain_ref[:, columns] * products.T
                out_ref[:rows, columns] = back.astype(jnp.bfloat16)

            for_tiles(width, tile, work)
            out_ref[rows:, :] = jnp.zeros((TAIL, width), jnp.bfloat16)
            for number, chunk in enumerate([out_ref] + list(chunk_refs)):
                pack_ref[number * chunk_rows : (number + 1) * chunk_rows, :] = chunk[...]

    return local_kernel(
        kernel,
        place,
        [w_far, w_near, gain_row] + chunks,
        [bf16(chunk_rows, width), bf16((1 + len(chunks)) * chunk_rows, width)],
        cost=matmul_cost(rows, width, 2 * count),
    )


def early_products(place, chunks, pack, w_far, w_near, only):
    count, width, _ = w_far.shape
    given = [chunk for chunk in chunks if not isinstance(chunk, int)]
    rows = pack.shape[0] // (1 + 2 * count) - TAIL
    chunk_rows = rows + TAIL
    tile = min(width, 256)

    def kernel(tp, section, far_ref, near_ref, pack_ref, *refs):
        w_refs = [far_ref.at[k] for k in range(count)] + [near_ref.at[k] for k in range(count)]
        given_refs = list(refs[:-1])
        chunk_refs = [
            pack_ref.at[pl.ds(chunk * chunk_rows, chunk_rows), :]
            if isinstance(chunk, int)
            else given_refs.pop(0)
            for chunk in chunks
        ]

        @pl.when(section == only)
        def _():
            def work(start):
                refs[-1][pl.ds(start, tile), :] = block_products(
                    list(zip(w_refs, chunk_refs)), rows, start, tile
                )

            for_tiles(width, tile, work)

    return local_kernel(
        kernel,
        place,
        [w_far, w_near, pack] + given,
        [f32(width, rows)],
        cost=matmul_cost(rows, width, 2 * count),
    )[0]


def backward_part(place, chunks, w_half, numbers, rows, before=None):
    width = w_half.shape[1]
    tile = min(width, 256 if before else 512)
    given = [] if before is None else list(before)

    def kernel(tp, section, w_ref, *refs):
        chunk_refs, (out_ref, sum_ref) = refs[: len(chunks)], refs[-2:]
        blocks = [(w_ref.at[k], chunk) for k, chunk in zip(numbers, chunk_refs)]

        def work(start):
            products = block_products(blocks, rows, start, tile)
            if given:
                products = products + refs[len(chunks)][pl.ds(start, tile), :]
            out_ref[pl.ds(start, tile), :] = products

        if given:
            for start in range(0, width, tile):
                work(start)
        else:
            for_tiles(width, tile, work)
        sums = tail_sum(chunk_refs, rows)
        sum_ref[...] = sums + refs[len(chunks) + 1][...] if given else sums

    return local_kernel(
        kernel,
        place,
        [w_half] + chunks + given,
        [f32(width, rows), f32(TAIL, rows)],
        cost=matmul_cost(rows, width, len(chunks)),
    )


def finish_backward(place, chunks, w_half, numbers, before, own, gain_row, a, full_width, last_block=None, finals=()):
    rows, width = a.shape
    chunk_rows = rows + TAIL
    count = len(chunks)
    tile = min(width, 256)
    extra = [] if last_block is None else list(last_block)
    chosen = [[array for array in arrays if array is not None] for arrays in finals]

    def kernel(tp, section, w_ref, *refs):
        chunk_refs = refs[:count]
        before_ref, sum_ref, own_ref, gain_ref, a_ref = refs[count : count + 5]
        rest = list(refs[count + 5 :])
        out_refs = rest[len(extra) + sum(len(arrays) for arrays in chosen) :]
        out_ref = out_refs[0]
        sums = sum_ref[...] + tail_sum(chunk_refs, rows)
        tail = own_ref[rows:chunk_rows, :rows].astype(jnp.float32)

        def pair(lines, number):
            return lines[number : number + 1] + lines[number + 1 : number + 2]

        if extra:
            cot_ref, gained_ref, cot_ref_products, gained_ref_products = rest[:4]
            last_rms = lax.rsqrt(pair(sums, 0) / full_width + EPSILON)
            last_scale = last_rms * last_rms * last_rms / full_width * pair(sums, 2)
            dots = pair(sums, 4) + last_rms * pair(sums, 6) - last_scale * pair(sums, 8)
            rms = as_column(pair(tail, 10))
            rms_column, scale_column = as_column(last_rms), as_column(last_scale)
            out_refs[1][...] = (
                cot_ref[...].astype(jnp.float32)
                + rms_column * gained_ref[:rows, :].astype(jnp.float32)
                - scale_column * own_ref[:rows, :].astype(jnp.float32)
            ).astype(jnp.bfloat16)
            up_ref = out_refs[1]
        else:
            dots = sums[:1]
            rms = as_column(pair(tail, 1))
            up_ref = own_ref
        scale = rms * rms * rms / full_width * as_column(dots)
        blocks = [(w_ref.at[k], chunk) for k, chunk in zip(numbers, chunk_refs)]
        for start in range(0, width, tile):
            columns = slice(start, start + tile)
            products = block_products(blocks, rows, start, tile) + before_ref[columns, :]
            if extra:
                products = (
                    cot_ref_products[columns, :]
                    + last_rms * gained_ref_products[columns, :]
                    - last_scale * products
                )
            out_ref[:, columns] = (
                up_ref[:rows, columns].astype(jnp.float32)
                + rms * gain_ref[:, columns] * products.T
                - scale * a_ref[:, columns].astype(jnp.float32)
            ).astype(jnp.bfloat16)
        final_refs = rest[len(extra) :]
        for arrays, final_ref in zip(finals, out_refs[1 + bool(extra) :]):
            for number, array in enumerate(arrays):
                source = out_ref if array is None else final_refs.pop(0)

                @pl.when(section == number)
                def _(source=source, final_ref=final_ref):
                    final_ref[...] = source[...]

    return local_kernel(
        kernel,
        place,
        [w_half, *chunks, *before, own, gain_row, a, *extra]
        + [array for arrays in chosen for array in arrays],
        [bf16(rows, width)] * (1 + bool(extra) + len(finals)),
        cost=matmul_cost(rows, width, count),
    )


def on_device(inputs, cotangent, weights, gains):
    section_count = lax.axis_size("section")
    tp_count = lax.axis_size("tp")
    micro_count, row_count, width = inputs.shape
    rows = micro_count * row_count
    full_width = weights.shape[2]
    last = section_count - 1
    below = last - 1
    place = jnp.stack([lax.axis_index("tp"), lax.axis_index("section")])
    across = tp_count // 2
    near = list(range(1, across))
    near_codes = [0] + near
    far_codes = [across ^ e for e in near_codes]
    numbers = {code: number for number, code in enumerate(near_codes)}
    inside = [(last, last)]

    def send(value, routes, step=0):
        pairs = [
            (source * tp_count + t, target * tp_count + (t ^ step))
            for source, target in routes
            for t in range(tp_count)
        ]
        return lax.ppermute(value, ("section", "tp"), pairs)

    def gather(chunk, source, target, near_chunks=None, riding=(), forward_riding=(), pack=None):
        route = [(source, target)]
        crossed = send(chunk, [(source, source)], across)
        found = [send(chunk if pack is None else pack, route)]
        for e in near:
            near_chunk = near_chunks[e] if near_chunks else chunk
            found.append(send(near_chunk, route + list(riding), e))
        far_chunk, _ = lax.optimization_barrier((crossed, found[0]))
        forwarded = [send(far_chunk, route)]
        forwarded += [send(crossed, route + list(forward_riding), e) for e in near]
        return found, forwarded, crossed

    cot = cotangent.reshape(rows, width)

    block_in = inputs.reshape(rows, width)
    block_ins = []
    passed = []
    cot_far = send(cot, inside, across)
    for section in range(last):
        beside = section ^ 1
        route = [(section, beside)]
        first_pass = section == 0
        if first_pass:
            w_far, *far, cot_chunk = first_forward_blocks(
                place, block_in, gains, weights[0], far_codes, other=cot, other_from=last
            )
            w_far = in_vmem(w_far)
        else:
            far = forward_blocks(place, block_in, gains, w_far, only=section)
        near_route = route + inside if first_pass else route
        arrived = [send(chunk, near_route, e) for e, chunk in zip(near, far[1:])]
        if first_pass:
            w_near, *own, cot_far = first_forward_blocks(
                place, block_in, gains, weights[0], near_codes, pack=True, other=cot_far, other_from=last
            )
            w_near = in_vmem(w_near)
        else:
            own = forward_blocks(place, block_in, gains, w_near, pack=True, only=section)
        far_own = send(far[0], route)
        combined = add_chunks(place, arrived + [far_own])
        pack, _ = lax.optimization_barrier((own[0], far_own))
        crossed = send(combined, [(beside, beside)], across)
        direct = [send(chunk, near_route, e) for e, chunk in zip(near, own[1:])]
        if first_pass:
            cot_chunks = [cot_far] + direct + [cot_chunk] + arrived
        if section == below:
            gained_pack, combined = lax.optimization_barrier((gained_pack, combined))
            gained_products = early_products(
                place,
                [gained_found[code] for code in far_codes + near_codes],
                gained_pack,
                w_far,
                w_near,
                below,
            )
            crossed, gained_products = lax.optimization_barrier((crossed, gained_products))
        passed.append(
            finish_forward(place, send(pack, route), direct + [crossed], None, full_width)
        )
        block_ins.append(block_in)
        output = passed[-1][0]
        if section == 1:
            order = near_codes
            cot_chunks, output = lax.optimization_barrier((cot_chunks, output))
            gained, gained_pack = gained_chunks(place, cot_chunks, w_far, w_near, gains, last)
            found, forwarded, far_chunk = gather(gained, last, below, pack=gained_pack)
            output, found, _ = lax.optimization_barrier((output, found, far_chunk))
            gained_found = dict(zip(order, found))
            gained_pack = gained_found[0]
            gained_found[0] = 0
            cot_products = early_products(
                place, list(range(1, 1 + tp_count)), gained_pack, w_far, w_near, below
            )
        block_in = send(output, [(beside, section + 1)]) if section % 2 else output
        if section == 1:
            block_in, forwarded, gained_pack, cot_products = lax.optimization_barrier(
                (block_in, forwarded, gained_pack, cot_products)
            )
            gained_found.update({across ^ code: chunk for code, chunk in zip(order, forwarded)})
    last_in = block_in
    chunk = statistics_chunk(place, block_in, gained, cot, *passed[below][1:])
    grads = [None] * section_count
    acts = [None] * section_count
    for section in range(below, -1, -1):
        turn = below - section
        beside = section ^ 1
        near_chunks, riding = None, ()
        if turn:
            upstream = send(grad, [(section + 1, beside)]) if section % 2 else grad
            others = [None]
            if turn == 1:
                others += last_far[1:]
            if turn == 2:
                others += last_own[1:]
            chunk, *rest = gradient_chunks(place, upstream, *passed[section][1:], others, last)
            if turn <= 2:
                near_chunks, riding = dict(zip(near, rest)), inside
        found, forwarded, _ = gather(
            chunk, beside, section, near_chunks, riding, inside if turn == 1 else ()
        )
        part = backward_part(
            place, found, w_near, [numbers[e] for e in [0] + near], rows
        )
        early = [0] + near[-max(1, across // 4) :]
        late = [e for e in near if e not in early]
        by_code = dict(zip([0] + near, forwarded))
        part = backward_part(
            place, [by_code[e] for e in early], w_far, [numbers[e] for e in early], rows, part
        )
        if turn == 1:
            last_combined = add_chunks(place, [last_far[0]] + found[1:], only=last)
            last_crossed = send(last_combined, inside, across)
        if turn == 2:
            last_output, _, _ = finish_forward(
                place, last_own[0], found[1:] + [last_crossed], last_in, full_width, only=last
            )
            acts[last] = last_output
        finish = [
            place,
            [by_code[e] for e in late],
            w_far,
            [numbers[e] for e in late],
            part,
            found[0],
            gains,
            block_ins[section],
            full_width,
        ]
        if turn == 0:
            grad, last_grad = finish_backward(*finish, [cot, gained_pack, cot_products, gained_products])
            acts[:below] = [
                send(passed[number][0], [(number ^ 1, number)]) for number in range(below)
            ]
            grad, last_grad, last_in, acts[:below] = lax.optimization_barrier(
                (grad, last_grad, last_in, acts[:below])
            )
            last_far = forward_blocks(place, last_in, gains, w_far, only=last, looped=True)
            last_own = forward_blocks(place, last_in, gains, w_near, only=last, looped=True)
        elif section:
            (grad,) = finish_backward(*finish)
        else:
            grad, own_grad, own_output = finish_backward(*finish, None, [grads, acts])
        if turn == 1:
            grads[last] = send(last_grad, [(below, last)])
            acts[below] = send(passed[below][0], [(last, below)])
            grad, grads[last], acts[below] = lax.optimization_barrier(
                (grad, grads[last], acts[below])
            )
        if section:
            grads[section] = grad
    shape = (1, micro_count, row_count, width)
    return own_output.reshape(shape), own_grad.reshape(shape)


def solution(mesh):
    placed = (
        P(None, None, "tp"),
        P(None, None, "tp"),
        P("section", "tp", None),
        P("section", "tp"),
    )
    return jax.shard_map(
        on_device,
        mesh=mesh,
        in_specs=placed,
        out_specs=(P("section", None, None, "tp"), P("section", None, None, "tp")),
        check_vma=False,
    )
```

```python
import jax
import jax.numpy as jnp
from jax import lax
from jax.experimental import pallas as pl
from jax.experimental.pallas import tpu as pltpu
from jax.sharding import PartitionSpec as P

EPSILON = 1e-05
MIB = 1 << 20
TAIL = 16
LANES = 128
SMEM_SPEC = pl.BlockSpec(memory_space=pltpu.SMEM)
VMEM_SPEC = pl.BlockSpec(memory_space=pltpu.VMEM)


def local_kernel(kernel, place, operands, out_shapes, limit=12 * MIB, cost=None, **options):
    def body(place_ref, *refs):
        kernel(place_ref[0], place_ref[1], *refs)

    options.setdefault("in_specs", [SMEM_SPEC] + [VMEM_SPEC] * len(operands))
    call = pl.pallas_call(
        body,
        out_shape=out_shapes,
        out_specs=[VMEM_SPEC] * len(out_shapes),
        compiler_params=pltpu.CompilerParams(vmem_limit_bytes=limit),
        cost_estimate=cost,
        **options,
    )
    return list(call(place, *operands))


def bf16(*shape):
    return jax.ShapeDtypeStruct(shape, jnp.bfloat16)


def f32(*shape):
    return jax.ShapeDtypeStruct(shape, jnp.float32)


def as_line(column):
    return jnp.broadcast_to(column, (column.shape[0], LANES)).T[:1]


def as_column(line):
    return jnp.broadcast_to(line, (LANES, line.shape[1])).T[:, :1]


def row_sum(value):
    return jnp.sum(value, axis=1, keepdims=True).astype(jnp.bfloat16).astype(jnp.float32)


def tail_sum(chunk_refs, rows):
    total = chunk_refs[0][rows : rows + TAIL, :rows].astype(jnp.float32)
    for chunk in chunk_refs[1:]:
        total = total + chunk[rows : rows + TAIL, :rows].astype(jnp.float32)
    return total


def matmul_cost(rows, width, count):
    return pl.CostEstimate(
        flops=2 * rows * width * width * count,
        bytes_accessed=2 * width * width * count,
        transcendentals=0,
    )


def in_hbm(array):
    return pltpu.with_memory_space_constraint(array, pltpu.HBM)


def in_vmem(array):
    return pltpu.with_memory_space_constraint(array, pltpu.VMEM)


def for_tiles(width, tile, body):
    def step(number, carry):
        body(pl.multiple_of(number * tile, tile))
        return carry

    lax.fori_loop(0, width // tile, step, 0)


def partial_chunks(tp, wide, gain_ref, take_block, out_refs, looped=False):
    rows, width = wide.shape
    tile = min(width, 256 if looped else 512)
    scaled = (wide * gain_ref[...]).astype(jnp.bfloat16)
    for number, out_ref in enumerate(out_refs):
        w_ref = take_block(number)

        def work(start, w_ref=w_ref, out_ref=out_ref):
            columns = pl.ds(start, tile)
            partial = jnp.dot(scaled, w_ref[:, columns], preferred_element_type=jnp.float32)
            out_ref[:rows, columns] = partial.astype(jnp.bfloat16)

        if looped:
            for_tiles(width, tile, work)
        else:
            for start in range(0, width, tile):
                work(start)
    line = as_line(jnp.sum(wide * wide, axis=1, keepdims=True))
    row_ids = lax.broadcasted_iota(jnp.int32, (TAIL, rows), 0)
    own_row = jnp.where(row_ids == tp % TAIL, jnp.broadcast_to(line, (TAIL, rows)), 0.0)
    for out_ref in out_refs:
        out_ref[rows : rows + TAIL, :] = jnp.zeros((TAIL, width), jnp.bfloat16)
        out_ref[rows : rows + TAIL, :rows] = own_row.astype(jnp.bfloat16)


def chunk_shapes(rows, width, count, pack):
    shapes = [bf16(rows + TAIL, width)] * count
    if pack:
        shapes[0] = bf16(2 * rows + TAIL, width)
    return shapes


def first_forward_blocks(place, a, gain_row, weights, codes, pack=False, other=None, other_from=None):
    rows, width = a.shape
    count = len(codes)
    others = [] if other is None else [other]

    def kernel(tp, section, a_hbm, gain_ref, w_hbm, *refs):
        w_ref, out_refs = refs[len(others)], refs[len(others) + 1 : len(others) + 1 + count]
        a_ref, a_done, w_done = refs[-3:]
        a_copy = pltpu.make_async_copy(a_hbm, a_ref, a_done)
        a_copy.start()
        copies = []
        for number, code in enumerate(codes):
            columns = pl.ds(pl.multiple_of((tp ^ code) * width, width), width)
            copies.append(
                pltpu.make_async_copy(w_hbm.at[:, columns], w_ref.at[number], w_done.at[number])
            )
            copies[-1].start()
        if others:
            chunk_ref = refs[len(others) + 1 + count]
            chunk_ref[:rows, :] = refs[0][...]
            chunk_ref[rows:, :] = jnp.zeros((TAIL, width), jnp.bfloat16)
        a_copy.wait()

        def take_block(number):
            copies[number].wait()
            return w_ref.at[number]

        partial_chunks(tp, a_ref[...].astype(jnp.float32), gain_ref, take_block, out_refs)
        if pack:
            out_refs[0][rows + TAIL :, :] = a_ref[...]
        if others:

            @pl.when(section >= other_from)
            def _():
                for out_ref in out_refs:
                    out_ref[: rows + TAIL, :] = chunk_ref[...]

    return local_kernel(
        kernel,
        place,
        [in_hbm(a), gain_row, in_hbm(weights)] + others,
        [pltpu.VMEM((count, width, width), jnp.bfloat16)]
        + chunk_shapes(rows, width, count, pack)
        + [bf16(rows + TAIL, width)] * len(others),
        in_specs=[SMEM_SPEC, pl.BlockSpec(memory_space=pltpu.HBM), VMEM_SPEC]
        + [pl.BlockSpec(memory_space=pltpu.HBM)]
        + [VMEM_SPEC] * len(others),
        scratch_shapes=[
            pltpu.VMEM((rows, width), jnp.bfloat16),
            pltpu.SemaphoreType.DMA,
            pltpu.SemaphoreType.DMA((count,)),
        ],
        cost=matmul_cost(rows, width, count),
    )


def forward_blocks(place, a, gain_row, w_half, pack=False, only=None, looped=False):
    rows, width = a.shape
    count = w_half.shape[0]

    def kernel(tp, section, a_ref, gain_ref, w_ref, *out_refs):
        def work():
            wide = a_ref[...].astype(jnp.float32)
            partial_chunks(
                tp, wide, gain_ref, lambda number: w_ref.at[number], out_refs, looped
            )
            if pack:
                out_refs[0][rows + TAIL :, :] = a_ref[...]

        if only is not None:
            pl.when(section == only)(work)
        else:
            work()

    return local_kernel(
        kernel,
        place,
        [a, gain_row, w_half],
        chunk_shapes(rows, width, count, pack),
        cost=matmul_cost(rows, width, count),
    )


def add_chunks(place, chunks, only=None):
    def kernel(tp, section, *refs):
        def work():
            total = refs[0][...].astype(jnp.float32)
            for chunk in refs[1:-1]:
                total = total + chunk[...].astype(jnp.float32)
            refs[-1][...] = total.astype(refs[-1].dtype)

        if only is not None:
            pl.when(section == only)(work)
        else:
            work()

    return local_kernel(kernel, place, chunks, [bf16(*chunks[0].shape)])[0]


def finish_forward(place, first, chunks, a, full_width, only=None):
    chunk_rows, width = chunks[0].shape
    rows = chunk_rows - TAIL
    given = [] if a is None else [a]

    def kernel(tp, section, first_ref, *refs):
        chunk_refs, (out_ref, branch_ref, rms_ref) = refs[: len(chunks)], refs[-3:]
        def work():
            source = first_ref[chunk_rows:, :] if a is None else refs[len(chunks)][...]
            branch = first_ref[:rows, :].astype(jnp.float32)
            for chunk in chunk_refs:
                branch = branch + chunk[:rows, :].astype(jnp.float32)
            squares = jnp.sum(tail_sum((first_ref,) + chunk_refs, rows), axis=0, keepdims=True)
            inv_rms = lax.rsqrt(as_column(squares) / full_width + EPSILON)
            out_ref[...] = (source.astype(jnp.float32) + inv_rms * branch).astype(jnp.bfloat16)
            branch_ref[...] = branch
            rms_ref[...] = jnp.broadcast_to(inv_rms, (rows, LANES))

        if only is not None:
            pl.when(section == only)(work)
        else:
            work()

    return local_kernel(
        kernel,
        place,
        [first] + chunks + given,
        [bf16(rows, width), f32(rows, width), f32(rows, LANES)],
    )


def two_parts(line):
    high = line.astype(jnp.bfloat16).astype(jnp.float32)
    return [high, line - high]


def store_tail(out_ref, rows, lines):
    row_ids = lax.broadcasted_iota(jnp.int32, (TAIL, rows), 0)
    tile = jnp.zeros((TAIL, rows), jnp.float32)
    for number, line in enumerate(lines):
        tile = jnp.where(row_ids == number, line, tile)
    out_ref[rows:, :] = jnp.zeros((TAIL, out_ref.shape[1]), out_ref.dtype)
    out_ref[rows:, :rows] = tile.astype(out_ref.dtype)


def row_line(value):
    return as_line(jnp.sum(value, axis=1, keepdims=True))


def gradient_chunks(place, upstream, branch, inv_rms, others, other_at):
    rows, width = upstream.shape
    replaced = [other for other in others if other is not None]

    def kernel(tp, section, up_ref, branch_ref, rms_ref, *refs):
        other_refs, out_refs = list(refs[: len(replaced)]), refs[len(replaced) :]
        dots = row_line(up_ref[...].astype(jnp.float32) * branch_ref[...])
        lines = [dots] + two_parts(rms_ref[...].T[:1])
        for out_ref in out_refs:
            out_ref[:rows, :] = up_ref[...]
            store_tail(out_ref, rows, lines)
        if replaced:

            @pl.when(section == other_at)
            def _():
                for other, out_ref in zip(others, out_refs):
                    if other is not None:
                        out_ref[...] = other_refs.pop(0)[...]

    shapes = [bf16(rows + TAIL, width)] * len(others)
    return local_kernel(kernel, place, [upstream, branch, inv_rms, *replaced], shapes)


def statistics_chunk(place, a, back_chunk, cot, branch, inv_rms):
    rows, width = a.shape

    def kernel(tp, section, a_ref, back_ref, cot_ref, branch_ref, rms_ref, out_ref):
        wide = a_ref[...].astype(jnp.float32)
        back = back_ref[:rows, :].astype(jnp.float32)
        cot_wide = cot_ref[...].astype(jnp.float32)
        lines = []
        for product in (
            wide * wide,
            wide * back,
            cot_wide * branch_ref[...],
            back * branch_ref[...],
            wide * branch_ref[...],
        ):
            lines += two_parts(row_line(product))
        out_ref[:rows, :] = a_ref[...]
        store_tail(out_ref, rows, lines + two_parts(rms_ref[...].T[:1]))

    return local_kernel(
        kernel, place, [a, back_chunk, cot, branch, inv_rms], [bf16(rows + TAIL, width)]
    )[0]


def block_products(blocks, rows, start, tile):
    total = None
    for w_ref, chunk in blocks:
        product = lax.dot_general(
            w_ref[pl.ds(start, tile), :],
            chunk[:rows, :],
            (((1,), (1,)), ((), ())),
            preferred_element_type=jnp.float32,
        )
        total = product if total is None else total + product
    return total


def gained_chunks(place, chunks, w_far, w_near, gain_row, only):
    count, width, _ = w_far.shape
    chunk_rows = chunks[0].shape[0]
    rows = chunk_rows - TAIL
    tile = min(width, 256)

    def kernel(tp, section, far_ref, near_ref, gain_ref, *refs):
        w_refs = [far_ref.at[k] for k in range(count)] + [near_ref.at[k] for k in range(count)]
        chunk_refs, (out_ref, pack_ref) = refs[:-2], refs[-2:]

        @pl.when(section == only)
        def _():
            def work(start):
                columns = pl.ds(start, tile)
                products = block_products(list(zip(w_refs, chunk_refs)), rows, start, tile)
                back = gain_ref[:, columns] * products.T
                out_ref[:rows, columns] = back.astype(jnp.bfloat16)

            for_tiles(width, tile, work)
            out_ref[rows:, :] = jnp.zeros((TAIL, width), jnp.bfloat16)
            for number, chunk in enumerate([out_ref] + list(chunk_refs)):
                pack_ref[number * chunk_rows : (number + 1) * chunk_rows, :] = chunk[...]

    return local_kernel(
        kernel,
        place,
        [w_far, w_near, gain_row] + chunks,
        [bf16(chunk_rows, width), bf16((1 + len(chunks)) * chunk_rows, width)],
        cost=matmul_cost(rows, width, 2 * count),
    )


def early_products(place, pack, gained, w_far, w_near, only):
    count, width, _ = w_far.shape
    given = [chunk for chunk in gained if chunk is not None]
    chunk_rows = given[0].shape[0]
    rows = chunk_rows - TAIL
    tile = min(width, 256)

    def kernel(tp, section, far_ref, near_ref, pack_ref, *refs):
        w_refs = [far_ref.at[k] for k in range(count)] + [near_ref.at[k] for k in range(count)]
        packed = [pack_ref.at[pl.ds(k * chunk_rows, chunk_rows), :] for k in range(1 + 2 * count)]
        gained_refs = list(refs[:-2])
        gained_refs = [packed[0] if chunk is None else gained_refs.pop(0) for chunk in gained]

        @pl.when(section == only)
        def _():
            def work(start):
                for chunk_refs, out_ref in zip((packed[1:], gained_refs), refs[-2:]):
                    out_ref[pl.ds(start, tile), :] = block_products(
                        list(zip(w_refs, chunk_refs)), rows, start, tile
                    )

            for_tiles(width, tile, work)

    return local_kernel(
        kernel,
        place,
        [w_far, w_near, pack] + given,
        [f32(width, rows)] * 2,
        cost=matmul_cost(rows, width, 4 * count),
    )


def backward_part(place, chunks, w_half, numbers, rows, before=None):
    width = w_half.shape[1]
    tile = min(width, 256 if before else 512)
    given = [] if before is None else list(before)

    def kernel(tp, section, w_ref, *refs):
        chunk_refs, (out_ref, sum_ref) = refs[: len(chunks)], refs[-2:]
        blocks = [(w_ref.at[k], chunk) for k, chunk in zip(numbers, chunk_refs)]

        def work(start):
            products = block_products(blocks, rows, start, tile)
            if given:
                products = products + refs[len(chunks)][pl.ds(start, tile), :]
            out_ref[pl.ds(start, tile), :] = products

        if given:
            for start in range(0, width, tile):
                work(start)
        else:
            for_tiles(width, tile, work)
        sums = tail_sum(chunk_refs, rows)
        sum_ref[...] = sums + refs[len(chunks) + 1][...] if given else sums

    return local_kernel(
        kernel,
        place,
        [w_half] + chunks + given,
        [f32(width, rows), f32(TAIL, rows)],
        cost=matmul_cost(rows, width, len(chunks)),
    )


def finish_backward(place, chunks, w_half, numbers, before, own, gain_row, a, full_width, last_block=None, finals=()):
    rows, width = a.shape
    chunk_rows = rows + TAIL
    count = len(chunks)
    tile = min(width, 256)
    extra = [] if last_block is None else list(last_block)
    chosen = [[array for array in arrays if array is not None] for arrays in finals]

    def kernel(tp, section, w_ref, *refs):
        chunk_refs = refs[:count]
        before_ref, sum_ref, own_ref, gain_ref, a_ref = refs[count : count + 5]
        rest = list(refs[count + 5 :])
        out_refs = rest[len(extra) + sum(len(arrays) for arrays in chosen) :]
        out_ref = out_refs[0]
        sums = sum_ref[...] + tail_sum(chunk_refs, rows)
        tail = own_ref[rows:chunk_rows, :rows].astype(jnp.float32)

        def pair(lines, number):
            return lines[number : number + 1] + lines[number + 1 : number + 2]

        if extra:
            cot_ref, gained_ref, cot_ref_products, gained_ref_products = rest[:4]
            last_rms = lax.rsqrt(pair(sums, 0) / full_width + EPSILON)
            last_scale = last_rms * last_rms * last_rms / full_width * pair(sums, 2)
            dots = pair(sums, 4) + last_rms * pair(sums, 6) - last_scale * pair(sums, 8)
            rms = as_column(pair(tail, 10))
            rms_column, scale_column = as_column(last_rms), as_column(last_scale)
            out_refs[1][...] = (
                cot_ref[...].astype(jnp.float32)
                + rms_column * gained_ref[:rows, :].astype(jnp.float32)
                - scale_column * own_ref[:rows, :].astype(jnp.float32)
            ).astype(jnp.bfloat16)
            up_ref = out_refs[1]
        else:
            dots = sums[:1]
            rms = as_column(pair(tail, 1))
            up_ref = own_ref
        scale = rms * rms * rms / full_width * as_column(dots)
        blocks = [(w_ref.at[k], chunk) for k, chunk in zip(numbers, chunk_refs)]
        for start in range(0, width, tile):
            columns = slice(start, start + tile)
            products = block_products(blocks, rows, start, tile) + before_ref[columns, :]
            if extra:
                products = (
                    cot_ref_products[columns, :]
                    + last_rms * gained_ref_products[columns, :]
                    - last_scale * products
                )
            out_ref[:, columns] = (
                up_ref[:rows, columns].astype(jnp.float32)
                + rms * gain_ref[:, columns] * products.T
                - scale * a_ref[:, columns].astype(jnp.float32)
            ).astype(jnp.bfloat16)
        final_refs = rest[len(extra) :]
        for arrays, final_ref in zip(finals, out_refs[1 + bool(extra) :]):
            for number, array in enumerate(arrays):
                source = out_ref if array is None else final_refs.pop(0)

                @pl.when(section == number)
                def _(source=source, final_ref=final_ref):
                    final_ref[...] = source[...]

    return local_kernel(
        kernel,
        place,
        [w_half, *chunks, *before, own, gain_row, a, *extra]
        + [array for arrays in chosen for array in arrays],
        [bf16(rows, width)] * (1 + bool(extra) + len(finals)),
        cost=matmul_cost(rows, width, count),
    )


def on_device(inputs, cotangent, weights, gains):
    section_count = lax.axis_size("section")
    tp_count = lax.axis_size("tp")
    micro_count, row_count, width = inputs.shape
    rows = micro_count * row_count
    full_width = weights.shape[2]
    last = section_count - 1
    below = last - 1
    place = jnp.stack([lax.axis_index("tp"), lax.axis_index("section")])
    across = tp_count // 2
    near = list(range(1, across))
    near_codes = [0] + near
    far_codes = [across ^ e for e in near_codes]
    numbers = {code: number for number, code in enumerate(near_codes)}
    inside = [(last, last)]

    def send(value, routes, step=0):
        pairs = [
            (source * tp_count + t, target * tp_count + (t ^ step))
            for source, target in routes
            for t in range(tp_count)
        ]
        return lax.ppermute(value, ("section", "tp"), pairs)

    def gather(chunk, source, target, near_chunks=None, riding=(), forward_riding=(), pack=None):
        route = [(source, target)]
        crossed = send(chunk, [(source, source)], across)
        found = [send(chunk if pack is None else pack, route)]
        for e in near:
            near_chunk = near_chunks[e] if near_chunks else chunk
            found.append(send(near_chunk, route + list(riding), e))
        far_chunk, _ = lax.optimization_barrier((crossed, found[0]))
        forwarded = [send(far_chunk, route)]
        forwarded += [send(crossed, route + list(forward_riding), e) for e in near]
        return found, forwarded, crossed

    cot = cotangent.reshape(rows, width)

    block_in = inputs.reshape(rows, width)
    block_ins = []
    passed = []
    cot_far = send(cot, inside, across)
    for section in range(last):
        beside = section ^ 1
        route = [(section, beside)]
        first_pass = section == 0
        if first_pass:
            w_far, *far, cot_chunk = first_forward_blocks(
                place, block_in, gains, weights[0], far_codes, other=cot, other_from=last
            )
            w_far = in_vmem(w_far)
        else:
            far = forward_blocks(place, block_in, gains, w_far, only=section)
        near_route = route + inside if first_pass else route
        arrived = [send(chunk, near_route, e) for e, chunk in zip(near, far[1:])]
        if first_pass:
            w_near, *own, cot_far = first_forward_blocks(
                place, block_in, gains, weights[0], near_codes, pack=True, other=cot_far, other_from=last
            )
            w_near = in_vmem(w_near)
        else:
            own = forward_blocks(place, block_in, gains, w_near, pack=True, only=section)
        far_own = send(far[0], route)
        combined = add_chunks(place, arrived + [far_own])
        pack, _ = lax.optimization_barrier((own[0], far_own))
        crossed = send(combined, [(beside, beside)], across)
        direct = [send(chunk, near_route, e) for e, chunk in zip(near, own[1:])]
        if first_pass:
            cot_chunks = [cot_far] + direct + [cot_chunk] + arrived
        if section == below:
            gained_pack, combined = lax.optimization_barrier((gained_pack, combined))
            products = early_products(
                place,
                gained_pack,
                [gained_found[code] for code in far_codes + near_codes],
                w_far,
                w_near,
                below,
            )
            crossed, products = lax.optimization_barrier((crossed, products))
        passed.append(
            finish_forward(place, send(pack, route), direct + [crossed], None, full_width)
        )
        block_ins.append(block_in)
        output = passed[-1][0]
        if section == 1:
            order = near_codes
            cot_chunks, output = lax.optimization_barrier((cot_chunks, output))
            gained, gained_pack = gained_chunks(place, cot_chunks, w_far, w_near, gains, last)
            found, forwarded, far_chunk = gather(gained, last, below, pack=gained_pack)
            output, found, _ = lax.optimization_barrier((output, found, far_chunk))
            gained_found = dict(zip(order, found))
            gained_pack = gained_found[0]
            gained_found[0] = None
        block_in = send(output, [(beside, section + 1)]) if section % 2 else output
        if section == 1:
            block_in, forwarded, gained_pack = lax.optimization_barrier(
                (block_in, forwarded, gained_pack)
            )
            gained_found.update({across ^ code: chunk for code, chunk in zip(order, forwarded)})
    last_in = block_in
    chunk = statistics_chunk(place, block_in, gained, cot, *passed[below][1:])
    grads = [None] * section_count
    acts = [None] * section_count
    for section in range(below, -1, -1):
        turn = below - section
        beside = section ^ 1
        near_chunks, riding = None, ()
        if turn:
            upstream = send(grad, [(section + 1, beside)]) if section % 2 else grad
            others = [None]
            if turn == 1:
                others += last_far[1:]
            if turn == 2:
                others += last_own[1:]
            chunk, *rest = gradient_chunks(place, upstream, *passed[section][1:], others, last)
            if turn <= 2:
                near_chunks, riding = dict(zip(near, rest)), inside
        found, forwarded, _ = gather(
            chunk, beside, section, near_chunks, riding, inside if turn == 1 else ()
        )
        part = backward_part(
            place, found, w_near, [numbers[e] for e in [0] + near], rows
        )
        early = [0] + near[-max(1, across // 4) :]
        late = [e for e in near if e not in early]
        by_code = dict(zip([0] + near, forwarded))
        part = backward_part(
            place, [by_code[e] for e in early], w_far, [numbers[e] for e in early], rows, part
        )
        if turn == 1:
            last_combined = add_chunks(place, [last_far[0]] + found[1:], only=last)
            last_crossed = send(last_combined, inside, across)
        if turn == 2:
            last_output, _, _ = finish_forward(
                place, last_own[0], found[1:] + [last_crossed], last_in, full_width, only=last
            )
            acts[last] = last_output
        finish = [
            place,
            [by_code[e] for e in late],
            w_far,
            [numbers[e] for e in late],
            part,
            found[0],
            gains,
            block_ins[section],
            full_width,
        ]
        if turn == 0:
            grad, last_grad = finish_backward(*finish, [cot, gained_pack, *products])
            acts[:below] = [
                send(passed[number][0], [(number ^ 1, number)]) for number in range(below)
            ]
            grad, last_grad, last_in, acts[:below] = lax.optimization_barrier(
                (grad, last_grad, last_in, acts[:below])
            )
            last_far = forward_blocks(place, last_in, gains, w_far, only=last, looped=True)
            last_own = forward_blocks(place, last_in, gains, w_near, only=last, looped=True)
        elif section:
            (grad,) = finish_backward(*finish)
        else:
            grad, own_grad, own_output = finish_backward(*finish, None, [grads, acts])
        if turn == 1:
            grads[last] = send(last_grad, [(below, last)])
            acts[below] = send(passed[below][0], [(last, below)])
            grad, grads[last], acts[below] = lax.optimization_barrier(
                (grad, grads[last], acts[below])
            )
        if section:
            grads[section] = grad
    shape = (1, micro_count, row_count, width)
    return own_output.reshape(shape), own_grad.reshape(shape)


def solution(mesh):
    placed = (
        P(None, None, "tp"),
        P(None, None, "tp"),
        P("section", "tp", None),
        P("section", "tp"),
    )
    return jax.shard_map(
        on_device,
        mesh=mesh,
        in_specs=placed,
        out_specs=(P("section", None, None, "tp"), P("section", None, None, "tp")),
        check_vma=False,
    )
```

```python
import jax
import jax.numpy as jnp
from jax import lax
from jax.experimental import pallas as pl
from jax.experimental.pallas import tpu as pltpu
from jax.sharding import PartitionSpec as P

EPSILON = 1e-05
MIB = 1 << 20
TAIL = 16
LANES = 128
SMEM_SPEC = pl.BlockSpec(memory_space=pltpu.SMEM)
VMEM_SPEC = pl.BlockSpec(memory_space=pltpu.VMEM)


def local_kernel(kernel, place, operands, out_shapes, limit=12 * MIB, cost=None, **options):
    def body(place_ref, *refs):
        kernel(place_ref[0], place_ref[1], *refs)

    options.setdefault("in_specs", [SMEM_SPEC] + [VMEM_SPEC] * len(operands))
    call = pl.pallas_call(
        body,
        out_shape=out_shapes,
        out_specs=[VMEM_SPEC] * len(out_shapes),
        compiler_params=pltpu.CompilerParams(vmem_limit_bytes=limit),
        cost_estimate=cost,
        **options,
    )
    return list(call(place, *operands))


def bf16(*shape):
    return jax.ShapeDtypeStruct(shape, jnp.bfloat16)


def f32(*shape):
    return jax.ShapeDtypeStruct(shape, jnp.float32)


def as_line(column):
    return jnp.broadcast_to(column, (column.shape[0], LANES)).T[:1]


def as_column(line):
    return jnp.broadcast_to(line, (LANES, line.shape[1])).T[:, :1]


def row_sum(value):
    return jnp.sum(value, axis=1, keepdims=True).astype(jnp.bfloat16).astype(jnp.float32)


def tail_sum(chunk_refs, rows):
    total = chunk_refs[0][rows : rows + TAIL, :rows].astype(jnp.float32)
    for chunk in chunk_refs[1:]:
        total = total + chunk[rows : rows + TAIL, :rows].astype(jnp.float32)
    return total


def matmul_cost(rows, width, count):
    return pl.CostEstimate(
        flops=2 * rows * width * width * count,
        bytes_accessed=2 * width * width * count,
        transcendentals=0,
    )


def in_hbm(array):
    return pltpu.with_memory_space_constraint(array, pltpu.HBM)


def in_vmem(array):
    return pltpu.with_memory_space_constraint(array, pltpu.VMEM)


def for_tiles(width, tile, body):
    def step(number, carry):
        body(pl.multiple_of(number * tile, tile))
        return carry

    lax.fori_loop(0, width // tile, step, 0)


def partial_chunks(tp, wide, gain_ref, take_block, out_refs, looped=False):
    rows, width = wide.shape
    tile = min(width, 256 if looped else 512)
    scaled = (wide * gain_ref[...]).astype(jnp.bfloat16)
    for number, out_ref in enumerate(out_refs):
        w_ref = take_block(number)

        def work(start, w_ref=w_ref, out_ref=out_ref):
            columns = pl.ds(start, tile)
            partial = jnp.dot(scaled, w_ref[:, columns], preferred_element_type=jnp.float32)
            out_ref[:rows, columns] = partial.astype(jnp.bfloat16)

        if looped:
            for_tiles(width, tile, work)
        else:
            for start in range(0, width, tile):
                work(start)
    line = as_line(jnp.sum(wide * wide, axis=1, keepdims=True))
    row_ids = lax.broadcasted_iota(jnp.int32, (TAIL, rows), 0)
    own_row = jnp.where(row_ids == tp % TAIL, jnp.broadcast_to(line, (TAIL, rows)), 0.0)
    for out_ref in out_refs:
        out_ref[rows : rows + TAIL, :] = jnp.zeros((TAIL, width), jnp.bfloat16)
        out_ref[rows : rows + TAIL, :rows] = own_row.astype(jnp.bfloat16)


def chunk_shapes(rows, width, count, pack):
    shapes = [bf16(rows + TAIL, width)] * count
    if pack:
        shapes[0] = bf16(2 * rows + TAIL, width)
    return shapes


def first_forward_blocks(place, a, gain_row, weights, codes, pack=False, other=None, other_from=None):
    rows, width = a.shape
    count = len(codes)
    others = [] if other is None else [other]

    def kernel(tp, section, a_hbm, gain_ref, w_hbm, *refs):
        w_ref, out_refs = refs[len(others)], refs[len(others) + 1 : len(others) + 1 + count]
        a_ref, a_done, w_done = refs[-3:]
        a_copy = pltpu.make_async_copy(a_hbm, a_ref, a_done)
        a_copy.start()
        copies = []
        for number, code in enumerate(codes):
            columns = pl.ds(pl.multiple_of((tp ^ code) * width, width), width)
            copies.append(
                pltpu.make_async_copy(w_hbm.at[:, columns], w_ref.at[number], w_done.at[number])
            )
            copies[-1].start()
        if others:
            chunk_ref = refs[len(others) + 1 + count]
            chunk_ref[:rows, :] = refs[0][...]
            chunk_ref[rows:, :] = jnp.zeros((TAIL, width), jnp.bfloat16)
        a_copy.wait()

        def take_block(number):
            copies[number].wait()
            return w_ref.at[number]

        partial_chunks(tp, a_ref[...].astype(jnp.float32), gain_ref, take_block, out_refs)
        if pack:
            out_refs[0][rows + TAIL :, :] = a_ref[...]
        if others:

            @pl.when(section >= other_from)
            def _():
                for out_ref in out_refs:
                    out_ref[: rows + TAIL, :] = chunk_ref[...]

    return local_kernel(
        kernel,
        place,
        [in_hbm(a), gain_row, in_hbm(weights)] + others,
        [pltpu.VMEM((count, width, width), jnp.bfloat16)]
        + chunk_shapes(rows, width, count, pack)
        + [bf16(rows + TAIL, width)] * len(others),
        in_specs=[SMEM_SPEC, pl.BlockSpec(memory_space=pltpu.HBM), VMEM_SPEC]
        + [pl.BlockSpec(memory_space=pltpu.HBM)]
        + [VMEM_SPEC] * len(others),
        scratch_shapes=[
            pltpu.VMEM((rows, width), jnp.bfloat16),
            pltpu.SemaphoreType.DMA,
            pltpu.SemaphoreType.DMA((count,)),
        ],
        cost=matmul_cost(rows, width, count),
    )


def forward_blocks(place, a, gain_row, w_half, pack=False, only=None, looped=False):
    rows, width = a.shape
    count = w_half.shape[0]

    def kernel(tp, section, a_ref, gain_ref, w_ref, *out_refs):
        def work():
            wide = a_ref[...].astype(jnp.float32)
            partial_chunks(
                tp, wide, gain_ref, lambda number: w_ref.at[number], out_refs, looped
            )
            if pack:
                out_refs[0][rows + TAIL :, :] = a_ref[...]

        if only is not None:
            pl.when(section == only)(work)
        else:
            work()

    return local_kernel(
        kernel,
        place,
        [a, gain_row, w_half],
        chunk_shapes(rows, width, count, pack),
        cost=matmul_cost(rows, width, count),
    )


def add_chunks(place, chunks, only=None):
    def kernel(tp, section, *refs):
        def work():
            total = refs[0][...].astype(jnp.float32)
            for chunk in refs[1:-1]:
                total = total + chunk[...].astype(jnp.float32)
            refs[-1][...] = total.astype(refs[-1].dtype)

        if only is not None:
            pl.when(section == only)(work)
        else:
            work()

    return local_kernel(kernel, place, chunks, [bf16(*chunks[0].shape)])[0]


def block_output(first_ref, chunk_refs, source, full_width):
    rows = source.shape[0]
    branch = first_ref[:rows, :].astype(jnp.float32)
    for chunk in chunk_refs:
        branch = branch + chunk[:rows, :].astype(jnp.float32)
    squares = jnp.sum(tail_sum([first_ref] + list(chunk_refs), rows), axis=0, keepdims=True)
    inv_rms = lax.rsqrt(as_column(squares) / full_width + EPSILON)
    output = (source.astype(jnp.float32) + inv_rms * branch).astype(jnp.bfloat16)
    return output, branch, inv_rms


def finish_forward(place, first, chunks, full_width):
    chunk_rows, width = chunks[0].shape
    rows = chunk_rows - TAIL

    def kernel(tp, section, first_ref, *refs):
        out_ref, branch_ref, rms_ref = refs[-3:]
        out_ref[...], branch_ref[...], inv_rms = block_output(
            first_ref, refs[:-3], first_ref[chunk_rows:, :], full_width
        )
        rms_ref[...] = jnp.broadcast_to(inv_rms, (rows, LANES))

    return local_kernel(
        kernel,
        place,
        [first] + chunks,
        [bf16(rows, width), f32(rows, width), f32(rows, LANES)],
    )


def two_parts(line):
    high = line.astype(jnp.bfloat16).astype(jnp.float32)
    return [high, line - high]


def store_tail(out_ref, rows, lines):
    row_ids = lax.broadcasted_iota(jnp.int32, (TAIL, rows), 0)
    tile = jnp.zeros((TAIL, rows), jnp.float32)
    for number, line in enumerate(lines):
        tile = jnp.where(row_ids == number, line, tile)
    out_ref[rows:, :] = jnp.zeros((TAIL, out_ref.shape[1]), out_ref.dtype)
    out_ref[rows:, :rows] = tile.astype(out_ref.dtype)


def row_line(value):
    return as_line(jnp.sum(value, axis=1, keepdims=True))


def gradient_chunks(place, upstream, branch, inv_rms, others, other_at):
    rows, width = upstream.shape
    replaced = [other for other in others if other is not None]

    def kernel(tp, section, up_ref, branch_ref, rms_ref, *refs):
        other_refs, out_refs = list(refs[: len(replaced)]), refs[len(replaced) :]
        dots = row_line(up_ref[...].astype(jnp.float32) * branch_ref[...])
        lines = [dots] + two_parts(rms_ref[...].T[:1])
        for out_ref in out_refs:
            out_ref[:rows, :] = up_ref[...]
            store_tail(out_ref, rows, lines)
        if replaced:

            @pl.when(section == other_at)
            def _():
                for other, out_ref in zip(others, out_refs):
                    if other is not None:
                        out_ref[...] = other_refs.pop(0)[...]

    shapes = [bf16(rows + TAIL, width)] * len(others)
    return local_kernel(kernel, place, [upstream, branch, inv_rms, *replaced], shapes)


def statistics_chunk(place, a, back_chunk, cot, branch, inv_rms):
    rows, width = a.shape

    def kernel(tp, section, a_ref, back_ref, cot_ref, branch_ref, rms_ref, out_ref):
        wide = a_ref[...].astype(jnp.float32)
        back = back_ref[:rows, :].astype(jnp.float32)
        cot_wide = cot_ref[...].astype(jnp.float32)
        lines = []
        for product in (
            wide * wide,
            wide * back,
            cot_wide * branch_ref[...],
            back * branch_ref[...],
            wide * branch_ref[...],
        ):
            lines += two_parts(row_line(product))
        out_ref[:rows, :] = a_ref[...]
        store_tail(out_ref, rows, lines + two_parts(rms_ref[...].T[:1]))

    return local_kernel(
        kernel, place, [a, back_chunk, cot, branch, inv_rms], [bf16(rows + TAIL, width)]
    )[0]


def block_products(blocks, rows, start, tile):
    total = None
    for w_ref, chunk in blocks:
        product = lax.dot_general(
            w_ref[pl.ds(start, tile), :],
            chunk[:rows, :],
            (((1,), (1,)), ((), ())),
            preferred_element_type=jnp.float32,
        )
        total = product if total is None else total + product
    return total


def gained_chunks(place, chunks, w_far, w_near, gain_row, only):
    count, width, _ = w_far.shape
    chunk_rows = chunks[0].shape[0]
    rows = chunk_rows - TAIL
    tile = min(width, 256)

    def kernel(tp, section, far_ref, near_ref, gain_ref, *refs):
        w_refs = [far_ref.at[k] for k in range(count)] + [near_ref.at[k] for k in range(count)]
        chunk_refs, (out_ref, pack_ref) = refs[:-2], refs[-2:]

        @pl.when(section == only)
        def _():
            def work(start):
                columns = pl.ds(start, tile)
                products = block_products(list(zip(w_refs, chunk_refs)), rows, start, tile)
                back = gain_ref[:, columns] * products.T
                out_ref[:rows, columns] = back.astype(jnp.bfloat16)

            for_tiles(width, tile, work)
            out_ref[rows:, :] = jnp.zeros((TAIL, width), jnp.bfloat16)
            for number, chunk in enumerate([out_ref] + list(chunk_refs)):
                pack_ref[number * chunk_rows : (number + 1) * chunk_rows, :] = chunk[...]

    return local_kernel(
        kernel,
        place,
        [w_far, w_near, gain_row] + chunks,
        [bf16(chunk_rows, width), bf16((1 + len(chunks)) * chunk_rows, width)],
        cost=matmul_cost(rows, width, 2 * count),
    )


def early_products(place, pack, gained, w_far, w_near, only):
    count, width, _ = w_far.shape
    given = [chunk for chunk in gained if chunk is not None]
    chunk_rows = given[0].shape[0]
    rows = chunk_rows - TAIL
    tile = min(width, 256)

    def kernel(tp, section, far_ref, near_ref, pack_ref, *refs):
        w_refs = [far_ref.at[k] for k in range(count)] + [near_ref.at[k] for k in range(count)]
        packed = [pack_ref.at[pl.ds(k * chunk_rows, chunk_rows), :] for k in range(1 + 2 * count)]
        gained_refs = list(refs[:-2])
        gained_refs = [packed[0] if chunk is None else gained_refs.pop(0) for chunk in gained]

        @pl.when(section == only)
        def _():
            def work(start):
                for chunk_refs, out_ref in zip((packed[1:], gained_refs), refs[-2:]):
                    out_ref[pl.ds(start, tile), :] = block_products(
                        list(zip(w_refs, chunk_refs)), rows, start, tile
                    )

            for_tiles(width, tile, work)

    return local_kernel(
        kernel,
        place,
        [w_far, w_near, pack] + given,
        [f32(width, rows)] * 2,
        cost=matmul_cost(rows, width, 4 * count),
    )


def backward_part(place, chunks, w_half, numbers, rows, before=None):
    width = w_half.shape[1]
    tile = min(width, 256 if before else 512)
    given = [] if before is None else list(before)

    def kernel(tp, section, w_ref, *refs):
        chunk_refs, (out_ref, sum_ref) = refs[: len(chunks)], refs[-2:]
        blocks = [(w_ref.at[k], chunk) for k, chunk in zip(numbers, chunk_refs)]

        def work(start):
            products = block_products(blocks, rows, start, tile)
            if given:
                products = products + refs[len(chunks)][pl.ds(start, tile), :]
            out_ref[pl.ds(start, tile), :] = products

        if given:
            for start in range(0, width, tile):
                work(start)
        else:
            for_tiles(width, tile, work)
        sums = tail_sum(chunk_refs, rows)
        sum_ref[...] = sums + refs[len(chunks) + 1][...] if given else sums

    return local_kernel(
        kernel,
        place,
        [w_half] + chunks + given,
        [f32(width, rows), f32(TAIL, rows)],
        cost=matmul_cost(rows, width, len(chunks)),
    )


def finish_backward(place, chunks, w_half, numbers, before, own, gain_row, a, full_width, last_block=None, finals=(), last_parts=()):
    rows, width = a.shape
    chunk_rows = rows + TAIL
    count = len(chunks)
    tile = min(width, 256)
    extra = [] if last_block is None else list(last_block)
    chosen = [[array for array in arrays if array is not None] for arrays in finals]
    chosen.append(list(last_parts))

    def kernel(tp, section, w_ref, *refs):
        chunk_refs = refs[:count]
        before_ref, sum_ref, own_ref, gain_ref, a_ref = refs[count : count + 5]
        rest = list(refs[count + 5 :])
        out_refs = rest[len(extra) + sum(len(arrays) for arrays in chosen) :]
        out_ref = out_refs[0]
        sums = sum_ref[...] + tail_sum(chunk_refs, rows)
        tail = own_ref[rows:chunk_rows, :rows].astype(jnp.float32)

        def pair(lines, number):
            return lines[number : number + 1] + lines[number + 1 : number + 2]

        if extra:
            cot_ref, gained_ref, cot_ref_products, gained_ref_products = rest[:4]
            last_rms = lax.rsqrt(pair(sums, 0) / full_width + EPSILON)
            last_scale = last_rms * last_rms * last_rms / full_width * pair(sums, 2)
            dots = pair(sums, 4) + last_rms * pair(sums, 6) - last_scale * pair(sums, 8)
            rms = as_column(pair(tail, 10))
            rms_column, scale_column = as_column(last_rms), as_column(last_scale)
            out_refs[1][...] = (
                cot_ref[...].astype(jnp.float32)
                + rms_column * gained_ref[:rows, :].astype(jnp.float32)
                - scale_column * own_ref[:rows, :].astype(jnp.float32)
            ).astype(jnp.bfloat16)
            up_ref = out_refs[1]
        else:
            dots = sums[:1]
            rms = as_column(pair(tail, 1))
            up_ref = own_ref
        scale = rms * rms * rms / full_width * as_column(dots)
        blocks = [(w_ref.at[k], chunk) for k, chunk in zip(numbers, chunk_refs)]
        for start in range(0, width, tile):
            columns = slice(start, start + tile)
            products = block_products(blocks, rows, start, tile) + before_ref[columns, :]
            if extra:
                products = (
                    cot_ref_products[columns, :]
                    + last_rms * gained_ref_products[columns, :]
                    - last_scale * products
                )
            out_ref[:, columns] = (
                up_ref[:rows, columns].astype(jnp.float32)
                + rms * gain_ref[:, columns] * products.T
                - scale * a_ref[:, columns].astype(jnp.float32)
            ).astype(jnp.bfloat16)
        final_refs = rest[len(extra) :]
        for arrays, final_ref in zip(finals, out_refs[1 + bool(extra) :]):
            for number, array in enumerate(arrays):
                source = out_ref if array is None else final_refs.pop(0)

                @pl.when(section == number)
                def _(source=source, final_ref=final_ref):
                    final_ref[...] = source[...]

        if last_parts:

            @pl.when(section == len(finals[0]) - 1)
            def _():
                first_ref, *sum_refs, in_ref = final_refs[: len(last_parts)]
                out_refs[-1][...] = block_output(first_ref, sum_refs, in_ref[...], full_width)[0]

    return local_kernel(
        kernel,
        place,
        [w_half, *chunks, *before, own, gain_row, a, *extra]
        + [array for arrays in chosen for array in arrays],
        [bf16(rows, width)] * (1 + bool(extra) + len(finals)),
        cost=matmul_cost(rows, width, count),
    )


def on_device(inputs, cotangent, weights, gains):
    section_count = lax.axis_size("section")
    tp_count = lax.axis_size("tp")
    micro_count, row_count, width = inputs.shape
    rows = micro_count * row_count
    full_width = weights.shape[2]
    last = section_count - 1
    below = last - 1
    place = jnp.stack([lax.axis_index("tp"), lax.axis_index("section")])
    across = tp_count // 2
    near = list(range(1, across))
    near_codes = [0] + near
    far_order = sorted(near, key=lambda e: e != across // 2)
    own_order = near[::-1]
    far_codes = [across ^ e for e in near_codes]
    numbers = {code: number for number, code in enumerate(near_codes)}
    inside = [(last, last)]

    def send(value, routes, step=0):
        pairs = [
            (source * tp_count + t, target * tp_count + (t ^ step))
            for source, target in routes
            for t in range(tp_count)
        ]
        return lax.ppermute(value, ("section", "tp"), pairs)

    def gather(chunk, source, target, near_chunks=None, riding=(), forward_riding=(), pack=None):
        route = [(source, target)]
        crossed = send(chunk, [(source, source)], across)
        found = [send(chunk if pack is None else pack, route)]
        for e in near:
            near_chunk = near_chunks[e] if near_chunks else chunk
            found.append(send(near_chunk, route + list(riding), e))
        far_chunk, _ = lax.optimization_barrier((crossed, found[0]))
        forwarded = [send(far_chunk, route)]
        forwarded += [send(crossed, route + list(forward_riding), e) for e in near]
        return found, forwarded, crossed

    cot = cotangent.reshape(rows, width)

    block_in = inputs.reshape(rows, width)
    block_ins = []
    passed = []
    cot_far = send(cot, inside, across)
    for section in range(last):
        beside = section ^ 1
        route = [(section, beside)]
        first_pass = section == 0
        if first_pass:
            w_far, *far, cot_chunk = first_forward_blocks(
                place, block_in, gains, weights[0], far_codes, other=cot, other_from=last
            )
            w_far = in_vmem(w_far)
        else:
            far = forward_blocks(place, block_in, gains, w_far, only=section)
        near_route = route + inside if first_pass else route
        arrived = {e: send(far[near_codes.index(e)], near_route, e) for e in far_order}
        if first_pass:
            w_near, *own, cot_far = first_forward_blocks(
                place, block_in, gains, weights[0], near_codes, pack=True, other=cot_far, other_from=last
            )
            w_near = in_vmem(w_near)
        else:
            own = forward_blocks(place, block_in, gains, w_near, pack=True, only=section)
        far_own = send(far[0], route)
        combined = add_chunks(place, [arrived[e] for e in far_order] + [far_own])
        pack, _ = lax.optimization_barrier((own[0], far_own))
        crossed = send(combined, [(beside, beside)], across)
        direct = {e: send(own[near_codes.index(e)], near_route, e) for e in own_order}
        if first_pass:
            cot_chunks = [cot_far] + [direct[e] for e in near]
            cot_chunks += [cot_chunk] + [arrived[e] for e in near]
        if section == below:
            gained_pack, combined = lax.optimization_barrier((gained_pack, combined))
            products = early_products(
                place,
                gained_pack,
                [gained_found[code] for code in far_codes + near_codes],
                w_far,
                w_near,
                below,
            )
            crossed, products = lax.optimization_barrier((crossed, products))
        passed.append(
            finish_forward(
                place, send(pack, route), [direct[e] for e in own_order] + [crossed], full_width
            )
        )
        block_ins.append(block_in)
        output = passed[-1][0]
        if section == 1:
            order = near_codes
            cot_chunks, output = lax.optimization_barrier((cot_chunks, output))
            gained, gained_pack = gained_chunks(place, cot_chunks, w_far, w_near, gains, last)
            found, forwarded, far_chunk = gather(gained, last, below, pack=gained_pack)
            output, found, _ = lax.optimization_barrier((output, found, far_chunk))
            gained_found = dict(zip(order, found))
            gained_pack = gained_found[0]
            gained_found[0] = None
        block_in = send(output, [(beside, section + 1)]) if section % 2 else output
        if section == 1:
            block_in, forwarded, gained_pack = lax.optimization_barrier(
                (block_in, forwarded, gained_pack)
            )
            gained_found.update({across ^ code: chunk for code, chunk in zip(order, forwarded)})
    last_in = block_in
    chunk = statistics_chunk(place, block_in, gained, cot, *passed[below][1:])
    grads = [None] * section_count
    acts = [None] * section_count
    for section in range(below, -1, -1):
        turn = below - section
        beside = section ^ 1
        near_chunks, riding = None, ()
        if turn:
            upstream = send(grad, [(section + 1, beside)]) if section % 2 else grad
            others = [None]
            if turn == 1:
                others += last_far[1:]
            if turn == 2:
                others += last_own[1:]
            chunk, *rest = gradient_chunks(place, upstream, *passed[section][1:], others, last)
            if turn <= 2:
                near_chunks, riding = dict(zip(near, rest)), inside
        found, forwarded, _ = gather(
            chunk, beside, section, near_chunks, riding, inside if turn == 1 else ()
        )
        part = backward_part(
            place, found, w_near, [numbers[e] for e in [0] + near], rows
        )
        early = [0] + near[-max(1, across // 4) :]
        late = [e for e in near if e not in early]
        by_code = dict(zip([0] + near, forwarded))
        part = backward_part(
            place, [by_code[e] for e in early], w_far, [numbers[e] for e in early], rows, part
        )
        if turn == 1:
            last_combined = add_chunks(place, [last_far[0]] + found[1:], only=last)
            last_crossed = send(last_combined, inside, across)
        if turn == 2:
            last_parts = [last_own[0]] + found[1:] + [last_crossed, last_in]
        finish = [
            place,
            [by_code[e] for e in late],
            w_far,
            [numbers[e] for e in late],
            part,
            found[0],
            gains,
            block_ins[section],
            full_width,
        ]
        if turn == 0:
            grad, last_grad = finish_backward(*finish, [cot, gained_pack, *products])
            acts[:below] = [
                send(passed[number][0], [(number ^ 1, number)]) for number in range(below)
            ]
            grad, last_grad, last_in, acts[:below] = lax.optimization_barrier(
                (grad, last_grad, last_in, acts[:below])
            )
            last_far = forward_blocks(place, last_in, gains, w_far, only=last, looped=True)
            last_own = forward_blocks(place, last_in, gains, w_near, only=last, looped=True)
        elif section:
            (grad,) = finish_backward(*finish)
        else:
            grad, own_grad, own_output = finish_backward(*finish, None, [grads, acts[:last]], last_parts)
        if turn == 1:
            grads[last] = send(last_grad, [(below, last)])
            acts[below] = send(passed[below][0], [(last, below)])
            grad, grads[last], acts[below] = lax.optimization_barrier(
                (grad, grads[last], acts[below])
            )
        if section:
            grads[section] = grad
    shape = (1, micro_count, row_count, width)
    return own_output.reshape(shape), own_grad.reshape(shape)


def solution(mesh):
    placed = (
        P(None, None, "tp"),
        P(None, None, "tp"),
        P("section", "tp", None),
        P("section", "tp"),
    )
    return jax.shard_map(
        on_device,
        mesh=mesh,
        in_specs=placed,
        out_specs=(P("section", None, None, "tp"), P("section", None, None, "tp")),
        check_vma=False,
    )
```

```python
import jax
import jax.numpy as jnp
from jax import lax
from jax.experimental import pallas as pl
from jax.experimental.pallas import tpu as pltpu
from jax.sharding import PartitionSpec as P

EPSILON = 1e-05
MIB = 1 << 20
TAIL = 16
LANES = 128
SMEM_SPEC = pl.BlockSpec(memory_space=pltpu.SMEM)
VMEM_SPEC = pl.BlockSpec(memory_space=pltpu.VMEM)


def local_kernel(kernel, place, operands, out_shapes, limit=12 * MIB, cost=None, **options):
    def body(place_ref, *refs):
        kernel(place_ref[0], place_ref[1], *refs)

    options.setdefault("in_specs", [SMEM_SPEC] + [VMEM_SPEC] * len(operands))
    call = pl.pallas_call(
        body,
        out_shape=out_shapes,
        out_specs=[VMEM_SPEC] * len(out_shapes),
        compiler_params=pltpu.CompilerParams(vmem_limit_bytes=limit),
        cost_estimate=cost,
        **options,
    )
    return list(call(place, *operands))


def bf16(*shape):
    return jax.ShapeDtypeStruct(shape, jnp.bfloat16)


def f32(*shape):
    return jax.ShapeDtypeStruct(shape, jnp.float32)


def as_line(column):
    return jnp.broadcast_to(column, (column.shape[0], LANES)).T[:1]


def as_column(line):
    return jnp.broadcast_to(line, (LANES, line.shape[1])).T[:, :1]


def row_sum(value):
    return jnp.sum(value, axis=1, keepdims=True).astype(jnp.bfloat16).astype(jnp.float32)


def tail_sum(chunk_refs, rows):
    total = chunk_refs[0][rows : rows + TAIL, :rows].astype(jnp.float32)
    for chunk in chunk_refs[1:]:
        total = total + chunk[rows : rows + TAIL, :rows].astype(jnp.float32)
    return total


def matmul_cost(rows, width, count):
    return pl.CostEstimate(
        flops=2 * rows * width * width * count,
        bytes_accessed=2 * width * width * count,
        transcendentals=0,
    )


def in_hbm(array):
    return pltpu.with_memory_space_constraint(array, pltpu.HBM)


def in_vmem(array):
    return pltpu.with_memory_space_constraint(array, pltpu.VMEM)


def for_tiles(width, tile, body):
    def step(number, carry):
        body(pl.multiple_of(number * tile, tile))
        return carry

    lax.fori_loop(0, width // tile, step, 0)


def partial_chunks(tp, wide, gain_ref, take_block, out_refs, looped=False):
    rows, width = wide.shape
    tile = min(width, 256 if looped else 512)
    scaled = (wide * gain_ref[...]).astype(jnp.bfloat16)
    for number, out_ref in enumerate(out_refs):
        w_ref = take_block(number)

        def work(start, w_ref=w_ref, out_ref=out_ref):
            columns = pl.ds(start, tile)
            partial = jnp.dot(scaled, w_ref[:, columns], preferred_element_type=jnp.float32)
            out_ref[:rows, columns] = partial.astype(jnp.bfloat16)

        if looped:
            for_tiles(width, tile, work)
        else:
            for start in range(0, width, tile):
                work(start)
    line = as_line(jnp.sum(wide * wide, axis=1, keepdims=True))
    row_ids = lax.broadcasted_iota(jnp.int32, (TAIL, rows), 0)
    own_row = jnp.where(row_ids == tp % TAIL, jnp.broadcast_to(line, (TAIL, rows)), 0.0)
    for out_ref in out_refs:
        out_ref[rows : rows + TAIL, :] = jnp.zeros((TAIL, width), jnp.bfloat16)
        out_ref[rows : rows + TAIL, :rows] = own_row.astype(jnp.bfloat16)


def chunk_shapes(rows, width, count, pack):
    shapes = [bf16(rows + TAIL, width)] * count
    if pack:
        shapes[0] = bf16(2 * rows + TAIL, width)
    return shapes


def first_forward_blocks(place, a, gain_row, weights, codes, pack=False, other=None, other_from=None):
    rows, width = a.shape
    count = len(codes)
    others = [] if other is None else [other]

    def kernel(tp, section, a_hbm, gain_ref, w_hbm, *refs):
        w_ref, out_refs = refs[len(others)], refs[len(others) + 1 : len(others) + 1 + count]
        a_ref, a_done, w_done = refs[-3:]
        a_copy = pltpu.make_async_copy(a_hbm, a_ref, a_done)
        a_copy.start()
        copies = []
        for number, code in enumerate(codes):
            columns = pl.ds(pl.multiple_of((tp ^ code) * width, width), width)
            copies.append(
                pltpu.make_async_copy(w_hbm.at[:, columns], w_ref.at[number], w_done.at[number])
            )
            copies[-1].start()
        if others:
            chunk_ref = refs[len(others) + 1 + count]
            chunk_ref[:rows, :] = refs[0][...]
            chunk_ref[rows:, :] = jnp.zeros((TAIL, width), jnp.bfloat16)
        a_copy.wait()

        def take_block(number):
            copies[number].wait()
            return w_ref.at[number]

        partial_chunks(tp, a_ref[...].astype(jnp.float32), gain_ref, take_block, out_refs)
        if pack:
            out_refs[0][rows + TAIL :, :] = a_ref[...]
        if others:

            @pl.when(section >= other_from)
            def _():
                for out_ref in out_refs:
                    out_ref[: rows + TAIL, :] = chunk_ref[...]

    return local_kernel(
        kernel,
        place,
        [in_hbm(a), gain_row, in_hbm(weights)] + others,
        [pltpu.VMEM((count, width, width), jnp.bfloat16)]
        + chunk_shapes(rows, width, count, pack)
        + [bf16(rows + TAIL, width)] * len(others),
        in_specs=[SMEM_SPEC, pl.BlockSpec(memory_space=pltpu.HBM), VMEM_SPEC]
        + [pl.BlockSpec(memory_space=pltpu.HBM)]
        + [VMEM_SPEC] * len(others),
        scratch_shapes=[
            pltpu.VMEM((rows, width), jnp.bfloat16),
            pltpu.SemaphoreType.DMA,
            pltpu.SemaphoreType.DMA((count,)),
        ],
        cost=matmul_cost(rows, width, count),
    )


def forward_blocks(place, a, gain_row, w_half, pack=False, only=None, looped=False):
    rows, width = a.shape
    count = w_half.shape[0]

    def kernel(tp, section, a_ref, gain_ref, w_ref, *out_refs):
        def work():
            wide = a_ref[...].astype(jnp.float32)
            partial_chunks(
                tp, wide, gain_ref, lambda number: w_ref.at[number], out_refs, looped
            )
            if pack:
                out_refs[0][rows + TAIL :, :] = a_ref[...]

        if only is not None:
            pl.when(section == only)(work)
        else:
            work()

    return local_kernel(
        kernel,
        place,
        [a, gain_row, w_half],
        chunk_shapes(rows, width, count, pack),
        cost=matmul_cost(rows, width, count),
    )


def add_chunks(place, chunks, only=None):
    def kernel(tp, section, *refs):
        def work():
            total = refs[0][...].astype(jnp.float32)
            for chunk in refs[1:-1]:
                total = total + chunk[...].astype(jnp.float32)
            refs[-1][...] = total.astype(refs[-1].dtype)

        if only is not None:
            pl.when(section == only)(work)
        else:
            work()

    return local_kernel(kernel, place, chunks, [bf16(*chunks[0].shape)])[0]


def block_output(first_ref, chunk_refs, source, full_width):
    rows = source.shape[0]
    branch = first_ref[:rows, :].astype(jnp.float32)
    for chunk in chunk_refs:
        branch = branch + chunk[:rows, :].astype(jnp.float32)
    squares = jnp.sum(tail_sum([first_ref] + list(chunk_refs), rows), axis=0, keepdims=True)
    inv_rms = lax.rsqrt(as_column(squares) / full_width + EPSILON)
    output = (source.astype(jnp.float32) + inv_rms * branch).astype(jnp.bfloat16)
    return output, branch, inv_rms


def finish_forward(place, first, chunks, full_width):
    chunk_rows, width = chunks[0].shape
    rows = chunk_rows - TAIL

    def kernel(tp, section, first_ref, *refs):
        out_ref, branch_ref, rms_ref = refs[-3:]
        out_ref[...], branch_ref[...], inv_rms = block_output(
            first_ref, refs[:-3], first_ref[chunk_rows:, :], full_width
        )
        rms_ref[...] = jnp.broadcast_to(inv_rms, (rows, LANES))

    return local_kernel(
        kernel,
        place,
        [first] + chunks,
        [bf16(rows, width), f32(rows, width), f32(rows, LANES)],
    )


def two_parts(line):
    high = line.astype(jnp.bfloat16).astype(jnp.float32)
    return [high, line - high]


def store_tail(out_ref, rows, lines):
    row_ids = lax.broadcasted_iota(jnp.int32, (TAIL, rows), 0)
    tile = jnp.zeros((TAIL, rows), jnp.float32)
    for number, line in enumerate(lines):
        tile = jnp.where(row_ids == number, line, tile)
    out_ref[rows:, :] = jnp.zeros((TAIL, out_ref.shape[1]), out_ref.dtype)
    out_ref[rows:, :rows] = tile.astype(out_ref.dtype)


def row_line(value):
    return as_line(jnp.sum(value, axis=1, keepdims=True))


def gradient_chunks(place, upstream, branch, inv_rms, others, other_at):
    rows, width = upstream.shape
    replaced = [other for other in others if other is not None]

    def kernel(tp, section, up_ref, branch_ref, rms_ref, *refs):
        other_refs, out_refs = list(refs[: len(replaced)]), refs[len(replaced) :]
        dots = row_line(up_ref[...].astype(jnp.float32) * branch_ref[...])
        lines = [dots] + two_parts(rms_ref[...].T[:1])
        for out_ref in out_refs:
            out_ref[:rows, :] = up_ref[...]
            store_tail(out_ref, rows, lines)
        if replaced:

            @pl.when(section == other_at)
            def _():
                for other, out_ref in zip(others, out_refs):
                    if other is not None:
                        out_ref[...] = other_refs.pop(0)[...]

    shapes = [bf16(rows + TAIL, width)] * len(others)
    return local_kernel(kernel, place, [upstream, branch, inv_rms, *replaced], shapes)


def statistics_chunk(place, a, back_chunk, cot, branch, inv_rms):
    rows, width = a.shape

    def kernel(tp, section, a_ref, back_ref, cot_ref, branch_ref, rms_ref, out_ref):
        wide = a_ref[...].astype(jnp.float32)
        back = back_ref[:rows, :].astype(jnp.float32)
        cot_wide = cot_ref[...].astype(jnp.float32)
        lines = []
        for product in (
            wide * wide,
            wide * back,
            cot_wide * branch_ref[...],
            back * branch_ref[...],
            wide * branch_ref[...],
        ):
            lines += two_parts(row_line(product))
        out_ref[:rows, :] = a_ref[...]
        store_tail(out_ref, rows, lines + two_parts(rms_ref[...].T[:1]))

    return local_kernel(
        kernel, place, [a, back_chunk, cot, branch, inv_rms], [bf16(rows + TAIL, width)]
    )[0]


def block_products(blocks, rows, start, tile):
    total = None
    for w_ref, chunk in blocks:
        product = lax.dot_general(
            w_ref[pl.ds(start, tile), :],
            chunk[:rows, :],
            (((1,), (1,)), ((), ())),
            preferred_element_type=jnp.float32,
        )
        total = product if total is None else total + product
    return total


def gained_chunks(place, chunks, w_far, w_near, gain_row, only):
    count, width, _ = w_far.shape
    chunk_rows = chunks[0].shape[0]
    rows = chunk_rows - TAIL
    tile = min(width, 256)

    def kernel(tp, section, far_ref, near_ref, gain_ref, *refs):
        w_refs = [far_ref.at[k] for k in range(count)] + [near_ref.at[k] for k in range(count)]
        chunk_refs, (out_ref, pack_ref) = refs[:-2], refs[-2:]

        @pl.when(section == only)
        def _():
            def work(start):
                columns = pl.ds(start, tile)
                products = block_products(list(zip(w_refs, chunk_refs)), rows, start, tile)
                back = gain_ref[:, columns] * products.T
                out_ref[:rows, columns] = back.astype(jnp.bfloat16)

            for_tiles(width, tile, work)
            out_ref[rows:, :] = jnp.zeros((TAIL, width), jnp.bfloat16)
            for number, chunk in enumerate([out_ref] + list(chunk_refs)):
                pack_ref[number * chunk_rows : (number + 1) * chunk_rows, :] = chunk[...]

    return local_kernel(
        kernel,
        place,
        [w_far, w_near, gain_row] + chunks,
        [bf16(chunk_rows, width), bf16((1 + len(chunks)) * chunk_rows, width)],
        cost=matmul_cost(rows, width, 2 * count),
    )


def early_products(place, pack, gained, w_far, w_near, only):
    count, width, _ = w_far.shape
    given = [chunk for chunk in gained if chunk is not None]
    chunk_rows = given[0].shape[0]
    rows = chunk_rows - TAIL
    tile = min(width, 256)

    def kernel(tp, section, far_ref, near_ref, pack_ref, *refs):
        w_refs = [far_ref.at[k] for k in range(count)] + [near_ref.at[k] for k in range(count)]
        packed = [pack_ref.at[pl.ds(k * chunk_rows, chunk_rows), :] for k in range(1 + 2 * count)]
        gained_refs = list(refs[:-2])
        gained_refs = [packed[0] if chunk is None else gained_refs.pop(0) for chunk in gained]

        @pl.when(section == only)
        def _():
            def work(start):
                for chunk_refs, out_ref in zip((packed[1:], gained_refs), refs[-2:]):
                    out_ref[pl.ds(start, tile), :] = block_products(
                        list(zip(w_refs, chunk_refs)), rows, start, tile
                    )

            for_tiles(width, tile, work)

    return local_kernel(
        kernel,
        place,
        [w_far, w_near, pack] + given,
        [f32(width, rows)] * 2,
        cost=matmul_cost(rows, width, 4 * count),
    )


def backward_part(place, chunks, w_half, numbers, rows, before=None):
    width = w_half.shape[1]
    tile = min(width, 256 if before else 512)
    given = [] if before is None else list(before)

    def kernel(tp, section, w_ref, *refs):
        chunk_refs, (out_ref, sum_ref) = refs[: len(chunks)], refs[-2:]
        blocks = [(w_ref.at[k], chunk) for k, chunk in zip(numbers, chunk_refs)]

        def work(start):
            products = block_products(blocks, rows, start, tile)
            if given:
                products = products + refs[len(chunks)][pl.ds(start, tile), :]
            out_ref[pl.ds(start, tile), :] = products

        if given:
            for start in range(0, width, tile):
                work(start)
        else:
            for_tiles(width, tile, work)
        sums = tail_sum(chunk_refs, rows)
        sum_ref[...] = sums + refs[len(chunks) + 1][...] if given else sums

    return local_kernel(
        kernel,
        place,
        [w_half] + chunks + given,
        [f32(width, rows), f32(TAIL, rows)],
        cost=matmul_cost(rows, width, len(chunks)),
    )


def finish_backward(place, chunks, w_half, numbers, before, own, gain_row, a, full_width, last_block=None, finals=(), last_parts=()):
    rows, width = a.shape
    chunk_rows = rows + TAIL
    count = len(chunks)
    tile = min(width, 256)
    extra = [] if last_block is None else list(last_block)
    chosen = [[array for array in arrays if array is not None] for arrays in finals]
    chosen.append(list(last_parts))

    def kernel(tp, section, w_ref, *refs):
        chunk_refs = refs[:count]
        before_ref, sum_ref, own_ref, gain_ref, a_ref = refs[count : count + 5]
        rest = list(refs[count + 5 :])
        out_refs = rest[len(extra) + sum(len(arrays) for arrays in chosen) :]
        out_ref = out_refs[0]
        sums = sum_ref[...] + tail_sum(chunk_refs, rows)
        tail = own_ref[rows:chunk_rows, :rows].astype(jnp.float32)

        def pair(lines, number):
            return lines[number : number + 1] + lines[number + 1 : number + 2]

        if extra:
            cot_ref, gained_ref, cot_ref_products, gained_ref_products = rest[:4]
            last_rms = lax.rsqrt(pair(sums, 0) / full_width + EPSILON)
            last_scale = last_rms * last_rms * last_rms / full_width * pair(sums, 2)
            dots = pair(sums, 4) + last_rms * pair(sums, 6) - last_scale * pair(sums, 8)
            rms = as_column(pair(tail, 10))
            rms_column, scale_column = as_column(last_rms), as_column(last_scale)
            out_refs[1][...] = (
                cot_ref[...].astype(jnp.float32)
                + rms_column * gained_ref[:rows, :].astype(jnp.float32)
                - scale_column * own_ref[:rows, :].astype(jnp.float32)
            ).astype(jnp.bfloat16)
            up_ref = out_refs[1]
        else:
            dots = sums[:1]
            rms = as_column(pair(tail, 1))
            up_ref = own_ref
        scale = rms * rms * rms / full_width * as_column(dots)
        blocks = [(w_ref.at[k], chunk) for k, chunk in zip(numbers, chunk_refs)]
        for start in range(0, width, tile):
            columns = slice(start, start + tile)
            products = block_products(blocks, rows, start, tile) + before_ref[columns, :]
            if extra:
                products = (
                    cot_ref_products[columns, :]
                    + last_rms * gained_ref_products[columns, :]
                    - last_scale * products
                )
            out_ref[:, columns] = (
                up_ref[:rows, columns].astype(jnp.float32)
                + rms * gain_ref[:, columns] * products.T
                - scale * a_ref[:, columns].astype(jnp.float32)
            ).astype(jnp.bfloat16)
        final_refs = rest[len(extra) :]
        for arrays, final_ref in zip(finals, out_refs[1 + bool(extra) :]):
            for number, array in enumerate(arrays):
                source = out_ref if array is None else final_refs.pop(0)

                @pl.when(section == number)
                def _(source=source, final_ref=final_ref):
                    final_ref[...] = source[...]

        if last_parts:

            @pl.when(section == len(finals[0]) - 1)
            def _():
                first_ref, *sum_refs, in_ref = final_refs[: len(last_parts)]
                out_refs[-1][...] = block_output(first_ref, sum_refs, in_ref[...], full_width)[0]

    return local_kernel(
        kernel,
        place,
        [w_half, *chunks, *before, own, gain_row, a, *extra]
        + [array for arrays in chosen for array in arrays],
        [bf16(rows, width)] * (1 + bool(extra) + len(finals)),
        cost=matmul_cost(rows, width, count),
    )


def on_device(inputs, cotangent, weights, gains):
    section_count = lax.axis_size("section")
    tp_count = lax.axis_size("tp")
    micro_count, row_count, width = inputs.shape
    rows = micro_count * row_count
    full_width = weights.shape[2]
    last = section_count - 1
    below = last - 1
    place = jnp.stack([lax.axis_index("tp"), lax.axis_index("section")])
    across = tp_count // 2
    near = list(range(1, across))
    near_codes = [0] + near
    own_order = near[::-1]
    far_codes = [across ^ e for e in near_codes]
    numbers = {code: number for number, code in enumerate(near_codes)}
    inside = [(last, last)]

    def send(value, routes, step=0):
        pairs = [
            (source * tp_count + t, target * tp_count + (t ^ step))
            for source, target in routes
            for t in range(tp_count)
        ]
        return lax.ppermute(value, ("section", "tp"), pairs)

    def gather(chunk, source, target, near_chunks=None, riding=(), forward_riding=(), pack=None):
        route = [(source, target)]
        crossed = send(chunk, [(source, source)], across)
        found = [send(chunk if pack is None else pack, route)]
        for e in near:
            near_chunk = near_chunks[e] if near_chunks else chunk
            found.append(send(near_chunk, route + list(riding), e))
        far_chunk, _ = lax.optimization_barrier((crossed, found[0]))
        forwarded = [send(far_chunk, route)]
        forwarded += [send(crossed, route + list(forward_riding), e) for e in near]
        return found, forwarded, crossed

    cot = cotangent.reshape(rows, width)

    block_in = inputs.reshape(rows, width)
    block_ins = []
    passed = []
    cot_far = send(cot, inside, across)
    for section in range(last):
        beside = section ^ 1
        route = [(section, beside)]
        first_pass = section == 0
        if first_pass:
            w_far, *far, cot_chunk = first_forward_blocks(
                place, block_in, gains, weights[0], far_codes, other=cot, other_from=last
            )
            w_far = in_vmem(w_far)
        else:
            far = forward_blocks(place, block_in, gains, w_far, only=section)
        near_route = route + inside if first_pass else route
        far_order = sorted(near, key=lambda e: e != across // 2) if section < 2 else own_order
        arrived = {e: send(far[near_codes.index(e)], near_route, e) for e in far_order}
        if first_pass:
            w_near, *own, cot_far = first_forward_blocks(
                place, block_in, gains, weights[0], near_codes, pack=True, other=cot_far, other_from=last
            )
            w_near = in_vmem(w_near)
        else:
            own = forward_blocks(place, block_in, gains, w_near, pack=True, only=section)
        far_own = send(far[0], route)
        combined = add_chunks(place, [arrived[e] for e in far_order] + [far_own])
        pack, _ = lax.optimization_barrier((own[0], far_own))
        crossed = send(combined, [(beside, beside)], across)
        direct = {e: send(own[near_codes.index(e)], near_route, e) for e in own_order}
        if first_pass:
            cot_chunks = [cot_far] + [direct[e] for e in near]
            cot_chunks += [cot_chunk] + [arrived[e] for e in near]
        if section == below:
            gained_pack, combined = lax.optimization_barrier((gained_pack, combined))
            products = early_products(
                place,
                gained_pack,
                [gained_found[code] for code in far_codes + near_codes],
                w_far,
                w_near,
                below,
            )
            crossed, products = lax.optimization_barrier((crossed, products))
        passed.append(
            finish_forward(
                place, send(pack, route), [direct[e] for e in own_order] + [crossed], full_width
            )
        )
        block_ins.append(block_in)
        output = passed[-1][0]
        if section == 1:
            order = near_codes
            cot_chunks, output = lax.optimization_barrier((cot_chunks, output))
            gained, gained_pack = gained_chunks(place, cot_chunks, w_far, w_near, gains, last)
            found, forwarded, far_chunk = gather(gained, last, below, pack=gained_pack)
            output, found, _ = lax.optimization_barrier((output, found, far_chunk))
            gained_found = dict(zip(order, found))
            gained_pack = gained_found[0]
            gained_found[0] = None
        block_in = send(output, [(beside, section + 1)]) if section % 2 else output
        if section == 1:
            block_in, forwarded, gained_pack = lax.optimization_barrier(
                (block_in, forwarded, gained_pack)
            )
            gained_found.update({across ^ code: chunk for code, chunk in zip(order, forwarded)})
    last_in = block_in
    chunk = statistics_chunk(place, block_in, gained, cot, *passed[below][1:])
    grads = [None] * section_count
    acts = [None] * section_count
    for section in range(below, -1, -1):
        turn = below - section
        beside = section ^ 1
        near_chunks, riding = None, ()
        if turn:
            upstream = send(grad, [(section + 1, beside)]) if section % 2 else grad
            others = [None]
            if turn == 1:
                others += last_far[1:]
            if turn == 2:
                others += last_own[1:]
            chunk, *rest = gradient_chunks(place, upstream, *passed[section][1:], others, last)
            if turn <= 2:
                near_chunks, riding = dict(zip(near, rest)), inside
        found, forwarded, _ = gather(
            chunk, beside, section, near_chunks, riding, inside if turn == 1 else ()
        )
        part = backward_part(
            place, found, w_near, [numbers[e] for e in [0] + near], rows
        )
        early = [0] + near[-max(1, across // 4) :]
        late = [e for e in near if e not in early]
        by_code = dict(zip([0] + near, forwarded))
        part = backward_part(
            place, [by_code[e] for e in early], w_far, [numbers[e] for e in early], rows, part
        )
        if turn == 1:
            last_combined = add_chunks(place, [last_far[0]] + found[1:], only=last)
            last_crossed = send(last_combined, inside, across)
        if turn == 2:
            last_parts = [last_own[0]] + found[1:] + [last_crossed, last_in]
        finish = [
            place,
            [by_code[e] for e in late],
            w_far,
            [numbers[e] for e in late],
            part,
            found[0],
            gains,
            block_ins[section],
            full_width,
        ]
        if turn == 0:
            grad, last_grad = finish_backward(*finish, [cot, gained_pack, *products])
            acts[:below] = [
                send(passed[number][0], [(number ^ 1, number)]) for number in range(below)
            ]
            grad, last_grad, last_in, acts[:below] = lax.optimization_barrier(
                (grad, last_grad, last_in, acts[:below])
            )
            last_far = forward_blocks(place, last_in, gains, w_far, only=last, looped=True)
            last_own = forward_blocks(place, last_in, gains, w_near, only=last, looped=True)
        elif section:
            (grad,) = finish_backward(*finish)
        else:
            grad, own_grad, own_output = finish_backward(*finish, None, [grads, acts[:last]], last_parts)
        if turn == 1:
            grads[last] = send(last_grad, [(below, last)])
            acts[below] = send(passed[below][0], [(last, below)])
            grad, grads[last], acts[below], last_crossed = lax.optimization_barrier(
                (grad, grads[last], acts[below], last_crossed)
            )
        if section:
            grads[section] = grad
    shape = (1, micro_count, row_count, width)
    return own_output.reshape(shape), own_grad.reshape(shape)


def solution(mesh):
    placed = (
        P(None, None, "tp"),
        P(None, None, "tp"),
        P("section", "tp", None),
        P("section", "tp"),
    )
    return jax.shard_map(
        on_device,
        mesh=mesh,
        in_specs=placed,
        out_specs=(P("section", None, None, "tp"), P("section", None, None, "tp")),
        check_vma=False,
    )
```

```python
import jax
import jax.numpy as jnp
from jax import lax
from jax.experimental import pallas as pl
from jax.experimental.pallas import tpu as pltpu
from jax.sharding import PartitionSpec as P

EPSILON = 1e-05
MIB = 1 << 20
TAIL = 16
LANES = 128
SMEM_SPEC = pl.BlockSpec(memory_space=pltpu.SMEM)
VMEM_SPEC = pl.BlockSpec(memory_space=pltpu.VMEM)


def local_kernel(kernel, place, operands, out_shapes, limit=12 * MIB, cost=None, **options):
    def body(place_ref, *refs):
        kernel(place_ref[0], place_ref[1], *refs)

    options.setdefault("in_specs", [SMEM_SPEC] + [VMEM_SPEC] * len(operands))
    call = pl.pallas_call(
        body,
        out_shape=out_shapes,
        out_specs=[VMEM_SPEC] * len(out_shapes),
        compiler_params=pltpu.CompilerParams(vmem_limit_bytes=limit),
        cost_estimate=cost,
        **options,
    )
    return list(call(place, *operands))


def bf16(*shape):
    return jax.ShapeDtypeStruct(shape, jnp.bfloat16)


def f32(*shape):
    return jax.ShapeDtypeStruct(shape, jnp.float32)


def as_line(column):
    return jnp.broadcast_to(column, (column.shape[0], LANES)).T[:1]


def as_column(line):
    return jnp.broadcast_to(line, (LANES, line.shape[1])).T[:, :1]


def row_sum(value):
    return jnp.sum(value, axis=1, keepdims=True).astype(jnp.bfloat16).astype(jnp.float32)


def tail_sum(chunk_refs, rows):
    total = chunk_refs[0][rows : rows + TAIL, :rows].astype(jnp.float32)
    for chunk in chunk_refs[1:]:
        total = total + chunk[rows : rows + TAIL, :rows].astype(jnp.float32)
    return total


def matmul_cost(rows, width, count):
    return pl.CostEstimate(
        flops=2 * rows * width * width * count,
        bytes_accessed=2 * width * width * count,
        transcendentals=0,
    )


def in_hbm(array):
    return pltpu.with_memory_space_constraint(array, pltpu.HBM)


def in_vmem(array):
    return pltpu.with_memory_space_constraint(array, pltpu.VMEM)


def for_tiles(width, tile, body):
    def step(number, carry):
        body(pl.multiple_of(number * tile, tile))
        return carry

    lax.fori_loop(0, width // tile, step, 0)


def partial_chunks(tp, wide, gain_ref, take_block, out_refs, looped=False):
    rows, width = wide.shape
    tile = min(width, 256 if looped else 512)
    scaled = (wide * gain_ref[...]).astype(jnp.bfloat16)
    for number, out_ref in enumerate(out_refs):
        w_ref = take_block(number)

        def work(start, w_ref=w_ref, out_ref=out_ref):
            columns = pl.ds(start, tile)
            partial = jnp.dot(scaled, w_ref[:, columns], preferred_element_type=jnp.float32)
            out_ref[:rows, columns] = partial.astype(jnp.bfloat16)

        if looped:
            for_tiles(width, tile, work)
        else:
            for start in range(0, width, tile):
                work(start)
    line = as_line(jnp.sum(wide * wide, axis=1, keepdims=True))
    row_ids = lax.broadcasted_iota(jnp.int32, (TAIL, rows), 0)
    own_row = jnp.where(row_ids == tp % TAIL, jnp.broadcast_to(line, (TAIL, rows)), 0.0)
    for out_ref in out_refs:
        out_ref[rows : rows + TAIL, :] = jnp.zeros((TAIL, width), jnp.bfloat16)
        out_ref[rows : rows + TAIL, :rows] = own_row.astype(jnp.bfloat16)


def chunk_shapes(rows, width, count, pack):
    shapes = [bf16(rows + TAIL, width)] * count
    if pack:
        shapes[0] = bf16(2 * rows + TAIL, width)
    return shapes


def first_forward_blocks(place, a, gain_row, weights, codes, pack=False, other=None, other_from=None):
    rows, width = a.shape
    count = len(codes)
    others = [] if other is None else [other]

    def kernel(tp, section, a_hbm, gain_ref, w_hbm, *refs):
        w_ref, out_refs = refs[len(others)], refs[len(others) + 1 : len(others) + 1 + count]
        a_ref, a_done, w_done = refs[-3:]
        a_copy = pltpu.make_async_copy(a_hbm, a_ref, a_done)
        a_copy.start()
        copies = []
        for number, code in enumerate(codes):
            columns = pl.ds(pl.multiple_of((tp ^ code) * width, width), width)
            copies.append(
                pltpu.make_async_copy(w_hbm.at[:, columns], w_ref.at[number], w_done.at[number])
            )
            copies[-1].start()
        if others:
            chunk_ref = refs[len(others) + 1 + count]
            chunk_ref[:rows, :] = refs[0][...]
            chunk_ref[rows:, :] = jnp.zeros((TAIL, width), jnp.bfloat16)
        a_copy.wait()

        def take_block(number):
            copies[number].wait()
            return w_ref.at[number]

        partial_chunks(tp, a_ref[...].astype(jnp.float32), gain_ref, take_block, out_refs)
        if pack:
            out_refs[0][rows + TAIL :, :] = a_ref[...]
        if others:

            @pl.when(section >= other_from)
            def _():
                for out_ref in out_refs:
                    out_ref[: rows + TAIL, :] = chunk_ref[...]

    return local_kernel(
        kernel,
        place,
        [in_hbm(a), gain_row, in_hbm(weights)] + others,
        [pltpu.VMEM((count, width, width), jnp.bfloat16)]
        + chunk_shapes(rows, width, count, pack)
        + [bf16(rows + TAIL, width)] * len(others),
        in_specs=[SMEM_SPEC, pl.BlockSpec(memory_space=pltpu.HBM), VMEM_SPEC]
        + [pl.BlockSpec(memory_space=pltpu.HBM)]
        + [VMEM_SPEC] * len(others),
        scratch_shapes=[
            pltpu.VMEM((rows, width), jnp.bfloat16),
            pltpu.SemaphoreType.DMA,
            pltpu.SemaphoreType.DMA((count,)),
        ],
        cost=matmul_cost(rows, width, count),
    )


def forward_blocks(place, a, gain_row, w_half, pack=False, only=None, looped=False):
    rows, width = a.shape
    count = w_half.shape[0]

    def kernel(tp, section, a_ref, gain_ref, w_ref, *out_refs):
        def work():
            wide = a_ref[...].astype(jnp.float32)
            partial_chunks(
                tp, wide, gain_ref, lambda number: w_ref.at[number], out_refs, looped
            )
            if pack:
                out_refs[0][rows + TAIL :, :] = a_ref[...]

        if only is not None:
            pl.when(section == only)(work)
        else:
            work()

    return local_kernel(
        kernel,
        place,
        [a, gain_row, w_half],
        chunk_shapes(rows, width, count, pack),
        cost=matmul_cost(rows, width, count),
    )


def add_chunks(place, chunks, only=None):
    def kernel(tp, section, *refs):
        def work():
            total = refs[0][...].astype(jnp.float32)
            for chunk in refs[1:-1]:
                total = total + chunk[...].astype(jnp.float32)
            refs[-1][...] = total.astype(refs[-1].dtype)

        if only is not None:
            pl.when(section == only)(work)
        else:
            work()

    return local_kernel(kernel, place, chunks, [bf16(*chunks[0].shape)])[0]


def block_output(first_ref, chunk_refs, source, full_width):
    rows = source.shape[0]
    branch = first_ref[:rows, :].astype(jnp.float32)
    for chunk in chunk_refs:
        branch = branch + chunk[:rows, :].astype(jnp.float32)
    squares = jnp.sum(tail_sum([first_ref] + list(chunk_refs), rows), axis=0, keepdims=True)
    inv_rms = lax.rsqrt(as_column(squares) / full_width + EPSILON)
    output = (source.astype(jnp.float32) + inv_rms * branch).astype(jnp.bfloat16)
    return output, branch, inv_rms


def finish_forward(place, first, chunks, full_width):
    chunk_rows, width = chunks[0].shape
    rows = chunk_rows - TAIL

    def kernel(tp, section, first_ref, *refs):
        out_ref, branch_ref, rms_ref = refs[-3:]
        out_ref[...], branch_ref[...], inv_rms = block_output(
            first_ref, refs[:-3], first_ref[chunk_rows:, :], full_width
        )
        rms_ref[...] = jnp.broadcast_to(inv_rms, (rows, LANES))

    return local_kernel(
        kernel,
        place,
        [first] + chunks,
        [bf16(rows, width), f32(rows, width), f32(rows, LANES)],
    )


def two_parts(line):
    high = line.astype(jnp.bfloat16).astype(jnp.float32)
    return [high, line - high]


def store_tail(out_ref, rows, lines):
    row_ids = lax.broadcasted_iota(jnp.int32, (TAIL, rows), 0)
    tile = jnp.zeros((TAIL, rows), jnp.float32)
    for number, line in enumerate(lines):
        tile = jnp.where(row_ids == number, line, tile)
    out_ref[rows:, :] = jnp.zeros((TAIL, out_ref.shape[1]), out_ref.dtype)
    out_ref[rows:, :rows] = tile.astype(out_ref.dtype)


def row_line(value):
    return as_line(jnp.sum(value, axis=1, keepdims=True))


def gradient_chunks(place, upstream, branch, inv_rms, others, other_at):
    rows, width = upstream.shape
    replaced = [other for other in others if other is not None]

    def kernel(tp, section, up_ref, branch_ref, rms_ref, *refs):
        other_refs, out_refs = list(refs[: len(replaced)]), refs[len(replaced) :]
        dots = row_line(up_ref[...].astype(jnp.float32) * branch_ref[...])
        lines = [dots] + two_parts(rms_ref[...].T[:1])
        for out_ref in out_refs:
            out_ref[:rows, :] = up_ref[...]
            store_tail(out_ref, rows, lines)
        if replaced:

            @pl.when(section == other_at)
            def _():
                for other, out_ref in zip(others, out_refs):
                    if other is not None:
                        out_ref[...] = other_refs.pop(0)[...]

    shapes = [bf16(rows + TAIL, width)] * len(others)
    return local_kernel(kernel, place, [upstream, branch, inv_rms, *replaced], shapes)


def statistics_chunk(place, a, back_chunk, cot, branch, inv_rms):
    rows, width = a.shape

    def kernel(tp, section, a_ref, back_ref, cot_ref, branch_ref, rms_ref, out_ref):
        wide = a_ref[...].astype(jnp.float32)
        back = back_ref[:rows, :].astype(jnp.float32)
        cot_wide = cot_ref[...].astype(jnp.float32)
        lines = []
        for product in (
            wide * wide,
            wide * back,
            cot_wide * branch_ref[...],
            back * branch_ref[...],
            wide * branch_ref[...],
        ):
            lines += two_parts(row_line(product))
        out_ref[:rows, :] = a_ref[...]
        store_tail(out_ref, rows, lines + two_parts(rms_ref[...].T[:1]))

    return local_kernel(
        kernel, place, [a, back_chunk, cot, branch, inv_rms], [bf16(rows + TAIL, width)]
    )[0]


def block_products(blocks, rows, start, tile):
    total = None
    for w_ref, chunk in blocks:
        product = lax.dot_general(
            w_ref[pl.ds(start, tile), :],
            chunk[:rows, :],
            (((1,), (1,)), ((), ())),
            preferred_element_type=jnp.float32,
        )
        total = product if total is None else total + product
    return total


def gained_chunks(place, chunks, w_far, w_near, gain_row, only):
    count, width, _ = w_far.shape
    chunk_rows = chunks[0].shape[0]
    rows = chunk_rows - TAIL
    tile = min(width, 256)

    def kernel(tp, section, far_ref, near_ref, gain_ref, *refs):
        w_refs = [far_ref.at[k] for k in range(count)] + [near_ref.at[k] for k in range(count)]
        chunk_refs, (out_ref, pack_ref) = refs[:-2], refs[-2:]

        @pl.when(section == only)
        def _():
            def work(start):
                columns = pl.ds(start, tile)
                products = block_products(list(zip(w_refs, chunk_refs)), rows, start, tile)
                back = gain_ref[:, columns] * products.T
                out_ref[:rows, columns] = back.astype(jnp.bfloat16)

            for_tiles(width, tile, work)
            out_ref[rows:, :] = jnp.zeros((TAIL, width), jnp.bfloat16)
            for number, chunk in enumerate([out_ref] + list(chunk_refs)):
                pack_ref[number * chunk_rows : (number + 1) * chunk_rows, :] = chunk[...]

    return local_kernel(
        kernel,
        place,
        [w_far, w_near, gain_row] + chunks,
        [bf16(chunk_rows, width), bf16((1 + len(chunks)) * chunk_rows, width)],
        cost=matmul_cost(rows, width, 2 * count),
    )


def early_products(place, pack, gained, w_far, w_near, only):
    count, width, _ = w_far.shape
    given = [chunk for chunk in gained if chunk is not None]
    chunk_rows = given[0].shape[0]
    rows = chunk_rows - TAIL
    tile = min(width, 256)

    def kernel(tp, section, far_ref, near_ref, pack_ref, *refs):
        w_refs = [far_ref.at[k] for k in range(count)] + [near_ref.at[k] for k in range(count)]
        packed = [pack_ref.at[pl.ds(k * chunk_rows, chunk_rows), :] for k in range(1 + 2 * count)]
        gained_refs = list(refs[:-2])
        gained_refs = [packed[0] if chunk is None else gained_refs.pop(0) for chunk in gained]

        @pl.when(section == only)
        def _():
            def work(start):
                for chunk_refs, out_ref in zip((packed[1:], gained_refs), refs[-2:]):
                    out_ref[pl.ds(start, tile), :] = block_products(
                        list(zip(w_refs, chunk_refs)), rows, start, tile
                    )

            for_tiles(width, tile, work)

    return local_kernel(
        kernel,
        place,
        [w_far, w_near, pack] + given,
        [f32(width, rows)] * 2,
        cost=matmul_cost(rows, width, 4 * count),
    )


def backward_part(place, chunks, w_half, numbers, rows, before=None):
    width = w_half.shape[1]
    tile = min(width, 256 if before else 512)
    given = [] if before is None else list(before)

    def kernel(tp, section, w_ref, *refs):
        chunk_refs, (out_ref, sum_ref) = refs[: len(chunks)], refs[-2:]
        blocks = [(w_ref.at[k], chunk) for k, chunk in zip(numbers, chunk_refs)]

        def work(start):
            products = block_products(blocks, rows, start, tile)
            if given:
                products = products + refs[len(chunks)][pl.ds(start, tile), :]
            out_ref[pl.ds(start, tile), :] = products

        if given:
            for start in range(0, width, tile):
                work(start)
        else:
            for_tiles(width, tile, work)
        sums = tail_sum(chunk_refs, rows)
        sum_ref[...] = sums + refs[len(chunks) + 1][...] if given else sums

    return local_kernel(
        kernel,
        place,
        [w_half] + chunks + given,
        [f32(width, rows), f32(TAIL, rows)],
        cost=matmul_cost(rows, width, len(chunks)),
    )


def finish_backward(place, chunks, w_half, numbers, before, own, gain_row, a, full_width, last_block=None, finals=(), last_parts=()):
    rows, width = a.shape
    chunk_rows = rows + TAIL
    count = len(chunks)
    tile = min(width, 256)
    extra = [] if last_block is None else list(last_block)
    chosen = [[array for array in arrays if array is not None] for arrays in finals]
    chosen.append(list(last_parts))

    def kernel(tp, section, w_ref, *refs):
        chunk_refs = refs[:count]
        before_ref, sum_ref, own_ref, gain_ref, a_ref = refs[count : count + 5]
        rest = list(refs[count + 5 :])
        out_refs = rest[len(extra) + sum(len(arrays) for arrays in chosen) :]
        out_ref = out_refs[0]
        sums = sum_ref[...] + tail_sum(chunk_refs, rows)
        tail = own_ref[rows:chunk_rows, :rows].astype(jnp.float32)

        def pair(lines, number):
            return lines[number : number + 1] + lines[number + 1 : number + 2]

        if extra:
            cot_ref, gained_ref, cot_ref_products, gained_ref_products = rest[:4]
            last_rms = lax.rsqrt(pair(sums, 0) / full_width + EPSILON)
            last_scale = last_rms * last_rms * last_rms / full_width * pair(sums, 2)
            dots = pair(sums, 4) + last_rms * pair(sums, 6) - last_scale * pair(sums, 8)
            rms = as_column(pair(tail, 10))
            rms_column, scale_column = as_column(last_rms), as_column(last_scale)
            out_refs[1][...] = (
                cot_ref[...].astype(jnp.float32)
                + rms_column * gained_ref[:rows, :].astype(jnp.float32)
                - scale_column * own_ref[:rows, :].astype(jnp.float32)
            ).astype(jnp.bfloat16)
            up_ref = out_refs[1]
        else:
            dots = sums[:1]
            rms = as_column(pair(tail, 1))
            up_ref = own_ref
        scale = rms * rms * rms / full_width * as_column(dots)
        blocks = [(w_ref.at[k], chunk) for k, chunk in zip(numbers, chunk_refs)]
        for start in range(0, width, tile):
            columns = slice(start, start + tile)
            products = block_products(blocks, rows, start, tile) + before_ref[columns, :]
            if extra:
                products = (
                    cot_ref_products[columns, :]
                    + last_rms * gained_ref_products[columns, :]
                    - last_scale * products
                )
            out_ref[:, columns] = (
                up_ref[:rows, columns].astype(jnp.float32)
                + rms * gain_ref[:, columns] * products.T
                - scale * a_ref[:, columns].astype(jnp.float32)
            ).astype(jnp.bfloat16)
        final_refs = rest[len(extra) :]
        for arrays, final_ref in zip(finals, out_refs[1 + bool(extra) :]):
            for number, array in enumerate(arrays):
                source = out_ref if array is None else final_refs.pop(0)

                @pl.when(section == number)
                def _(source=source, final_ref=final_ref):
                    final_ref[...] = source[...]

        if last_parts:

            @pl.when(section == len(finals[0]) - 1)
            def _():
                first_ref, *sum_refs, in_ref = final_refs[: len(last_parts)]
                out_refs[-1][...] = block_output(first_ref, sum_refs, in_ref[...], full_width)[0]

    return local_kernel(
        kernel,
        place,
        [w_half, *chunks, *before, own, gain_row, a, *extra]
        + [array for arrays in chosen for array in arrays],
        [bf16(rows, width)] * (1 + bool(extra) + len(finals)),
        cost=matmul_cost(rows, width, count),
    )


def on_device(inputs, cotangent, weights, gains):
    section_count = lax.axis_size("section")
    tp_count = lax.axis_size("tp")
    micro_count, row_count, width = inputs.shape
    rows = micro_count * row_count
    full_width = weights.shape[2]
    last = section_count - 1
    below = last - 1
    place = jnp.stack([lax.axis_index("tp"), lax.axis_index("section")])
    across = tp_count // 2
    near = list(range(1, across))
    near_codes = [0] + near
    own_order = near[::-1]
    far_codes = [across ^ e for e in near_codes]
    numbers = {code: number for number, code in enumerate(near_codes)}
    inside = [(last, last)]

    def send(value, routes, step=0):
        pairs = [
            (source * tp_count + t, target * tp_count + (t ^ step))
            for source, target in routes
            for t in range(tp_count)
        ]
        return lax.ppermute(value, ("section", "tp"), pairs)

    def gather(chunk, source, target, near_chunks=None, riding=(), forward_riding=(), pack=None):
        route = [(source, target)]
        crossed = send(chunk, [(source, source)], across)
        found = [send(chunk if pack is None else pack, route)]
        for e in near:
            near_chunk = near_chunks[e] if near_chunks else chunk
            found.append(send(near_chunk, route + list(riding), e))
        far_chunk, _ = lax.optimization_barrier((crossed, found[0]))
        forwarded = [send(far_chunk, route)]
        forwarded += [send(crossed, route + list(forward_riding), e) for e in near]
        return found, forwarded, crossed

    cot = cotangent.reshape(rows, width)

    block_in = inputs.reshape(rows, width)
    block_ins = []
    passed = []
    cot_far = send(cot, inside, across)
    for section in range(last):
        beside = section ^ 1
        route = [(section, beside)]
        first_pass = section == 0
        if first_pass:
            w_far, *far, cot_chunk = first_forward_blocks(
                place, block_in, gains, weights[0], far_codes, other=cot, other_from=last
            )
            w_far = in_vmem(w_far)
        else:
            far = forward_blocks(place, block_in, gains, w_far, only=section)
        near_route = route + inside if first_pass else route
        far_order = sorted(near, key=lambda e: e != across // 2) if section < 2 else own_order
        arrived = {e: send(far[near_codes.index(e)], near_route, e) for e in far_order}
        if first_pass:
            w_near, *own, cot_far = first_forward_blocks(
                place, block_in, gains, weights[0], near_codes, pack=True, other=cot_far, other_from=last
            )
            w_near = in_vmem(w_near)
        else:
            own = forward_blocks(place, block_in, gains, w_near, pack=True, only=section)
        far_own = send(far[0], route)
        combined = add_chunks(place, [arrived[e] for e in far_order] + [far_own])
        pack, _ = lax.optimization_barrier((own[0], far_own))
        crossed = send(combined, [(beside, beside)], across)
        direct = {e: send(own[near_codes.index(e)], near_route, e) for e in own_order}
        if first_pass:
            cot_chunks = [cot_far] + [direct[e] for e in near]
            cot_chunks += [cot_chunk] + [arrived[e] for e in near]
        if section == below:
            gained_pack, combined = lax.optimization_barrier((gained_pack, combined))
            products = early_products(
                place,
                gained_pack,
                [gained_found[code] for code in far_codes + near_codes],
                w_far,
                w_near,
                below,
            )
            crossed, products = lax.optimization_barrier((crossed, products))
        passed.append(
            finish_forward(
                place, send(pack, route), [direct[e] for e in own_order] + [crossed], full_width
            )
        )
        block_ins.append(block_in)
        output = passed[-1][0]
        if section == 1:
            order = near_codes
            cot_chunks, output = lax.optimization_barrier((cot_chunks, output))
            gained, gained_pack = gained_chunks(place, cot_chunks, w_far, w_near, gains, last)
            found, forwarded, far_chunk = gather(gained, last, below, pack=gained_pack)
            output, found, _ = lax.optimization_barrier((output, found, far_chunk))
            gained_found = dict(zip(order, found))
            gained_pack = gained_found[0]
            gained_found[0] = None
        block_in = send(output, [(beside, section + 1)]) if section % 2 else output
        if section == 1:
            block_in, forwarded, gained_pack = lax.optimization_barrier(
                (block_in, forwarded, gained_pack)
            )
            gained_found.update({across ^ code: chunk for code, chunk in zip(order, forwarded)})
    last_in = block_in
    chunk = statistics_chunk(place, block_in, gained, cot, *passed[below][1:])
    grads = [None] * section_count
    acts = [None] * section_count
    for section in range(below, -1, -1):
        turn = below - section
        beside = section ^ 1
        near_chunks, riding = None, ()
        if turn:
            upstream = send(grad, [(section + 1, beside)]) if section % 2 else grad
            others = [None]
            if turn == 1:
                others += last_far[1:]
            if turn == 2:
                others += last_own[1:]
            chunk, *rest = gradient_chunks(place, upstream, *passed[section][1:], others, last)
            if turn <= 2:
                near_chunks, riding = dict(zip(near, rest)), inside
        found, forwarded, _ = gather(
            chunk, beside, section, near_chunks, riding, inside if turn == 1 else ()
        )
        part = backward_part(
            place, found, w_near, [numbers[e] for e in [0] + near], rows
        )
        forward_order = near[-1:] + near[:-1] + [0]
        early, late = forward_order[: across // 2], forward_order[across // 2 :]
        by_code = dict(zip([0] + near, forwarded))
        part = backward_part(
            place, [by_code[e] for e in early], w_far, [numbers[e] for e in early], rows, part
        )
        if turn == 1:
            last_combined = add_chunks(place, [last_far[0]] + found[1:], only=last)
            last_crossed = send(last_combined, inside, across)
        if turn == 2:
            last_parts = [last_own[0]] + found[1:] + [last_crossed, last_in]
        finish = [
            place,
            [by_code[e] for e in late],
            w_far,
            [numbers[e] for e in late],
            part,
            found[0],
            gains,
            block_ins[section],
            full_width,
        ]
        if turn == 0:
            grad, last_grad = finish_backward(*finish, [cot, gained_pack, *products])
            acts[:below] = [
                send(passed[number][0], [(number ^ 1, number)]) for number in range(below)
            ]
            grad, last_grad, last_in, acts[:below] = lax.optimization_barrier(
                (grad, last_grad, last_in, acts[:below])
            )
            last_far = forward_blocks(place, last_in, gains, w_far, only=last, looped=True)
            last_own = forward_blocks(place, last_in, gains, w_near, only=last, looped=True)
        elif section:
            (grad,) = finish_backward(*finish)
        else:
            grad, own_grad, own_output = finish_backward(*finish, None, [grads, acts[:last]], last_parts)
        if turn == 1:
            grads[last] = send(last_grad, [(below, last)])
            acts[below] = send(passed[below][0], [(last, below)])
            grad, grads[last], acts[below], last_crossed = lax.optimization_barrier(
                (grad, grads[last], acts[below], last_crossed)
            )
        if section:
            grads[section] = grad
    shape = (1, micro_count, row_count, width)
    return own_output.reshape(shape), own_grad.reshape(shape)


def solution(mesh):
    placed = (
        P(None, None, "tp"),
        P(None, None, "tp"),
        P("section", "tp", None),
        P("section", "tp"),
    )
    return jax.shard_map(
        on_device,
        mesh=mesh,
        in_specs=placed,
        out_specs=(P("section", None, None, "tp"), P("section", None, None, "tp")),
        check_vma=False,
    )
```

```python
import jax
import jax.numpy as jnp
from jax import lax
from jax.experimental import pallas as pl
from jax.experimental.pallas import tpu as pltpu
from jax.sharding import PartitionSpec as P

EPSILON = 1e-05
MIB = 1 << 20
TAIL = 16
LANES = 128
SMEM_SPEC = pl.BlockSpec(memory_space=pltpu.SMEM)
VMEM_SPEC = pl.BlockSpec(memory_space=pltpu.VMEM)


def local_kernel(kernel, place, operands, out_shapes, limit=12 * MIB, cost=None, **options):
    def body(place_ref, *refs):
        kernel(place_ref[0], place_ref[1], *refs)

    options.setdefault("in_specs", [SMEM_SPEC] + [VMEM_SPEC] * len(operands))
    call = pl.pallas_call(
        body,
        out_shape=out_shapes,
        out_specs=[VMEM_SPEC] * len(out_shapes),
        compiler_params=pltpu.CompilerParams(vmem_limit_bytes=limit),
        cost_estimate=cost,
        **options,
    )
    return list(call(place, *operands))


def bf16(*shape):
    return jax.ShapeDtypeStruct(shape, jnp.bfloat16)


def f32(*shape):
    return jax.ShapeDtypeStruct(shape, jnp.float32)


def as_line(column):
    return jnp.broadcast_to(column, (column.shape[0], LANES)).T[:1]


def as_column(line):
    return jnp.broadcast_to(line, (LANES, line.shape[1])).T[:, :1]


def row_sum(value):
    return jnp.sum(value, axis=1, keepdims=True).astype(jnp.bfloat16).astype(jnp.float32)


def tail_sum(chunk_refs, rows):
    total = chunk_refs[0][rows : rows + TAIL, :rows].astype(jnp.float32)
    for chunk in chunk_refs[1:]:
        total = total + chunk[rows : rows + TAIL, :rows].astype(jnp.float32)
    return total


def matmul_cost(rows, width, count):
    return pl.CostEstimate(
        flops=2 * rows * width * width * count,
        bytes_accessed=2 * width * width * count,
        transcendentals=0,
    )


def in_hbm(array):
    return pltpu.with_memory_space_constraint(array, pltpu.HBM)


def in_vmem(array):
    return pltpu.with_memory_space_constraint(array, pltpu.VMEM)


def for_tiles(width, tile, body):
    def step(number, carry):
        body(pl.multiple_of(number * tile, tile))
        return carry

    lax.fori_loop(0, width // tile, step, 0)


def partial_chunks(tp, wide, gain_ref, take_block, out_refs, looped=False):
    rows, width = wide.shape
    tile = min(width, 256 if looped else 512)
    scaled = (wide * gain_ref[...]).astype(jnp.bfloat16)
    for number, out_ref in enumerate(out_refs):
        w_ref = take_block(number)

        def work(start, w_ref=w_ref, out_ref=out_ref):
            columns = pl.ds(start, tile)
            partial = jnp.dot(scaled, w_ref[:, columns], preferred_element_type=jnp.float32)
            out_ref[:rows, columns] = partial.astype(jnp.bfloat16)

        if looped:
            for_tiles(width, tile, work)
        else:
            for start in range(0, width, tile):
                work(start)
    line = as_line(jnp.sum(wide * wide, axis=1, keepdims=True))
    row_ids = lax.broadcasted_iota(jnp.int32, (TAIL, rows), 0)
    own_row = jnp.where(row_ids == tp % TAIL, jnp.broadcast_to(line, (TAIL, rows)), 0.0)
    for out_ref in out_refs:
        out_ref[rows : rows + TAIL, :] = jnp.zeros((TAIL, width), jnp.bfloat16)
        out_ref[rows : rows + TAIL, :rows] = own_row.astype(jnp.bfloat16)


def chunk_shapes(rows, width, count, pack):
    shapes = [bf16(rows + TAIL, width)] * count
    if pack:
        shapes[0] = bf16(2 * rows + TAIL, width)
    return shapes


def first_forward_blocks(place, a, gain_row, weights, codes, pack=False, other=None, other_from=None):
    rows, width = a.shape
    count = len(codes)
    others = [] if other is None else [other]

    def kernel(tp, section, a_hbm, gain_ref, w_hbm, *refs):
        w_ref, out_refs = refs[len(others)], refs[len(others) + 1 : len(others) + 1 + count]
        a_ref, a_done, w_done = refs[-3:]
        a_copy = pltpu.make_async_copy(a_hbm, a_ref, a_done)
        a_copy.start()
        copies = []
        for number, code in enumerate(codes):
            columns = pl.ds(pl.multiple_of((tp ^ code) * width, width), width)
            copies.append(
                pltpu.make_async_copy(w_hbm.at[:, columns], w_ref.at[number], w_done.at[number])
            )
            copies[-1].start()
        if others:
            chunk_ref = refs[len(others) + 1 + count]
            chunk_ref[:rows, :] = refs[0][...]
            chunk_ref[rows:, :] = jnp.zeros((TAIL, width), jnp.bfloat16)
        a_copy.wait()

        def take_block(number):
            copies[number].wait()
            return w_ref.at[number]

        partial_chunks(tp, a_ref[...].astype(jnp.float32), gain_ref, take_block, out_refs)
        if pack:
            out_refs[0][rows + TAIL :, :] = a_ref[...]
        if others:

            @pl.when(section >= other_from)
            def _():
                for out_ref in out_refs:
                    out_ref[: rows + TAIL, :] = chunk_ref[...]

    return local_kernel(
        kernel,
        place,
        [in_hbm(a), gain_row, in_hbm(weights)] + others,
        [pltpu.VMEM((count, width, width), jnp.bfloat16)]
        + chunk_shapes(rows, width, count, pack)
        + [bf16(rows + TAIL, width)] * len(others),
        in_specs=[SMEM_SPEC, pl.BlockSpec(memory_space=pltpu.HBM), VMEM_SPEC]
        + [pl.BlockSpec(memory_space=pltpu.HBM)]
        + [VMEM_SPEC] * len(others),
        scratch_shapes=[
            pltpu.VMEM((rows, width), jnp.bfloat16),
            pltpu.SemaphoreType.DMA,
            pltpu.SemaphoreType.DMA((count,)),
        ],
        cost=matmul_cost(rows, width, count),
    )


def forward_blocks(place, a, gain_row, w_half, pack=False, only=None, looped=False):
    rows, width = a.shape
    count = w_half.shape[0]

    def kernel(tp, section, a_ref, gain_ref, w_ref, *out_refs):
        def work():
            wide = a_ref[...].astype(jnp.float32)
            partial_chunks(
                tp, wide, gain_ref, lambda number: w_ref.at[number], out_refs, looped
            )
            if pack:
                out_refs[0][rows + TAIL :, :] = a_ref[...]

        if only is not None:
            pl.when(section == only)(work)
        else:
            work()

    return local_kernel(
        kernel,
        place,
        [a, gain_row, w_half],
        chunk_shapes(rows, width, count, pack),
        cost=matmul_cost(rows, width, count),
    )


def add_chunks(place, chunks, only=None):
    def kernel(tp, section, *refs):
        def work():
            total = refs[0][...].astype(jnp.float32)
            for chunk in refs[1:-1]:
                total = total + chunk[...].astype(jnp.float32)
            refs[-1][...] = total.astype(refs[-1].dtype)

        if only is not None:
            pl.when(section == only)(work)
        else:
            work()

    return local_kernel(kernel, place, chunks, [bf16(*chunks[0].shape)])[0]


def block_output(first_ref, chunk_refs, source, full_width):
    rows = source.shape[0]
    branch = first_ref[:rows, :].astype(jnp.float32)
    for chunk in chunk_refs:
        branch = branch + chunk[:rows, :].astype(jnp.float32)
    squares = jnp.sum(tail_sum([first_ref] + list(chunk_refs), rows), axis=0, keepdims=True)
    inv_rms = lax.rsqrt(as_column(squares) / full_width + EPSILON)
    output = (source.astype(jnp.float32) + inv_rms * branch).astype(jnp.bfloat16)
    return output, branch, inv_rms


def finish_forward(place, first, chunks, full_width):
    chunk_rows, width = chunks[0].shape
    rows = chunk_rows - TAIL

    def kernel(tp, section, first_ref, *refs):
        out_ref, branch_ref, rms_ref = refs[-3:]
        out_ref[...], branch_ref[...], inv_rms = block_output(
            first_ref, refs[:-3], first_ref[chunk_rows:, :], full_width
        )
        rms_ref[...] = jnp.broadcast_to(inv_rms, (rows, LANES))

    return local_kernel(
        kernel,
        place,
        [first] + chunks,
        [bf16(rows, width), f32(rows, width), f32(rows, LANES)],
    )


def two_parts(line):
    high = line.astype(jnp.bfloat16).astype(jnp.float32)
    return [high, line - high]


def store_tail(out_ref, rows, lines):
    row_ids = lax.broadcasted_iota(jnp.int32, (TAIL, rows), 0)
    tile = jnp.zeros((TAIL, rows), jnp.float32)
    for number, line in enumerate(lines):
        tile = jnp.where(row_ids == number, line, tile)
    out_ref[rows:, :] = jnp.zeros((TAIL, out_ref.shape[1]), out_ref.dtype)
    out_ref[rows:, :rows] = tile.astype(out_ref.dtype)


def row_line(value):
    return as_line(jnp.sum(value, axis=1, keepdims=True))


def gradient_chunks(place, upstream, branch, inv_rms, others, other_at):
    rows, width = upstream.shape
    replaced = [other for other in others if other is not None]

    def kernel(tp, section, up_ref, branch_ref, rms_ref, *refs):
        other_refs, out_refs = list(refs[: len(replaced)]), refs[len(replaced) :]
        dots = row_line(up_ref[...].astype(jnp.float32) * branch_ref[...])
        lines = [dots] + two_parts(rms_ref[...].T[:1])
        for out_ref in out_refs:
            out_ref[:rows, :] = up_ref[...]
            store_tail(out_ref, rows, lines)
        if replaced:

            @pl.when(section == other_at)
            def _():
                for other, out_ref in zip(others, out_refs):
                    if other is not None:
                        out_ref[...] = other_refs.pop(0)[...]

    shapes = [bf16(rows + TAIL, width)] * len(others)
    return local_kernel(kernel, place, [upstream, branch, inv_rms, *replaced], shapes)


def statistics_chunk(place, a, back_chunk, cot, branch, inv_rms):
    rows, width = a.shape

    def kernel(tp, section, a_ref, back_ref, cot_ref, branch_ref, rms_ref, out_ref):
        wide = a_ref[...].astype(jnp.float32)
        back = back_ref[:rows, :].astype(jnp.float32)
        cot_wide = cot_ref[...].astype(jnp.float32)
        lines = []
        for product in (
            wide * wide,
            wide * back,
            cot_wide * branch_ref[...],
            back * branch_ref[...],
            wide * branch_ref[...],
        ):
            lines += two_parts(row_line(product))
        out_ref[:rows, :] = a_ref[...]
        store_tail(out_ref, rows, lines + two_parts(rms_ref[...].T[:1]))

    return local_kernel(
        kernel, place, [a, back_chunk, cot, branch, inv_rms], [bf16(rows + TAIL, width)]
    )[0]


def block_products(blocks, rows, start, tile):
    total = None
    for w_ref, chunk in blocks:
        product = lax.dot_general(
            w_ref[pl.ds(start, tile), :],
            chunk[:rows, :],
            (((1,), (1,)), ((), ())),
            preferred_element_type=jnp.float32,
        )
        total = product if total is None else total + product
    return total


def gained_chunks(place, chunks, w_far, w_near, gain_row, only):
    count, width, _ = w_far.shape
    chunk_rows = chunks[0].shape[0]
    rows = chunk_rows - TAIL
    tile = min(width, 256)

    def kernel(tp, section, far_ref, near_ref, gain_ref, *refs):
        w_refs = [far_ref.at[k] for k in range(count)] + [near_ref.at[k] for k in range(count)]
        chunk_refs, (out_ref, pack_ref) = refs[:-2], refs[-2:]

        @pl.when(section == only)
        def _():
            def work(start):
                columns = pl.ds(start, tile)
                products = block_products(list(zip(w_refs, chunk_refs)), rows, start, tile)
                back = gain_ref[:, columns] * products.T
                out_ref[:rows, columns] = back.astype(jnp.bfloat16)

            for_tiles(width, tile, work)
            out_ref[rows:, :] = jnp.zeros((TAIL, width), jnp.bfloat16)
            for number, chunk in enumerate([out_ref] + list(chunk_refs)):
                pack_ref[number * chunk_rows : (number + 1) * chunk_rows, :] = chunk[...]

    return local_kernel(
        kernel,
        place,
        [w_far, w_near, gain_row] + chunks,
        [bf16(chunk_rows, width), bf16((1 + len(chunks)) * chunk_rows, width)],
        cost=matmul_cost(rows, width, 2 * count),
    )


def early_products(place, pack, gained, w_far, w_near, only):
    count, width, _ = w_far.shape
    given = [chunk for chunk in gained if chunk is not None]
    chunk_rows = given[0].shape[0]
    rows = chunk_rows - TAIL
    tile = min(width, 256)

    def kernel(tp, section, far_ref, near_ref, pack_ref, *refs):
        w_refs = [far_ref.at[k] for k in range(count)] + [near_ref.at[k] for k in range(count)]
        packed = [pack_ref.at[pl.ds(k * chunk_rows, chunk_rows), :] for k in range(1 + 2 * count)]
        gained_refs = list(refs[:-2])
        gained_refs = [packed[0] if chunk is None else gained_refs.pop(0) for chunk in gained]

        @pl.when(section == only)
        def _():
            def work(start):
                for chunk_refs, out_ref in zip((packed[1:], gained_refs), refs[-2:]):
                    out_ref[pl.ds(start, tile), :] = block_products(
                        list(zip(w_refs, chunk_refs)), rows, start, tile
                    )

            for_tiles(width, tile, work)

    return local_kernel(
        kernel,
        place,
        [w_far, w_near, pack] + given,
        [f32(width, rows)] * 2,
        cost=matmul_cost(rows, width, 4 * count),
    )


def backward_part(place, chunks, w_half, numbers, rows, before=None):
    width = w_half.shape[1]
    tile = min(width, 256 if before else 512)
    given = [] if before is None else list(before)

    def kernel(tp, section, w_ref, *refs):
        chunk_refs, (out_ref, sum_ref) = refs[: len(chunks)], refs[-2:]
        blocks = [(w_ref.at[k], chunk) for k, chunk in zip(numbers, chunk_refs)]

        def work(start):
            products = block_products(blocks, rows, start, tile)
            if given:
                products = products + refs[len(chunks)][pl.ds(start, tile), :]
            out_ref[pl.ds(start, tile), :] = products

        if given:
            for start in range(0, width, tile):
                work(start)
        else:
            for_tiles(width, tile, work)
        sums = tail_sum(chunk_refs, rows)
        sum_ref[...] = sums + refs[len(chunks) + 1][...] if given else sums

    return local_kernel(
        kernel,
        place,
        [w_half] + chunks + given,
        [f32(width, rows), f32(TAIL, rows)],
        cost=matmul_cost(rows, width, len(chunks)),
    )


def finish_backward(place, chunks, w_half, numbers, before, own, gain_row, a, full_width, last_block=None, finals=(), last_parts=()):
    rows, width = a.shape
    chunk_rows = rows + TAIL
    count = len(chunks)
    tile = min(width, 256)
    extra = [] if last_block is None else list(last_block)
    chosen = [[array for array in arrays if array is not None] for arrays in finals]
    chosen.append(list(last_parts))

    def kernel(tp, section, w_ref, *refs):
        chunk_refs = refs[:count]
        before_ref, sum_ref, own_ref, gain_ref, a_ref = refs[count : count + 5]
        rest = list(refs[count + 5 :])
        out_refs = rest[len(extra) + sum(len(arrays) for arrays in chosen) :]
        out_ref = out_refs[0]
        sums = sum_ref[...] + tail_sum(chunk_refs, rows)
        tail = own_ref[rows:chunk_rows, :rows].astype(jnp.float32)

        def pair(lines, number):
            return lines[number : number + 1] + lines[number + 1 : number + 2]

        if extra:
            cot_ref, gained_ref, cot_ref_products, gained_ref_products = rest[:4]
            last_rms = lax.rsqrt(pair(sums, 0) / full_width + EPSILON)
            last_scale = last_rms * last_rms * last_rms / full_width * pair(sums, 2)
            dots = pair(sums, 4) + last_rms * pair(sums, 6) - last_scale * pair(sums, 8)
            rms = as_column(pair(tail, 10))
            rms_column, scale_column = as_column(last_rms), as_column(last_scale)
            out_refs[1][...] = (
                cot_ref[...].astype(jnp.float32)
                + rms_column * gained_ref[:rows, :].astype(jnp.float32)
                - scale_column * own_ref[:rows, :].astype(jnp.float32)
            ).astype(jnp.bfloat16)
            up_ref = out_refs[1]
        else:
            dots = sums[:1]
            rms = as_column(pair(tail, 1))
            up_ref = own_ref
        scale = rms * rms * rms / full_width * as_column(dots)
        blocks = [(w_ref.at[k], chunk) for k, chunk in zip(numbers, chunk_refs)]
        for start in range(0, width, tile):
            columns = slice(start, start + tile)
            products = block_products(blocks, rows, start, tile) + before_ref[columns, :]
            if extra:
                products = (
                    cot_ref_products[columns, :]
                    + last_rms * gained_ref_products[columns, :]
                    - last_scale * products
                )
            out_ref[:, columns] = (
                up_ref[:rows, columns].astype(jnp.float32)
                + rms * gain_ref[:, columns] * products.T
                - scale * a_ref[:, columns].astype(jnp.float32)
            ).astype(jnp.bfloat16)
        final_refs = rest[len(extra) :]
        for arrays, final_ref in zip(finals, out_refs[1 + bool(extra) :]):
            for number, array in enumerate(arrays):
                source = out_ref if array is None else final_refs.pop(0)

                @pl.when(section == number)
                def _(source=source, final_ref=final_ref):
                    final_ref[...] = source[...]

        if last_parts:

            @pl.when(section == len(finals[0]) - 1)
            def _():
                first_ref, *sum_refs, in_ref = final_refs[: len(last_parts)]
                out_refs[-1][...] = block_output(first_ref, sum_refs, in_ref[...], full_width)[0]

    return local_kernel(
        kernel,
        place,
        [w_half, *chunks, *before, own, gain_row, a, *extra]
        + [array for arrays in chosen for array in arrays],
        [bf16(rows, width)] * (1 + bool(extra) + len(finals)),
        cost=matmul_cost(rows, width, count),
    )


def on_device(inputs, cotangent, weights, gains):
    section_count = lax.axis_size("section")
    tp_count = lax.axis_size("tp")
    micro_count, row_count, width = inputs.shape
    rows = micro_count * row_count
    full_width = weights.shape[2]
    last = section_count - 1
    below = last - 1
    place = jnp.stack([lax.axis_index("tp"), lax.axis_index("section")])
    across = tp_count // 2
    near = list(range(1, across))
    near_codes = [0] + near
    own_order = near[::-1]
    far_codes = [across ^ e for e in near_codes]
    numbers = {code: number for number, code in enumerate(near_codes)}
    inside = [(last, last)]

    def send(value, routes, step=0):
        pairs = [
            (source * tp_count + t, target * tp_count + (t ^ step))
            for source, target in routes
            for t in range(tp_count)
        ]
        return lax.ppermute(value, ("section", "tp"), pairs)

    def gather(chunk, source, target, near_chunks=None, riding=(), forward_riding=(), pack=None, after=()):
        route = [(source, target)]
        crossed, _ = lax.optimization_barrier((send(chunk, [(source, source)], across), after))
        found = [send(chunk if pack is None else pack, route)]
        for e in near:
            near_chunk = near_chunks[e] if near_chunks else chunk
            found.append(send(near_chunk, route + list(riding), e))
        far_chunk, _ = lax.optimization_barrier((crossed, found[0]))
        forwarded = [send(far_chunk, route)]
        forwarded += [send(crossed, route + list(forward_riding), e) for e in near]
        return found, forwarded, crossed

    cot = cotangent.reshape(rows, width)

    block_in = inputs.reshape(rows, width)
    block_ins = []
    passed = []
    cot_far = send(cot, inside, across)
    for section in range(last):
        beside = section ^ 1
        route = [(section, beside)]
        first_pass = section == 0
        if first_pass:
            w_far, *far, cot_chunk = first_forward_blocks(
                place, block_in, gains, weights[0], far_codes, other=cot, other_from=last
            )
            w_far = in_vmem(w_far)
        else:
            far = forward_blocks(place, block_in, gains, w_far, only=section)
        near_route = route + inside if first_pass else route
        far_order = sorted(near, key=lambda e: e != across // 2) if section < 2 else own_order
        arrived = {e: send(far[near_codes.index(e)], near_route, e) for e in far_order}
        if first_pass:
            w_near, *own, cot_far = first_forward_blocks(
                place, block_in, gains, weights[0], near_codes, pack=True, other=cot_far, other_from=last
            )
            w_near = in_vmem(w_near)
        else:
            own = forward_blocks(place, block_in, gains, w_near, pack=True, only=section)
        far_own = send(far[0], route)
        combined = add_chunks(place, [arrived[e] for e in far_order] + [far_own])
        pack, _ = lax.optimization_barrier((own[0], far_own))
        crossed = send(combined, [(beside, beside)], across)
        direct = {e: send(own[near_codes.index(e)], near_route, e) for e in own_order}
        if first_pass:
            cot_chunks = [cot_far] + [direct[e] for e in near]
            cot_chunks += [cot_chunk] + [arrived[e] for e in near]
        if section == below:
            gained_pack, combined = lax.optimization_barrier((gained_pack, combined))
            products = early_products(
                place,
                gained_pack,
                [gained_found[code] for code in far_codes + near_codes],
                w_far,
                w_near,
                below,
            )
            crossed, products = lax.optimization_barrier((crossed, products))
        passed.append(
            finish_forward(
                place, send(pack, route), [direct[e] for e in own_order] + [crossed], full_width
            )
        )
        block_ins.append(block_in)
        output = passed[-1][0]
        if section == 1:
            order = near_codes
            cot_chunks, output = lax.optimization_barrier((cot_chunks, output))
            gained, gained_pack = gained_chunks(place, cot_chunks, w_far, w_near, gains, last)
            found, forwarded, far_chunk = gather(gained, last, below, pack=gained_pack)
            output, found, _ = lax.optimization_barrier((output, found, far_chunk))
            gained_found = dict(zip(order, found))
            gained_pack = gained_found[0]
            gained_found[0] = None
        block_in = send(output, [(beside, section + 1)]) if section % 2 else output
        if section == 1:
            block_in, forwarded, gained_pack = lax.optimization_barrier(
                (block_in, forwarded, gained_pack)
            )
            gained_found.update({across ^ code: chunk for code, chunk in zip(order, forwarded)})
    last_in = block_in
    chunk = statistics_chunk(place, block_in, gained, cot, *passed[below][1:])
    grads = [None] * section_count
    acts = [None] * section_count
    for section in range(below, -1, -1):
        turn = below - section
        beside = section ^ 1
        near_chunks, riding = None, ()
        if turn:
            upstream = send(grad, [(section + 1, beside)]) if section % 2 else grad
            others = [None]
            if turn == 1:
                others += last_far[1:]
            if turn == 2:
                others += last_own[1:]
            chunk, *rest = gradient_chunks(place, upstream, *passed[section][1:], others, last)
            if turn <= 2:
                near_chunks, riding = dict(zip(near, rest)), inside
        found, forwarded, _ = gather(
            chunk,
            beside,
            section,
            near_chunks,
            riding,
            inside if turn == 1 else (),
            after=last_crossed if turn == 2 else (),
        )
        part = backward_part(
            place, found, w_near, [numbers[e] for e in [0] + near], rows
        )
        early = [0] + near[-max(1, across // 4) :]
        late = [e for e in near if e not in early]
        by_code = dict(zip([0] + near, forwarded))
        part = backward_part(
            place, [by_code[e] for e in early], w_far, [numbers[e] for e in early], rows, part
        )
        if turn == 1:
            last_combined = add_chunks(place, [last_far[0]] + found[1:], only=last)
            last_crossed = send(last_combined, inside, across)
        if turn == 2:
            last_parts = [last_own[0]] + found[1:] + [last_crossed, last_in]
        finish = [
            place,
            [by_code[e] for e in late],
            w_far,
            [numbers[e] for e in late],
            part,
            found[0],
            gains,
            block_ins[section],
            full_width,
        ]
        if turn == 0:
            grad, last_grad = finish_backward(*finish, [cot, gained_pack, *products])
            acts[:below] = [
                send(passed[number][0], [(number ^ 1, number)]) for number in range(below)
            ]
            grad, last_grad, last_in, acts[:below] = lax.optimization_barrier(
                (grad, last_grad, last_in, acts[:below])
            )
            last_far = forward_blocks(place, last_in, gains, w_far, only=last, looped=True)
            last_own = forward_blocks(place, last_in, gains, w_near, only=last, looped=True)
        elif section:
            (grad,) = finish_backward(*finish)
        else:
            grad, own_grad, own_output = finish_backward(*finish, None, [grads, acts[:last]], last_parts)
        if turn == 1:
            grads[last] = send(last_grad, [(below, last)])
            acts[below] = send(passed[below][0], [(last, below)])
            grad, grads[last], acts[below] = lax.optimization_barrier(
                (grad, grads[last], acts[below])
            )
        if section:
            grads[section] = grad
    shape = (1, micro_count, row_count, width)
    return own_output.reshape(shape), own_grad.reshape(shape)


def solution(mesh):
    placed = (
        P(None, None, "tp"),
        P(None, None, "tp"),
        P("section", "tp", None),
        P("section", "tp"),
    )
    return jax.shard_map(
        on_device,
        mesh=mesh,
        in_specs=placed,
        out_specs=(P("section", None, None, "tp"), P("section", None, None, "tp")),
        check_vma=False,
    )
```

```python
import jax
import jax.numpy as jnp
from jax import lax
from jax.experimental import pallas as pl
from jax.experimental.pallas import tpu as pltpu
from jax.sharding import PartitionSpec as P

EPSILON = 1e-05
MIB = 1 << 20
TAIL = 16
LANES = 128
SMEM_SPEC = pl.BlockSpec(memory_space=pltpu.SMEM)
VMEM_SPEC = pl.BlockSpec(memory_space=pltpu.VMEM)


def local_kernel(kernel, place, operands, out_shapes, limit=12 * MIB, cost=None, **options):
    def body(place_ref, *refs):
        kernel(place_ref[0], place_ref[1], *refs)

    options.setdefault("in_specs", [SMEM_SPEC] + [VMEM_SPEC] * len(operands))
    call = pl.pallas_call(
        body,
        out_shape=out_shapes,
        out_specs=[VMEM_SPEC] * len(out_shapes),
        compiler_params=pltpu.CompilerParams(vmem_limit_bytes=limit),
        cost_estimate=cost,
        **options,
    )
    return list(call(place, *operands))


def bf16(*shape):
    return jax.ShapeDtypeStruct(shape, jnp.bfloat16)


def f32(*shape):
    return jax.ShapeDtypeStruct(shape, jnp.float32)


def as_line(column):
    return jnp.broadcast_to(column, (column.shape[0], LANES)).T[:1]


def as_column(line):
    return jnp.broadcast_to(line, (LANES, line.shape[1])).T[:, :1]


def row_sum(value):
    return jnp.sum(value, axis=1, keepdims=True).astype(jnp.bfloat16).astype(jnp.float32)


def tail_sum(chunk_refs, rows):
    total = chunk_refs[0][rows : rows + TAIL, :rows].astype(jnp.float32)
    for chunk in chunk_refs[1:]:
        total = total + chunk[rows : rows + TAIL, :rows].astype(jnp.float32)
    return total


def matmul_cost(rows, width, count):
    return pl.CostEstimate(
        flops=2 * rows * width * width * count,
        bytes_accessed=2 * width * width * count,
        transcendentals=0,
    )


def in_hbm(array):
    return pltpu.with_memory_space_constraint(array, pltpu.HBM)


def in_vmem(array):
    return pltpu.with_memory_space_constraint(array, pltpu.VMEM)


def for_tiles(width, tile, body):
    def step(number, carry):
        body(pl.multiple_of(number * tile, tile))
        return carry

    lax.fori_loop(0, width // tile, step, 0)


def partial_chunks(tp, wide, gain_ref, take_block, out_refs, looped=False):
    rows, width = wide.shape
    tile = min(width, 256 if looped else 512)
    scaled = (wide * gain_ref[...]).astype(jnp.bfloat16)
    for number, out_ref in enumerate(out_refs):
        w_ref = take_block(number)

        def work(start, w_ref=w_ref, out_ref=out_ref):
            columns = pl.ds(start, tile)
            partial = jnp.dot(scaled, w_ref[:, columns], preferred_element_type=jnp.float32)
            out_ref[:rows, columns] = partial.astype(jnp.bfloat16)

        if looped:
            for_tiles(width, tile, work)
        else:
            for start in range(0, width, tile):
                work(start)
    line = as_line(jnp.sum(wide * wide, axis=1, keepdims=True))
    row_ids = lax.broadcasted_iota(jnp.int32, (TAIL, rows), 0)
    own_row = jnp.where(row_ids == tp % TAIL, jnp.broadcast_to(line, (TAIL, rows)), 0.0)
    for out_ref in out_refs:
        out_ref[rows : rows + TAIL, :] = jnp.zeros((TAIL, width), jnp.bfloat16)
        out_ref[rows : rows + TAIL, :rows] = own_row.astype(jnp.bfloat16)


def chunk_shapes(rows, width, count, pack):
    shapes = [bf16(rows + TAIL, width)] * count
    if pack:
        shapes[0] = bf16(2 * rows + TAIL, width)
    return shapes


def first_forward_blocks(place, a, gain_row, weights, codes, pack=False, other=None, other_from=None):
    rows, width = a.shape
    count = len(codes)
    others = [] if other is None else [other]

    def kernel(tp, section, a_hbm, gain_ref, w_hbm, *refs):
        w_ref, out_refs = refs[len(others)], refs[len(others) + 1 : len(others) + 1 + count]
        a_ref, a_done, w_done = refs[-3:]
        a_copy = pltpu.make_async_copy(a_hbm, a_ref, a_done)
        a_copy.start()
        copies = []
        for number, code in enumerate(codes):
            columns = pl.ds(pl.multiple_of((tp ^ code) * width, width), width)
            copies.append(
                pltpu.make_async_copy(w_hbm.at[:, columns], w_ref.at[number], w_done.at[number])
            )
            copies[-1].start()
        if others:
            chunk_ref = refs[len(others) + 1 + count]
            chunk_ref[:rows, :] = refs[0][...]
            chunk_ref[rows:, :] = jnp.zeros((TAIL, width), jnp.bfloat16)
        a_copy.wait()

        def take_block(number):
            copies[number].wait()
            return w_ref.at[number]

        partial_chunks(tp, a_ref[...].astype(jnp.float32), gain_ref, take_block, out_refs)
        if pack:
            out_refs[0][rows + TAIL :, :] = a_ref[...]
        if others:

            @pl.when(section >= other_from)
            def _():
                for out_ref in out_refs:
                    out_ref[: rows + TAIL, :] = chunk_ref[...]

    return local_kernel(
        kernel,
        place,
        [in_hbm(a), gain_row, in_hbm(weights)] + others,
        [pltpu.VMEM((count, width, width), jnp.bfloat16)]
        + chunk_shapes(rows, width, count, pack)
        + [bf16(rows + TAIL, width)] * len(others),
        in_specs=[SMEM_SPEC, pl.BlockSpec(memory_space=pltpu.HBM), VMEM_SPEC]
        + [pl.BlockSpec(memory_space=pltpu.HBM)]
        + [VMEM_SPEC] * len(others),
        scratch_shapes=[
            pltpu.VMEM((rows, width), jnp.bfloat16),
            pltpu.SemaphoreType.DMA,
            pltpu.SemaphoreType.DMA((count,)),
        ],
        cost=matmul_cost(rows, width, count),
    )


def forward_blocks(place, a, gain_row, w_half, pack=False, only=None, looped=False):
    rows, width = a.shape
    count = w_half.shape[0]

    def kernel(tp, section, a_ref, gain_ref, w_ref, *out_refs):
        def work():
            wide = a_ref[...].astype(jnp.float32)
            partial_chunks(
                tp, wide, gain_ref, lambda number: w_ref.at[number], out_refs, looped
            )
            if pack:
                out_refs[0][rows + TAIL :, :] = a_ref[...]

        if only is not None:
            pl.when(section == only)(work)
        else:
            work()

    return local_kernel(
        kernel,
        place,
        [a, gain_row, w_half],
        chunk_shapes(rows, width, count, pack),
        cost=matmul_cost(rows, width, count),
    )


def add_chunks(place, chunks, only=None):
    def kernel(tp, section, *refs):
        def work():
            total = refs[0][...].astype(jnp.float32)
            for chunk in refs[1:-1]:
                total = total + chunk[...].astype(jnp.float32)
            refs[-1][...] = total.astype(refs[-1].dtype)

        if only is not None:
            pl.when(section == only)(work)
        else:
            work()

    return local_kernel(kernel, place, chunks, [bf16(*chunks[0].shape)])[0]


def block_output(first_ref, chunk_refs, source, full_width):
    rows = source.shape[0]
    branch = first_ref[:rows, :].astype(jnp.float32)
    for chunk in chunk_refs:
        branch = branch + chunk[:rows, :].astype(jnp.float32)
    squares = jnp.sum(tail_sum([first_ref] + list(chunk_refs), rows), axis=0, keepdims=True)
    inv_rms = lax.rsqrt(as_column(squares) / full_width + EPSILON)
    output = (source.astype(jnp.float32) + inv_rms * branch).astype(jnp.bfloat16)
    return output, branch, inv_rms


def finish_forward(place, first, chunks, full_width):
    chunk_rows, width = chunks[0].shape
    rows = chunk_rows - TAIL

    def kernel(tp, section, first_ref, *refs):
        out_ref, branch_ref, rms_ref = refs[-3:]
        out_ref[...], branch_ref[...], inv_rms = block_output(
            first_ref, refs[:-3], first_ref[chunk_rows:, :], full_width
        )
        rms_ref[...] = jnp.broadcast_to(inv_rms, (rows, LANES))

    return local_kernel(
        kernel,
        place,
        [first] + chunks,
        [bf16(rows, width), f32(rows, width), f32(rows, LANES)],
    )


def two_parts(line):
    high = line.astype(jnp.bfloat16).astype(jnp.float32)
    return [high, line - high]


def store_tail(out_ref, rows, lines):
    row_ids = lax.broadcasted_iota(jnp.int32, (TAIL, rows), 0)
    tile = jnp.zeros((TAIL, rows), jnp.float32)
    for number, line in enumerate(lines):
        tile = jnp.where(row_ids == number, line, tile)
    out_ref[rows:, :] = jnp.zeros((TAIL, out_ref.shape[1]), out_ref.dtype)
    out_ref[rows:, :rows] = tile.astype(out_ref.dtype)


def row_line(value):
    return as_line(jnp.sum(value, axis=1, keepdims=True))


def gradient_chunks(place, upstream, branch, inv_rms, others, other_at):
    rows, width = upstream.shape
    replaced = [other for other in others if other is not None]

    def kernel(tp, section, up_ref, branch_ref, rms_ref, *refs):
        other_refs, out_refs = list(refs[: len(replaced)]), refs[len(replaced) :]
        dots = row_line(up_ref[...].astype(jnp.float32) * branch_ref[...])
        lines = [dots] + two_parts(rms_ref[...].T[:1])
        for out_ref in out_refs:
            out_ref[:rows, :] = up_ref[...]
            store_tail(out_ref, rows, lines)
        if replaced:

            @pl.when(section == other_at)
            def _():
                for other, out_ref in zip(others, out_refs):
                    if other is not None:
                        out_ref[...] = other_refs.pop(0)[...]

    shapes = [bf16(rows + TAIL, width)] * len(others)
    return local_kernel(kernel, place, [upstream, branch, inv_rms, *replaced], shapes)


def statistics_chunk(place, a, back_chunk, cot, branch, inv_rms):
    rows, width = a.shape

    def kernel(tp, section, a_ref, back_ref, cot_ref, branch_ref, rms_ref, out_ref):
        wide = a_ref[...].astype(jnp.float32)
        back = back_ref[:rows, :].astype(jnp.float32)
        cot_wide = cot_ref[...].astype(jnp.float32)
        lines = []
        for product in (
            wide * wide,
            wide * back,
            cot_wide * branch_ref[...],
            back * branch_ref[...],
            wide * branch_ref[...],
        ):
            lines += two_parts(row_line(product))
        out_ref[:rows, :] = a_ref[...]
        store_tail(out_ref, rows, lines + two_parts(rms_ref[...].T[:1]))

    return local_kernel(
        kernel, place, [a, back_chunk, cot, branch, inv_rms], [bf16(rows + TAIL, width)]
    )[0]


def block_products(blocks, rows, start, tile):
    total = None
    for w_ref, chunk in blocks:
        product = lax.dot_general(
            w_ref[pl.ds(start, tile), :],
            chunk[:rows, :],
            (((1,), (1,)), ((), ())),
            preferred_element_type=jnp.float32,
        )
        total = product if total is None else total + product
    return total


def gained_chunks(place, chunks, w_far, w_near, gain_row, only):
    count, width, _ = w_far.shape
    chunk_rows = chunks[0].shape[0]
    rows = chunk_rows - TAIL
    tile = min(width, 256)

    def kernel(tp, section, far_ref, near_ref, gain_ref, *refs):
        w_refs = [far_ref.at[k] for k in range(count)] + [near_ref.at[k] for k in range(count)]
        chunk_refs, (out_ref, pack_ref) = refs[:-2], refs[-2:]

        @pl.when(section == only)
        def _():
            def work(start):
                columns = pl.ds(start, tile)
                products = block_products(list(zip(w_refs, chunk_refs)), rows, start, tile)
                back = gain_ref[:, columns] * products.T
                out_ref[:rows, columns] = back.astype(jnp.bfloat16)

            for_tiles(width, tile, work)
            out_ref[rows:, :] = jnp.zeros((TAIL, width), jnp.bfloat16)
            for number, chunk in enumerate([out_ref] + list(chunk_refs)):
                pack_ref[number * chunk_rows : (number + 1) * chunk_rows, :] = chunk[...]

    return local_kernel(
        kernel,
        place,
        [w_far, w_near, gain_row] + chunks,
        [bf16(chunk_rows, width), bf16((1 + len(chunks)) * chunk_rows, width)],
        cost=matmul_cost(rows, width, 2 * count),
    )


def early_products(place, pack, gained, w_far, w_near, only):
    count, width, _ = w_far.shape
    given = [chunk for chunk in gained if chunk is not None]
    chunk_rows = given[0].shape[0]
    rows = chunk_rows - TAIL
    tile = min(width, 256)

    def kernel(tp, section, far_ref, near_ref, pack_ref, *refs):
        w_refs = [far_ref.at[k] for k in range(count)] + [near_ref.at[k] for k in range(count)]
        packed = [pack_ref.at[pl.ds(k * chunk_rows, chunk_rows), :] for k in range(1 + 2 * count)]
        gained_refs = list(refs[:-2])
        gained_refs = [packed[0] if chunk is None else gained_refs.pop(0) for chunk in gained]

        @pl.when(section == only)
        def _():
            def work(start):
                for chunk_refs, out_ref in zip((packed[1:], gained_refs), refs[-2:]):
                    out_ref[pl.ds(start, tile), :] = block_products(
                        list(zip(w_refs, chunk_refs)), rows, start, tile
                    )

            for_tiles(width, tile, work)

    return local_kernel(
        kernel,
        place,
        [w_far, w_near, pack] + given,
        [f32(width, rows)] * 2,
        cost=matmul_cost(rows, width, 4 * count),
    )


def backward_part(place, chunks, w_half, numbers, rows, before=None):
    width = w_half.shape[1]
    tile = min(width, 256 if before else 512)
    given = [] if before is None else list(before)

    def kernel(tp, section, w_ref, *refs):
        chunk_refs, (out_ref, sum_ref) = refs[: len(chunks)], refs[-2:]
        blocks = [(w_ref.at[k], chunk) for k, chunk in zip(numbers, chunk_refs)]

        def work(start):
            products = block_products(blocks, rows, start, tile)
            if given:
                products = products + refs[len(chunks)][pl.ds(start, tile), :]
            out_ref[pl.ds(start, tile), :] = products

        if given:
            for start in range(0, width, tile):
                work(start)
        else:
            for_tiles(width, tile, work)
        sums = tail_sum(chunk_refs, rows)
        sum_ref[...] = sums + refs[len(chunks) + 1][...] if given else sums

    return local_kernel(
        kernel,
        place,
        [w_half] + chunks + given,
        [f32(width, rows), f32(TAIL, rows)],
        cost=matmul_cost(rows, width, len(chunks)),
    )


def finish_backward(place, chunks, w_half, numbers, before, own, gain_row, a, full_width, last_block=None, finals=(), last_parts=()):
    rows, width = a.shape
    chunk_rows = rows + TAIL
    count = len(chunks)
    tile = min(width, 256)
    extra = [] if last_block is None else list(last_block)
    chosen = [[array for array in arrays if array is not None] for arrays in finals]
    chosen.append(list(last_parts))

    def kernel(tp, section, w_ref, *refs):
        chunk_refs = refs[:count]
        before_ref, sum_ref, own_ref, gain_ref, a_ref = refs[count : count + 5]
        rest = list(refs[count + 5 :])
        out_refs = rest[len(extra) + sum(len(arrays) for arrays in chosen) :]
        out_ref = out_refs[0]
        sums = sum_ref[...] + tail_sum(chunk_refs, rows)
        tail = own_ref[rows:chunk_rows, :rows].astype(jnp.float32)

        def pair(lines, number):
            return lines[number : number + 1] + lines[number + 1 : number + 2]

        if extra:
            cot_ref, gained_ref, cot_ref_products, gained_ref_products = rest[:4]
            last_rms = lax.rsqrt(pair(sums, 0) / full_width + EPSILON)
            last_scale = last_rms * last_rms * last_rms / full_width * pair(sums, 2)
            dots = pair(sums, 4) + last_rms * pair(sums, 6) - last_scale * pair(sums, 8)
            rms = as_column(pair(tail, 10))
            rms_column, scale_column = as_column(last_rms), as_column(last_scale)
            out_refs[1][...] = (
                cot_ref[...].astype(jnp.float32)
                + rms_column * gained_ref[:rows, :].astype(jnp.float32)
                - scale_column * own_ref[:rows, :].astype(jnp.float32)
            ).astype(jnp.bfloat16)
            up_ref = out_refs[1]
        else:
            dots = sums[:1]
            rms = as_column(pair(tail, 1))
            up_ref = own_ref
        scale = rms * rms * rms / full_width * as_column(dots)
        blocks = [(w_ref.at[k], chunk) for k, chunk in zip(numbers, chunk_refs)]
        for start in range(0, width, tile):
            columns = slice(start, start + tile)
            products = block_products(blocks, rows, start, tile) + before_ref[columns, :]
            if extra:
                products = (
                    cot_ref_products[columns, :]
                    + last_rms * gained_ref_products[columns, :]
                    - last_scale * products
                )
            out_ref[:, columns] = (
                up_ref[:rows, columns].astype(jnp.float32)
                + rms * gain_ref[:, columns] * products.T
                - scale * a_ref[:, columns].astype(jnp.float32)
            ).astype(jnp.bfloat16)
        final_refs = rest[len(extra) :]
        for arrays, final_ref in zip(finals, out_refs[1 + bool(extra) :]):
            for number, array in enumerate(arrays):
                source = out_ref if array is None else final_refs.pop(0)

                @pl.when(section == number)
                def _(source=source, final_ref=final_ref):
                    final_ref[...] = source[...]

        if last_parts:

            @pl.when(section == len(finals[0]) - 1)
            def _():
                first_ref, *sum_refs, in_ref = final_refs[: len(last_parts)]
                out_refs[-1][...] = block_output(first_ref, sum_refs, in_ref[...], full_width)[0]

    return local_kernel(
        kernel,
        place,
        [w_half, *chunks, *before, own, gain_row, a, *extra]
        + [array for arrays in chosen for array in arrays],
        [bf16(rows, width)] * (1 + bool(extra) + len(finals)),
        cost=matmul_cost(rows, width, count),
    )


def on_device(inputs, cotangent, weights, gains):
    section_count = lax.axis_size("section")
    tp_count = lax.axis_size("tp")
    micro_count, row_count, width = inputs.shape
    rows = micro_count * row_count
    full_width = weights.shape[2]
    last = section_count - 1
    below = last - 1
    place = jnp.stack([lax.axis_index("tp"), lax.axis_index("section")])
    across = tp_count // 2
    near = list(range(1, across))
    near_codes = [0] + near
    own_order = near[::-1]
    far_codes = [across ^ e for e in near_codes]
    numbers = {code: number for number, code in enumerate(near_codes)}
    inside = [(last, last)]

    def send(value, routes, step=0):
        pairs = [
            (source * tp_count + t, target * tp_count + (t ^ step))
            for source, target in routes
            for t in range(tp_count)
        ]
        return lax.ppermute(value, ("section", "tp"), pairs)

    def gather(chunk, source, target, near_chunks=None, riding=(), forward_riding=(), pack=None, after=()):
        route = [(source, target)]
        crossed, _ = lax.optimization_barrier((send(chunk, [(source, source)], across), after))
        found = [send(chunk if pack is None else pack, route)]
        for e in near:
            near_chunk = near_chunks[e] if near_chunks else chunk
            found.append(send(near_chunk, route + list(riding), e))
        far_chunk, _ = lax.optimization_barrier((crossed, found[0]))
        forwarded = [send(far_chunk, route)]
        forwarded += [send(crossed, route + list(forward_riding), e) for e in near]
        return found, forwarded, crossed

    cot = cotangent.reshape(rows, width)

    block_in = inputs.reshape(rows, width)
    block_ins = []
    passed = []
    cot_far = send(cot, inside, across)
    for section in range(last):
        beside = section ^ 1
        route = [(section, beside)]
        first_pass = section == 0
        if first_pass:
            w_far, *far, cot_chunk = first_forward_blocks(
                place, block_in, gains, weights[0], far_codes, other=cot, other_from=last
            )
            w_far = in_vmem(w_far)
        else:
            far = forward_blocks(place, block_in, gains, w_far, only=section)
        near_route = route + inside if first_pass else route
        far_order = sorted(near, key=lambda e: e != across // 2) if section < 2 else own_order
        arrived = {e: send(far[near_codes.index(e)], near_route, e) for e in far_order}
        if first_pass:
            w_near, *own, cot_far = first_forward_blocks(
                place, block_in, gains, weights[0], near_codes, pack=True, other=cot_far, other_from=last
            )
            w_near = in_vmem(w_near)
        else:
            own = forward_blocks(place, block_in, gains, w_near, pack=True, only=section)
        far_own = send(far[0], route)
        combined = add_chunks(place, [arrived[e] for e in far_order] + [far_own])
        pack, _ = lax.optimization_barrier((own[0], far_own))
        crossed = send(combined, [(beside, beside)], across)
        direct = {e: send(own[near_codes.index(e)], near_route, e) for e in own_order}
        if first_pass:
            cot_chunks = [cot_far] + [direct[e] for e in near]
            cot_chunks += [cot_chunk] + [arrived[e] for e in near]
        if section == below:
            gained_pack, combined = lax.optimization_barrier((gained_pack, combined))
            products = early_products(
                place,
                gained_pack,
                [gained_found[code] for code in far_codes + near_codes],
                w_far,
                w_near,
                below,
            )
            crossed, products = lax.optimization_barrier((crossed, products))
        passed.append(
            finish_forward(
                place, send(pack, route), [direct[e] for e in own_order] + [crossed], full_width
            )
        )
        block_ins.append(block_in)
        output = passed[-1][0]
        if section == 1:
            order = near_codes
            cot_chunks, output = lax.optimization_barrier((cot_chunks, output))
            gained, gained_pack = gained_chunks(place, cot_chunks, w_far, w_near, gains, last)
            found, forwarded, far_chunk = gather(gained, last, below, pack=gained_pack)
            output, found, _ = lax.optimization_barrier((output, found, far_chunk))
            gained_found = dict(zip(order, found))
            gained_pack = gained_found[0]
            gained_found[0] = None
        block_in = send(output, [(beside, section + 1)]) if section % 2 else output
        if section == 1:
            block_in, forwarded, gained_pack = lax.optimization_barrier(
                (block_in, forwarded, gained_pack)
            )
            gained_found.update({across ^ code: chunk for code, chunk in zip(order, forwarded)})
    last_in = block_in
    chunk = statistics_chunk(place, block_in, gained, cot, *passed[below][1:])
    grads = [None] * section_count
    acts = [None] * section_count
    for section in range(below, -1, -1):
        turn = below - section
        beside = section ^ 1
        near_chunks, riding = None, ()
        if turn:
            upstream = send(grad, [(section + 1, beside)]) if section % 2 else grad
            others = [None]
            if turn == 1:
                upstream, last_own = lax.optimization_barrier((upstream, last_own))
                others += last_far[1:]
            if turn == 2:
                others += last_own[1:]
            chunk, *rest = gradient_chunks(place, upstream, *passed[section][1:], others, last)
            if turn <= 2:
                near_chunks, riding = dict(zip(near, rest)), inside
        found, forwarded, _ = gather(
            chunk,
            beside,
            section,
            near_chunks,
            riding,
            inside if turn == 1 else (),
            after=last_crossed if turn == 2 else (),
        )
        part = backward_part(
            place, found, w_near, [numbers[e] for e in [0] + near], rows
        )
        early = [0] + near[-max(1, across // 4) :]
        late = [e for e in near if e not in early]
        by_code = dict(zip([0] + near, forwarded))
        part = backward_part(
            place, [by_code[e] for e in early], w_far, [numbers[e] for e in early], rows, part
        )
        if turn == 1:
            last_combined = add_chunks(place, [last_far[0]] + found[1:], only=last)
            last_crossed = send(last_combined, inside, across)
        if turn == 2:
            last_parts = [last_own[0]] + found[1:] + [last_crossed, last_in]
        finish = [
            place,
            [by_code[e] for e in late],
            w_far,
            [numbers[e] for e in late],
            part,
            found[0],
            gains,
            block_ins[section],
            full_width,
        ]
        if turn == 0:
            grad, last_grad = finish_backward(*finish, [cot, gained_pack, *products])
            acts[:below] = [
                send(passed[number][0], [(number ^ 1, number)]) for number in range(below)
            ]
            grad, last_grad, last_in, acts[:below] = lax.optimization_barrier(
                (grad, last_grad, last_in, acts[:below])
            )
            last_far = forward_blocks(place, last_in, gains, w_far, only=last, looped=True)
            last_own = forward_blocks(place, last_in, gains, w_near, only=last, looped=True)
        elif section:
            (grad,) = finish_backward(*finish)
        else:
            grad, own_grad, own_output = finish_backward(*finish, None, [grads, acts[:last]], last_parts)
        if turn == 1:
            grads[last] = send(last_grad, [(below, last)])
            acts[below] = send(passed[below][0], [(last, below)])
            grad, grads[last], acts[below] = lax.optimization_barrier(
                (grad, grads[last], acts[below])
            )
        if section:
            grads[section] = grad
    shape = (1, micro_count, row_count, width)
    return own_output.reshape(shape), own_grad.reshape(shape)


def solution(mesh):
    placed = (
        P(None, None, "tp"),
        P(None, None, "tp"),
        P("section", "tp", None),
        P("section", "tp"),
    )
    return jax.shard_map(
        on_device,
        mesh=mesh,
        in_specs=placed,
        out_specs=(P("section", None, None, "tp"), P("section", None, None, "tp")),
        check_vma=False,
    )
```
